512 devices in a mesh: seq: 128 (over z, y, core), head: 4 (over x).
Axes of the slice: x: 4, y: 4, z: 16, core: 2. Of those that a mesh axis runs over, the one named last changes fastest.
Arguments:
- queries: bfloat16 [32768, 1024], P('seq', 'head'), may hold values from -240 to 240
- keys: bfloat16 [32768, 1024], P('seq', 'head'), may hold values from -7.25 to 7.25
- values: bfloat16 [32768, 1024], P('seq', 'head'), may hold values from -6 to 6
- w_out: bfloat16 [1024, 1024], P('head'), may hold values from -0.1875 to 0.1875
Outputs:
- mixed: bfloat16 [1024, 32768], P('head', 'seq')
The draws below stay inside these ranges and needn't reach their ends.
All inputs are finite; a program needn't handle non-finite values.
Results may differ from the reference program's by a relative error of at most 0.005.
Values may be sent and summed in bfloat16 or wider, within the bound.
A program may use at most 64 MiB of HBM per device.

```python
import jax
import jax.numpy as jnp
from jax import lax

HEADS = 16
HEAD_DIM = 64
D = 1024
BLOCK = 128
LEVELS = 6
TOKENS = 32768


def shared_base(key):
    return jnp.clip(jax.random.normal(key, (TOKENS, D), jnp.float32), -6.0, 6.0)


def regional(key, spread, bound):
    region_span = BLOCK * 2 ** LEVELS // 4
    regions = TOKENS // region_span + 1
    table = jnp.clip(spread * jax.random.normal(key, (regions, D), jnp.float32), -bound, bound)
    owner = jnp.arange(TOKENS, dtype=jnp.int32) // region_span
    return jnp.take(table, owner, axis=0)


def draw_keys(key, part):
    base = shared_base(key)
    key = jax.random.fold_in(key, 3)
    drift = regional(jax.random.fold_in(key, 1), 1.5, 3.0)
    return (0.7 * base + drift).astype(jnp.bfloat16)


def draw_queries(key, part):
    key = jax.random.fold_in(key, 5)
    free = jnp.clip(jax.random.normal(key, (TOKENS, D), jnp.float32), -6.0, 6.0)
    return (2.0 * free).astype(jnp.bfloat16)


def draw_values(key, part):
    key = jax.random.fold_in(key, 7)
    first, second = jax.random.split(key)
    drift = regional(second, 1.0, 2.0)
    noise = jnp.clip(jax.random.normal(first, (TOKENS, D), jnp.float32), -4.0, 4.0)
    return (noise + drift).astype(jnp.bfloat16)


def block_levels(key, dims, cuts, low, high):
    level, own = 1.0, jax.random.fold_in(key, 6)
    for position, parts in cuts:
        draws = jnp.exp(jax.random.uniform(jax.random.fold_in(own, position), (parts,), jnp.float32, low / len(cuts), high / len(cuts)))
        level = level * jnp.repeat(draws, dims[position] // parts).reshape([-1 if axis == position else 1 for axis in range(len(dims))])
    return level


def scatter_about(rng, shape, deviation, reach, shards=(), held_as=jnp.bfloat16):
    result = deviation * jax.random.normal(rng, shape, jnp.float32)
    if shards:
        result = result * block_levels(rng, shape, shards, -0.22, 0.18)
    return jnp.clip(result, -reach, reach).astype(held_as)


def setup_inputs(seed: int = 0) -> dict:
    streams_of = jax.random.split(jax.random.key(seed), 5)
    queries = draw_queries(jax.random.fold_in(streams_of[4], 71), 0)
    keys = draw_keys(jax.random.fold_in(streams_of[4], 71), 0)
    values = draw_values(jax.random.fold_in(streams_of[4], 71), 0)
    w_out = scatter_about(streams_of[3], (D, D), D ** -0.5, 0.1875, ((0, 4),))
    return {"queries": queries, "keys": keys, "values": values, "w_out": w_out}


def coarsen(rows, level):
    count = rows.shape[0] // (2 ** level)
    merged = rows.astype(jnp.float32).reshape(count, 2 ** level, rows.shape[1])
    return jnp.mean(merged, axis=1).astype(jnp.bfloat16)


def reference(queries, keys, values, w_out):
    total = queries.shape[0]
    width = queries.shape[1]
    scale = HEAD_DIM ** -0.5
    fine_keys = jnp.pad(keys, ((BLOCK, BLOCK), (0, 0)))
    fine_values = jnp.pad(values, ((BLOCK, BLOCK), (0, 0)))
    coarse_sets = []
    for level in range(1, LEVELS + 1):
        coarse_keys = jnp.pad(coarsen(keys, level), ((2 * BLOCK, 2 * BLOCK), (0, 0)))
        coarse_values = jnp.pad(coarsen(values, level), ((2 * BLOCK, 2 * BLOCK), (0, 0)))
        coarse_sets.append((level, coarse_keys, coarse_values))
    offsets = jnp.arange(3 * BLOCK, dtype=jnp.int32)

    def one_block(block):
        query_rows = lax.dynamic_slice_in_dim(queries, block * BLOCK, BLOCK, 0)
        key_list = [lax.dynamic_slice_in_dim(fine_keys, block * BLOCK, 3 * BLOCK, 0)]
        value_list = [lax.dynamic_slice_in_dim(fine_values, block * BLOCK, 3 * BLOCK, 0)]
        index = (block - 1) * BLOCK + offsets
        mask_list = [(index >= 0) & (index < total)]
        for level, coarse_keys, coarse_values in coarse_sets:
            parent = block // (2 ** level)
            start = (parent - 1) * BLOCK
            key_list.append(lax.dynamic_slice_in_dim(coarse_keys, start + 2 * BLOCK, 3 * BLOCK, 0))
            value_list.append(lax.dynamic_slice_in_dim(coarse_values, start + 2 * BLOCK, 3 * BLOCK, 0))
            coarse_index = start + offsets
            finer = block // (2 ** (level - 1))
            child = (2 * coarse_index) // BLOCK
            inside = (child >= finer - 1) & (child <= finer + 1)
            valid = (coarse_index >= 0) & (coarse_index < total // (2 ** level)) & jnp.logical_not(inside)
            mask_list.append(valid)
        key_rows = jnp.concatenate(key_list, 0).astype(jnp.float32).reshape(-1, HEADS, HEAD_DIM)
        value_rows = jnp.concatenate(value_list, 0).astype(jnp.float32).reshape(-1, HEADS, HEAD_DIM)
        mask = jnp.concatenate(mask_list, 0)
        query_float = query_rows.astype(jnp.float32).reshape(BLOCK, HEADS, HEAD_DIM)
        scores = jnp.einsum("qhd,khd->hqk", query_float, key_rows) * scale
        scores = jnp.where(mask[None, None, :], scores, -jnp.inf)
        top = jnp.max(scores, axis=2, keepdims=True)
        weights = jnp.exp(scores - top)
        totals = jnp.sum(weights, axis=2)
        probs = lax.optimization_barrier(weights.astype(jnp.bfloat16)).astype(jnp.float32)
        summed = jnp.einsum("hqk,khd->qhd", probs, value_rows)
        attended = summed / jnp.transpose(totals)[:, :, None]
        return attended.reshape(BLOCK, width).astype(jnp.bfloat16)

    blocks = lax.map(one_block, jnp.arange(total // BLOCK, dtype=jnp.int32))
    attended = blocks.reshape(total, width)
    product = jnp.dot(attended.astype(jnp.float32), w_out.astype(jnp.float32), preferred_element_type=jnp.float32)
    return jnp.transpose(product).astype(jnp.bfloat16)
```

```python
import functools

import jax
import jax.numpy as jnp
from jax import lax
from jax.experimental import pallas as pl
from jax.experimental.pallas import tpu as pltpu
from jax.sharding import PartitionSpec as P

HEAD_DIM = 64
BLOCK = 128
LEVELS = 6
HALF = BLOCK // 2
F32 = jnp.float32
BF16 = jnp.bfloat16
MESH = pl.DeviceIdType.MESH
FAR = (3, 4, 5, 6)
OFF = -1e30


def dot(a, b):
    return jnp.dot(a, b, preferred_element_type=F32)


def iota(shape, dim):
    return lax.broadcasted_iota(jnp.int32, shape, dim)


def pool(rows, fine, level, repeat):
    r, c = iota((rows, fine), 0), iota((rows, fine), 1)
    hit = (c >> level) == (r & (repeat - 1))
    return jnp.where(hit, 2.0**-level, 0.0).astype(BF16)


def unpack(n):
    r, c = iota((256, 256), 0), iota((256, 256), 1)
    group, inside = r >> 6, r & 63
    source, row = inside // n, inside & (n - 1)
    return jnp.where(c == source * (4 * n) + group * n + row, 1.0, 0.0).astype(BF16)


def scores_top(s, slabs):
    top = None
    for start, rows, bias in slabs:
        m = jnp.max(s[start : start + rows], axis=0, keepdims=True)
        if bias is not None:
            m = m + bias
        top = m if top is None else jnp.maximum(top, m)
    return top


def attend(k, vt, q, slabs):
    s = dot(k, q)
    top = scores_top(s, slabs)
    parts, total = [], None
    for start, rows, bias in slabs:
        shift = top if bias is None else top - bias
        p = jnp.exp(s[start : start + rows] - shift)
        t = jnp.sum(p, axis=0, keepdims=True)
        total = t if total is None else total + t
        parts.append(p.astype(BF16))
    o = dot(vt, jnp.concatenate(parts, 0))
    o = jnp.concatenate([o[:HEAD_DIM, :BLOCK], o[HEAD_DIM:, BLOCK:]], 1)
    return top, total, o


def merge(a, b):
    top = jnp.maximum(a[0], b[0])
    fa, fb = jnp.exp(a[0] - top), jnp.exp(b[0] - top)
    return top, a[1] * fa + b[1] * fb, a[2] * fa + b[2] * fb


def kernel(
    devices, heads,
    q_ref, k_ref, v_ref, w_ref, out_ref,
    near, near1, g2, g3, g4, g5, g6, s1, s2, s3, s4, s5, s6,
    qbd, kb, vbt, kc, vct, wg, wt, att, got, st_m, st_l, st_o,
    p1_s, p1_r, p2_s, p2_r, p3_s, p3_r, near_s, near_r, w_s, w_r, att_s, att_r,
):
    d = lax.axis_index("seq")
    x = lax.axis_index("head")
    core = d % 2
    gathers = {3: g3, 4: g4, 5: g5, 6: g6}
    stages = {2: s2, 3: s3, 4: s4, 5: s5, 6: s6}

    def seq(steps):
        return (d + steps + 2 * devices) % devices

    def group(level):
        return 2 ** (level - 2)

    def far_steps(level, p):
        g = group(level)
        if p == 0:
            return 2 * g
        if p == 1:
            return -2 * g
        return (3 - 6 * ((d // g) % 2)) * g

    def remote(src, dst, send, recv, axis, target):
        return pltpu.make_async_remote_copy(
            src_ref=src, dst_ref=dst, send_sem=send, recv_sem=recv,
            device_id={axis: target}, device_id_type=MESH,
        )

    def phase1(level, p):
        at = (level - 2, p)
        if level == 2:
            dst = g2.at[p]
        else:
            rank = (d % group(level)) // 2
            dst = gathers[level].at[rank, core, p]
        return remote(stages[level], dst, p1_s.at[at], p1_r.at[at], "seq", seq(far_steps(level, p)))

    def phase2(level, j):
        chips = group(level) // 2
        slot = {4: 0, 5: 1, 6: 4}[level] + j - 1
        mine = (d // 2) % chips
        target = d - 2 * mine + 2 * ((mine + j) % chips)
        block = gathers[level].at[mine, core]
        return remote(block, block, p2_s.at[slot], p2_r.at[slot], "seq", target)

    def phase3(level):
        block = gathers[level].at[:, core]
        slot = level - 3
        return remote(block, block, p3_s.at[slot], p3_r.at[slot], "seq", d + 1 - 2 * core)

    def neighbour(which, up):
        side = 0 if up else 1
        rows = pl.ds(BLOCK, BLOCK) if up else pl.ds(0, BLOCK)
        src = (k_ref.at[rows], v_ref.at[rows], s1.at[side])[which]
        dst = (near.at[0, side], near.at[1, side], near1.at[side])[which]
        at = (which, side)
        return remote(src, dst, near_s.at[at], near_r.at[at], "seq", seq(1 if up else -1))

    def weights(t):
        to = (x + t) % heads
        width = wg.shape[2]
        src = w_ref.at[:, pl.ds(pl.multiple_of(to * width, width), width)]
        return remote(src, wg.at[t - 1], w_s.at[t - 1], w_r.at[t - 1], "head", to)

    def share(b, hp, t):
        at = (b, hp, t - 1)
        rows = pl.ds(hp * BLOCK, BLOCK)
        return remote(
            att.at[b, rows], got.at[t - 1, b, rows], att_s.at[at], att_r.at[at], "head", (x + t) % heads
        )

    all1 = [(level, p) for level in (6, 5, 4, 3, 2) for p in range(3)]
    all2 = [(level, j) for level in (6, 5, 4) for j in range(1, group(level) // 2)]

    barrier = pltpu.get_barrier_semaphore()
    targets = [("seq", seq(far_steps(level, p))) for level, p in all1]
    mine = (d // 2) % 8
    targets += [("seq", d - 2 * mine + 2 * ((mine + j) % 8)) for j in range(1, 8)]
    targets += [("seq", d + 1 - 2 * core), ("seq", seq(1)), ("seq", seq(-1))]
    targets += [("head", (x + t) % heads) for t in range(1, heads)]
    for axis, target in targets:
        pl.semaphore_signal(barrier, inc=1, device_id={axis: target}, device_id_type=MESH)

    pools = jnp.concatenate(
        [pool(BLOCK, 256, 1, 128), pool(64, 256, 2, 64), pool(32, 256, 3, 32), pool(16, 256, 4, 16),
         pool(32, 256, 5, 8), pool(16, 256, 6, 4)], 0)
    k, v = k_ref[...], v_ref[...]
    ck, cv = dot(pools, k), dot(pools, v)
    blocks = [ck[:, :128], ck[:, 128:], cv[:, :128], cv[:, 128:]]
    for level, start, n in ((2, 128, 64), (3, 192, 32), (4, 224, 16)):
        for c in range(4):
            stages[level][c * n : (c + 1) * n, :] = blocks[c][start : start + n].astype(BF16)
    for level, start, n in ((5, 240, 8), (6, 272, 4)):
        owner = iota((4 * n, 128), 0) // n
        packed = blocks[0][start : start + 4 * n]
        for c in range(1, 4):
            packed = jnp.where(owner == c, blocks[c][start : start + 4 * n], packed)
        stages[level][...] = packed.astype(BF16)
    for half in range(2):
        for c in range(4):
            s1[half, c * HALF : (c + 1) * HALF, :] = blocks[c][half * HALF : (half + 1) * HALF].astype(BF16)

    pl.semaphore_wait(barrier, len(targets))
    for level, p in all1[:12]:
        phase1(level, p).start()
    for which in range(3):
        neighbour(which, True).start()
        neighbour(which, False).start()
    for level, p in all1[12:]:
        phase1(level, p).start()
    for t in range(1, heads):
        weights(t).start()

    qt = (q_ref[...].astype(F32) * HEAD_DIM**-0.5).T
    feature = iota((BLOCK, BLOCK), 0)
    for b in range(2):
        for hp in range(2):
            part = qt[hp * BLOCK : (hp + 1) * BLOCK, b * BLOCK : (b + 1) * BLOCK]
            low = jnp.where(feature < HEAD_DIM, part, 0.0)
            high = jnp.where(feature < HEAD_DIM, 0.0, part)
            qbd[b, hp] = jnp.concatenate([low, high], 1).astype(BF16)

    def keep(u, state):
        st_m[u, 0:1, :], st_l[u, 0:1, :], st_o[u] = state

    def kept(u):
        return st_m[u, 0:1, :], st_l[u, 0:1, :], st_o[u]

    units = [(b, hp) for b in range(2) for hp in range(2)]
    for hp in range(2):
        lanes = slice(hp * BLOCK, (hp + 1) * BLOCK)
        vt = v_ref[:, lanes].T
        kk = k_ref[:, lanes]
        for b in range(2):
            keep(b * 2 + hp, attend(kk, vt, qbd[b, hp], [(0, 256, None)]))

    for level, p in all1[:12]:
        phase1(level, p).wait_recv()
        if p == 2:
            for other, j in all2:
                if other == level:
                    phase2(level, j).start()
    phase3(3).start()

    for which in range(3):
        neighbour(which, True).wait_recv()
        neighbour(which, False).wait_recv()
    for level, p in all1[12:]:
        phase1(level, p).wait_recv()
    half_pool = pool(HALF, BLOCK, 1, HALF)
    lower_ok = jnp.where(d > 0, 0.0, OFF).astype(F32)
    upper_ok = jnp.where(d < devices - 1, 0.0, OFF).astype(F32)

    def far_bias(level):
        g, out = group(level), []
        e, last = d // g, devices // g - 1
        steps = (-2, 2, 3 - 6 * (e % 2))
        for step in steps:
            there = e + step
            out.append(jnp.where((there >= 0) & (there <= last), 0.0, OFF).astype(F32))
        return out

    bias2 = far_bias(2)
    for kind in range(2):
        pooled = [dot(half_pool, near[kind, side]).astype(BF16) for side in range(2)]
        for hp in range(2):
            lanes = slice(hp * BLOCK, (hp + 1) * BLOCK)
            c = 2 * kind + hp
            rows = slice(c * HALF, (c + 1) * HALF)
            common = [near1[0, rows, :], near1[1, rows, :]] + [g2[p, rows, :] for p in range(3)]
            for b in range(2):
                full = jnp.concatenate([near[kind, b, :, lanes], pooled[1 - b][:, lanes]] + common, 0)
                if kind == 0:
                    kb[b, hp] = full
                else:
                    vbt[b, hp] = full.T
    for b, hp in units:
        first, second = (lower_ok, upper_ok) if b == 0 else (upper_ok, lower_ok)
        slabs = [(0, 128, first), (128, 64, second), (192, 64, lower_ok), (256, 64, upper_ok)]
        slabs += [(320 + 64 * p, 64, bias2[p]) for p in range(3)]
        u = b * 2 + hp
        keep(u, merge(kept(u), attend(kb[b, hp], vbt[b, hp], qbd[b, hp], slabs)))
        if u == 1:
            for level in (4, 5, 6):
                for other, j in all2:
                    if other == level:
                        phase2(level, j).wait_recv()
                phase3(level).start()

    me = pl.ds(pl.multiple_of(x * wg.shape[2], wg.shape[2]), wg.shape[2])
    wt[0] = w_ref[:, me].T
    for t in range(1, heads):
        weights(t).wait_recv()
        wt[t] = wg[t - 1].T

    for level in FAR:
        phase3(level).wait_recv()
    slabs, keys, values = [], ([], []), ([], [])
    for level in FAR:
        n = 256 // 2**level
        g = group(level)
        for p, bias in enumerate(far_bias(level)):
            slabs.append((64 * len(slabs), 64, bias))
            whole = gathers[level][:, :, p].reshape(g, 4 * n, 128)
            if n >= 16:
                four = [whole[:, c * n : (c + 1) * n, :].reshape(64, 128) for c in range(4)]
            else:
                moved = dot(unpack(n), whole.reshape(256, 128)).astype(BF16)
                four = [moved[c * 64 : (c + 1) * 64] for c in range(4)]
            for hp in range(2):
                keys[hp].append(four[hp])
                values[hp].append(four[2 + hp])
    for hp in range(2):
        kc[hp] = jnp.concatenate(keys[hp], 0)
        vct[hp] = jnp.concatenate(values[hp], 0).T
    for b, hp in units:
        u = b * 2 + hp
        _, total, o = merge(kept(u), attend(kc[hp], vct[hp], qbd[b, hp], slabs))
        o = (o / total).astype(BF16)
        att[b, hp * BLOCK : (hp + 1) * BLOCK, :] = jnp.concatenate([o[:, :BLOCK], o[:, BLOCK:]], 0)
        for t in range(1, heads):
            share(b, hp, t).start()

    total = dot(wt[0], jnp.concatenate([att[0], att[1]], 1))
    for t in range(1, heads):
        for b, hp in units:
            share(b, hp, t).wait_recv()
        total = total + dot(wt[t], jnp.concatenate([got[t - 1, 0], got[t - 1, 1]], 1))
    out_ref[...] = total.astype(BF16)

    for level, p in all1:
        phase1(level, p).wait_send()
    for level, j in all2:
        phase2(level, j).wait_send()
    for level in FAR:
        phase3(level).wait_send()
    for which in range(3):
        neighbour(which, True).wait_send()
        neighbour(which, False).wait_send()
    for t in range(1, heads):
        weights(t).wait_send()
        for b, hp in units:
            share(b, hp, t).wait_send()


def solution(mesh):
    devices, heads = mesh.shape["seq"], mesh.shape["head"]

    def shards(q, k, v, w):
        rows, width = q.shape
        lanes = w.shape[1] // heads
        vmem = pl.BlockSpec(memory_space=pltpu.VMEM)
        dma = pltpu.SemaphoreType.DMA

        def gather(level):
            return pltpu.VMEM((2 ** (level - 3), 2, 3, 4 * (rows >> level), 128), BF16)

        def stage(level):
            return pltpu.VMEM((4 * (rows >> level), 128), BF16)

        return pl.pallas_call(
            functools.partial(kernel, devices, heads),
            out_shape=jax.ShapeDtypeStruct((lanes, rows), BF16),
            in_specs=[vmem] * 4,
            out_specs=vmem,
            scratch_shapes=[
                pltpu.VMEM((2, 2, BLOCK, width), BF16),
                pltpu.VMEM((2, 4 * HALF, 128), BF16),
                pltpu.VMEM((3, 4 * HALF, 128), BF16),
                gather(3), gather(4), gather(5), gather(6),
                pltpu.VMEM((2, 4 * HALF, 128), BF16),
                stage(2), stage(3), stage(4), stage(5), stage(6),
                pltpu.VMEM((2, 2, 128, 256), BF16),
                pltpu.VMEM((2, 2, 512, 128), BF16),
                pltpu.VMEM((2, 2, 128, 512), BF16),
                pltpu.VMEM((2, 768, 128), BF16),
                pltpu.VMEM((2, 128, 768), BF16),
                pltpu.VMEM((heads - 1, width, lanes), BF16),
                pltpu.VMEM((heads, lanes, width), BF16),
                pltpu.VMEM((2, width, BLOCK), BF16),
                pltpu.VMEM((heads - 1, 2, width, BLOCK), BF16),
                pltpu.VMEM((4, 8, 256), F32),
                pltpu.VMEM((4, 8, 256), F32),
                pltpu.VMEM((4, HEAD_DIM, 256), F32),
                dma((5, 3)), dma((5, 3)), dma((11,)), dma((11,)), dma((4,)), dma((4,)),
                dma((3, 2)), dma((3, 2)), dma((heads - 1,)), dma((heads - 1,)),
                dma((2, 2, heads - 1)), dma((2, 2, heads - 1)),
            ],
            compiler_params=pltpu.CompilerParams(
                collective_id=0, has_side_effects=True, vmem_limit_bytes=48 * 1024 * 1024
            ),
            cost_estimate=pl.CostEstimate(
                flops=2_000_000_000, bytes_accessed=1_200_000, transcendentals=1_600_000
            ),
        )(q, k, v, w)

    placed = (P("seq", "head"), P("seq", "head"), P("seq", "head"), P("head", None))
    return jax.shard_map(
        shards, mesh=mesh, in_specs=placed, out_specs=P("head", "seq"), check_vma=False
    )
```

```python
import functools

import jax
import jax.numpy as jnp
from jax import lax
from jax.experimental import pallas as pl
from jax.experimental.pallas import tpu as pltpu
from jax.sharding import PartitionSpec as P

HEAD_DIM = 64
BLOCK = 128
LEVELS = 6
HALF = BLOCK // 2
F32 = jnp.float32
BF16 = jnp.bfloat16
MESH = pl.DeviceIdType.MESH
FAR = (3, 4, 5, 6)
OFF = -1e30


def dot(a, b):
    return jnp.dot(a, b, preferred_element_type=F32)


def iota(shape, dim):
    return lax.broadcasted_iota(jnp.int32, shape, dim)


def pool(rows, fine, level, repeat):
    r, c = iota((rows, fine), 0), iota((rows, fine), 1)
    hit = (c >> level) == (r & (repeat - 1))
    return jnp.where(hit, 2.0**-level, 0.0).astype(BF16)


def unpack(n):
    r, c = iota((256, 256), 0), iota((256, 256), 1)
    group, inside = r >> 6, r & 63
    source, row = inside // n, inside & (n - 1)
    return jnp.where(c == source * (4 * n) + group * n + row, 1.0, 0.0).astype(BF16)


def scores_top(s, slabs):
    top = None
    for start, rows, bias in slabs:
        m = jnp.max(s[start : start + rows], axis=0, keepdims=True)
        if bias is not None:
            m = m + bias
        top = m if top is None else jnp.maximum(top, m)
    return top


def attend(k, vt, q, slabs):
    s = dot(k, q)
    top = scores_top(s, slabs)
    parts, total = [], None
    for start, rows, bias in slabs:
        shift = top if bias is None else top - bias
        p = jnp.exp(s[start : start + rows] - shift)
        t = jnp.sum(p, axis=0, keepdims=True)
        total = t if total is None else total + t
        parts.append(p.astype(BF16))
    o = dot(vt, jnp.concatenate(parts, 0))
    o = jnp.concatenate([o[:HEAD_DIM, :BLOCK], o[HEAD_DIM:, BLOCK:]], 1)
    return top, total, o


def merge(a, b):
    top = jnp.maximum(a[0], b[0])
    fa, fb = jnp.exp(a[0] - top), jnp.exp(b[0] - top)
    return top, a[1] * fa + b[1] * fb, a[2] * fa + b[2] * fb


def kernel(
    devices, heads,
    q_hbm, k_hbm, v_hbm, w_hbm, out_ref,
    q_ref, k_ref, v_ref, w_own, near, near1, g2, g3, g4, g5, g6, s1, s2, s3, s4, s5, s6,
    qbd, kb, vbt, kc, vct, wg, wt, att, got, st_m, st_l, st_o, in_s,
    p1_s, p1_r, p2_s, p2_r, p3_s, p3_r, near_s, near_r, w_s, w_r, att_s, att_r, relay_s, relay_r,
):
    d = lax.axis_index("seq")
    x = lax.axis_index("head")
    core = d % 2
    gathers = {3: g3, 4: g4, 5: g5, 6: g6}
    stages = {2: s2, 3: s3, 4: s4, 5: s5, 6: s6}

    def seq(steps):
        return (d + steps + 2 * devices) % devices

    def group(level):
        return 2 ** (level - 2)

    def far_steps(level, p):
        g = group(level)
        if p == 0:
            return 2 * g
        if p == 1:
            return -2 * g
        return (3 - 6 * ((d // g) % 2)) * g

    def remote(src, dst, send, recv, axis, target):
        return pltpu.make_async_remote_copy(
            src_ref=src, dst_ref=dst, send_sem=send, recv_sem=recv,
            device_id={axis: target}, device_id_type=MESH,
        )

    def far_target(level, p):
        target = seq(far_steps(level, p))
        if level == 4 and p == 2:
            target = target + 2 - 4 * ((target // 2) % 2)
        return target

    def phase1(level, p):
        at = (level - 2, p)
        rank = (d % group(level)) // 2
        if level == 2:
            dst = g2.at[p]
        elif level == 4 and p == 2:
            dst = g4.at[1 - rank, core, p]
        else:
            dst = gathers[level].at[rank, core, p]
        return remote(stages[level], dst, p1_s.at[at], p1_r.at[at], "seq", far_target(level, p))

    odd = (d // 2) % 2

    def phase2_target(level, j):
        if level == 3:
            return seq((1, 5)[j - 1] * 2 * (1 - 2 * odd))
        chips = group(level) // 2
        mine = (d // 2) % chips
        return d - 2 * mine + 2 * ((mine + j) % chips)

    def phase2(level, j):
        slot = {3: 0, 4: 2, 5: 3, 6: 6}[level] + j - 1
        if level == 3:
            src = g3.at[0, core, 2]
            dst = g3.at[0, core, 1 - odd if j == 1 else odd]
        else:
            src = dst = gathers[level].at[(d // 2) % (group(level) // 2), core]
        return remote(src, dst, p2_s.at[slot], p2_r.at[slot], "seq", phase2_target(level, j))

    def phase3(level):
        if level == 2:
            src, dst = g2.at[core], g2.at[2]
        else:
            src = dst = gathers[level].at[:, core]
        slot = level - 2
        return remote(src, dst, p3_s.at[slot], p3_r.at[slot], "seq", d + 1 - 2 * core)

    def neighbour(which, up):
        side = 0 if up else 1
        rows = pl.ds(BLOCK, BLOCK) if up else pl.ds(0, BLOCK)
        src = (k_hbm.at[rows], v_hbm.at[rows], s1.at[side])[which]
        dst = (near.at[0, side], near.at[1, side], near1.at[side])[which]
        at = (which, side)
        return remote(src, dst, near_s.at[at], near_r.at[at], "seq", seq(1 if up else -1))

    def weights(t):
        to = (x + t) % heads
        width = wg.shape[3]
        rows = pl.ds(pl.multiple_of(core * BLOCK, BLOCK), BLOCK)
        src = w_hbm.at[rows, pl.ds(pl.multiple_of(to * width, width), width)]
        return remote(src, wg.at[t - 1, core], w_s.at[t - 1], w_r.at[t - 1], "head", to)

    def weights_swap():
        block = wg.at[:, core]
        slot = heads - 1
        return remote(block, block, w_s.at[slot], w_r.at[slot], "seq", d + 1 - 2 * core)

    def share(b, hp, t):
        at = (b, hp, t // 2)
        rows = pl.ds(hp * BLOCK, BLOCK)
        return remote(
            att.at[b, rows], got.at[t - 1, b, rows], att_s.at[at], att_r.at[at], "head", (x + t) % heads
        )

    def relay(b, hp):
        rows = pl.ds(hp * BLOCK, BLOCK)
        t = 1 + 2 * hp
        src, dst = got.at[t - 1, b, rows], got.at[1, b, rows]
        return remote(src, dst, relay_s.at[b, hp], relay_r.at[b, hp], "head", (x + t) % heads)

    far1 = [(6, 0), (6, 1), (6, 2), (5, 0), (5, 1), (5, 2), (4, 2), (4, 0), (4, 1), (3, 2)]
    two1 = [(2, 0), (2, 1)]
    all1 = far1 + two1
    all2 = [(3, 1), (3, 2)] + [(level, j) for level in (4, 5, 6) for j in range(1, group(level) // 2)]

    def pass_on(level):
        for other, j in all2:
            if other == level:
                phase2(level, j).start()

    def passed(level):
        for other, j in all2:
            if other == level:
                phase2(level, j).wait_recv()

    barrier = pltpu.get_barrier_semaphore()
    targets = [("seq", far_target(level, p)) for level, p in all1]
    targets += [("seq", phase2_target(6, j)) for j in range(1, 8)]
    targets += [("seq", phase2_target(3, 2))]
    targets += [("seq", seq(1)), ("seq", seq(-1))]
    targets += [("head", (x + t) % heads) for t in range(1, heads)]
    for axis, target in targets:
        pl.semaphore_signal(barrier, inc=1, device_id={axis: target}, device_id_type=MESH)
    width = wg.shape[3]
    own = pl.ds(pl.multiple_of(x * width, width), width)
    loads = [
        pltpu.make_async_copy(src, dst, in_s.at[i])
        for i, (src, dst) in enumerate(
            [(k_hbm, k_ref), (v_hbm, v_ref), (q_hbm, q_ref), (w_hbm.at[:, own], w_own)]
        )
    ]
    for load in loads:
        load.start()

    pools = jnp.concatenate(
        [pool(BLOCK, 256, 1, 128), pool(64, 256, 2, 64), pool(32, 256, 3, 32), pool(16, 256, 4, 16),
         pool(32, 256, 5, 8), pool(16, 256, 6, 4)], 0)
    loads[0].wait()
    loads[1].wait()
    k, v = k_ref[...], v_ref[...]
    ck, cv = dot(pools, k), dot(pools, v)
    blocks = [ck[:, :128], ck[:, 128:], cv[:, :128], cv[:, 128:]]
    for level, start, n in ((2, 128, 64), (3, 192, 32), (4, 224, 16)):
        for c in range(4):
            stages[level][c * n : (c + 1) * n, :] = blocks[c][start : start + n].astype(BF16)
    for level, start, n in ((5, 240, 8), (6, 272, 4)):
        owner = iota((4 * n, 128), 0) // n
        packed = blocks[0][start : start + 4 * n]
        for c in range(1, 4):
            packed = jnp.where(owner == c, blocks[c][start : start + 4 * n], packed)
        stages[level][...] = packed.astype(BF16)
    for half in range(2):
        for c in range(4):
            s1[half, c * HALF : (c + 1) * HALF, :] = blocks[c][half * HALF : (half + 1) * HALF].astype(BF16)

    pl.semaphore_wait(barrier, len(targets))
    for level, p in far1:
        phase1(level, p).start()
    for which in range(3):
        neighbour(which, True).start()
        neighbour(which, False).start()
    for level, p in two1:
        phase1(level, p).start()
    for t in range(1, heads):
        weights(t).start()

    loads[2].wait()
    qt = (q_ref[...].astype(F32) * HEAD_DIM**-0.5).T
    feature = iota((BLOCK, BLOCK), 0)
    for b in range(2):
        for hp in range(2):
            part = qt[hp * BLOCK : (hp + 1) * BLOCK, b * BLOCK : (b + 1) * BLOCK]
            low = jnp.where(feature < HEAD_DIM, part, 0.0)
            high = jnp.where(feature < HEAD_DIM, 0.0, part)
            qbd[b, hp] = jnp.concatenate([low, high], 1).astype(BF16)

    def keep(u, state):
        st_m[u, 0:1, :], st_l[u, 0:1, :], st_o[u] = state

    def kept(u):
        return st_m[u, 0:1, :], st_l[u, 0:1, :], st_o[u]

    units = [(b, hp) for b in range(2) for hp in range(2)]
    for hp in range(2):
        lanes = slice(hp * BLOCK, (hp + 1) * BLOCK)
        vt = v_ref[:, lanes].T
        kk = k_ref[:, lanes]
        for b in range(2):
            keep(b * 2 + hp, attend(kk, vt, qbd[b, hp], [(0, 256, None)]))

    for level, p in far1:
        phase1(level, p).wait_recv()
        if (level, p) in ((6, 2), (5, 2), (4, 1), (3, 2)):
            pass_on(level)

    for level, p in two1:
        phase1(level, p).wait_recv()
    phase3(2).start()
    for which in range(3):
        neighbour(which, True).wait_recv()
        neighbour(which, False).wait_recv()
    half_pool = pool(HALF, BLOCK, 1, HALF)
    lower_ok = jnp.where(d > 0, 0.0, OFF).astype(F32)
    upper_ok = jnp.where(d < devices - 1, 0.0, OFF).astype(F32)

    def far_bias(level):
        g, out = group(level), []
        e, last = d // g, devices // g - 1
        steps = (-2, 2, 3 - 6 * (e % 2))
        for step in steps:
            there = e + step
            out.append(jnp.where((there >= 0) & (there <= last), 0.0, OFF).astype(F32))
        return out

    bias2 = far_bias(2)
    phase3(2).wait_recv()
    for kind in range(2):
        pooled = [dot(half_pool, near[kind, side]).astype(BF16) for side in range(2)]
        for hp in range(2):
            lanes = slice(hp * BLOCK, (hp + 1) * BLOCK)
            c = 2 * kind + hp
            rows = slice(c * HALF, (c + 1) * HALF)
            common = [near1[0, rows, :], near1[1, rows, :]] + [g2[p, rows, :] for p in range(3)]
            for b in range(2):
                full = jnp.concatenate([near[kind, b, :, lanes], pooled[1 - b][:, lanes]] + common, 0)
                if kind == 0:
                    kb[b, hp] = full
                else:
                    vbt[b, hp] = full.T
    for b, hp in units:
        first, second = (lower_ok, upper_ok) if b == 0 else (upper_ok, lower_ok)
        slabs = [(0, 128, first), (128, 64, second), (192, 64, lower_ok), (256, 64, upper_ok)]
        slabs += [(320 + 64 * p, 64, bias2[p]) for p in range(3)]
        u = b * 2 + hp
        keep(u, merge(kept(u), attend(kb[b, hp], vbt[b, hp], qbd[b, hp], slabs)))
        if u == 1:
            for level in FAR:
                passed(level)
                phase3(level).start()

    for t in range(1, heads):
        weights(t).wait_recv()
    weights_swap().start()
    loads[3].wait()
    wt[0] = w_own[...].T

    def far_chunk(i):
        slabs, keys, values = [], ([], []), ([], [])
        for level in FAR[2 * i : 2 * i + 2]:
            phase3(level).wait_recv()
            n = 256 // 2**level
            g = group(level)
            for p, bias in enumerate(far_bias(level)):
                slabs.append((64 * len(slabs), 64, bias))
                whole = gathers[level][:, :, p].reshape(g, 4 * n, 128)
                if n >= 16:
                    four = [whole[:, c * n : (c + 1) * n, :].reshape(64, 128) for c in range(4)]
                else:
                    moved = dot(unpack(n), whole.reshape(256, 128)).astype(BF16)
                    four = [moved[c * 64 : (c + 1) * 64] for c in range(4)]
                for hp in range(2):
                    keys[hp].append(four[hp])
                    values[hp].append(four[2 + hp])
        for hp in range(2):
            kc[i, hp] = jnp.concatenate(keys[hp], 0)
            vct[i, hp] = jnp.concatenate(values[hp], 0).T
        return slabs

    slabs = far_chunk(0)
    for b, hp in units:
        u = b * 2 + hp
        keep(u, merge(kept(u), attend(kc[0, hp], vct[0, hp], qbd[b, hp], slabs)))
    weights_swap().wait_recv()
    for t in range(1, heads):
        wt[t] = wg[t - 1].reshape(2 * BLOCK, width).T
    slabs = far_chunk(1)
    for b, hp in units:
        u = b * 2 + hp
        _, total, o = merge(kept(u), attend(kc[1, hp], vct[1, hp], qbd[b, hp], slabs))
        o = (o / total).astype(BF16)
        att[b, hp * BLOCK : (hp + 1) * BLOCK, :] = jnp.concatenate([o[:, :BLOCK], o[:, BLOCK:]], 0)
        share(b, hp, 1).start()
        share(b, hp, 3).start()

    for b, hp in units:
        share(b, hp, 1 + 2 * hp).wait_recv()
        relay(b, hp).start()
    total = dot(wt[0], jnp.concatenate([att[0], att[1]], 1))
    for b, hp in units:
        share(b, hp, 3 - 2 * hp).wait_recv()
    for t in (1, 3):
        total = total + dot(wt[t], jnp.concatenate([got[t - 1, 0], got[t - 1, 1]], 1))
    for b, hp in units:
        relay(b, hp).wait_recv()
    total = total + dot(wt[2], jnp.concatenate([got[1, 0], got[1, 1]], 1))
    out_ref[...] = total.astype(BF16)

    for level, p in all1:
        phase1(level, p).wait_send()
    for level, j in all2:
        phase2(level, j).wait_send()
    for level in (2,) + FAR:
        phase3(level).wait_send()
    for which in range(3):
        neighbour(which, True).wait_send()
        neighbour(which, False).wait_send()
    for t in range(1, heads):
        weights(t).wait_send()
    weights_swap().wait_send()
    for b, hp in units:
        share(b, hp, 1).wait_send()
        share(b, hp, 3).wait_send()
        relay(b, hp).wait_send()


def solution(mesh):
    devices, heads = mesh.shape["seq"], mesh.shape["head"]

    def shards(q, k, v, w):
        rows, width = q.shape
        lanes = w.shape[1] // heads
        vmem = pl.BlockSpec(memory_space=pltpu.VMEM)
        dma = pltpu.SemaphoreType.DMA

        def gather(level):
            return pltpu.VMEM((2 ** (level - 3), 2, 3, 4 * (rows >> level), 128), BF16)

        def stage(level):
            return pltpu.VMEM((4 * (rows >> level), 128), BF16)

        return pl.pallas_call(
            functools.partial(kernel, devices, heads),
            out_shape=jax.ShapeDtypeStruct((lanes, rows), BF16),
            in_specs=[pl.BlockSpec(memory_space=pltpu.HBM)] * 4,
            out_specs=vmem,
            scratch_shapes=[
                pltpu.VMEM((rows, width), BF16),
                pltpu.VMEM((rows, width), BF16),
                pltpu.VMEM((rows, width), BF16),
                pltpu.VMEM((width, lanes), BF16),
                pltpu.VMEM((2, 2, BLOCK, width), BF16),
                pltpu.VMEM((2, 4 * HALF, 128), BF16),
                pltpu.VMEM((3, 4 * HALF, 128), BF16),
                gather(3), gather(4), gather(5), gather(6),
                pltpu.VMEM((2, 4 * HALF, 128), BF16),
                stage(2), stage(3), stage(4), stage(5), stage(6),
                pltpu.VMEM((2, 2, 128, 256), BF16),
                pltpu.VMEM((2, 2, 512, 128), BF16),
                pltpu.VMEM((2, 2, 128, 512), BF16),
                pltpu.VMEM((2, 2, 384, 128), BF16),
                pltpu.VMEM((2, 2, 128, 384), BF16),
                pltpu.VMEM((heads - 1, 2, BLOCK, lanes), BF16),
                pltpu.VMEM((heads, lanes, width), BF16),
                pltpu.VMEM((2, width, BLOCK), BF16),
                pltpu.VMEM((heads - 1, 2, width, BLOCK), BF16),
                pltpu.VMEM((4, 8, 256), F32),
                pltpu.VMEM((4, 8, 256), F32),
                pltpu.VMEM((4, HEAD_DIM, 256), F32),
                dma((4,)),
                dma((5, 3)), dma((5, 3)), dma((13,)), dma((13,)), dma((5,)), dma((5,)),
                dma((3, 2)), dma((3, 2)), dma((heads,)), dma((heads,)),
                dma((2, 2, 2)), dma((2, 2, 2)), dma((2, 2)), dma((2, 2)),
            ],
            compiler_params=pltpu.CompilerParams(
                collective_id=0, has_side_effects=True, vmem_limit_bytes=60 * 1024 * 1024
            ),
            cost_estimate=pl.CostEstimate(
                flops=2_000_000_000, bytes_accessed=1_200_000, transcendentals=1_600_000
            ),
        )(q, k, v, w)

    placed = (P("seq", "head"), P("seq", "head"), P("seq", "head"), P("head", None))
    return jax.shard_map(
        shards, mesh=mesh, in_specs=placed, out_specs=P("head", "seq"), check_vma=False
    )
```

```python
import functools

import jax
import jax.numpy as jnp
from jax import lax
from jax.experimental import pallas as pl
from jax.experimental.pallas import tpu as pltpu
from jax.sharding import PartitionSpec as P

HEAD_DIM = 64
BLOCK = 128
LEVELS = 6
HALF = BLOCK // 2
F32 = jnp.float32
BF16 = jnp.bfloat16
MESH = pl.DeviceIdType.MESH
FAR = (3, 4, 5, 6)
OFF = -1e30


def dot(a, b):
    return jnp.dot(a, b, preferred_element_type=F32)


def iota(shape, dim):
    return lax.broadcasted_iota(jnp.int32, shape, dim)


def pool(rows, fine, level, repeat):
    r, c = iota((rows, fine), 0), iota((rows, fine), 1)
    hit = (c >> level) == (r & (repeat - 1))
    return jnp.where(hit, 2.0**-level, 0.0).astype(BF16)


def unpack(n):
    r, c = iota((256, 256), 0), iota((256, 256), 1)
    group, inside = r >> 6, r & 63
    source, row = inside // n, inside & (n - 1)
    return jnp.where(c == source * (4 * n) + group * n + row, 1.0, 0.0).astype(BF16)


def scores_top(s, slabs):
    top = None
    for start, rows, bias in slabs:
        m = jnp.max(s[start : start + rows], axis=0, keepdims=True)
        if bias is not None:
            m = m + bias
        top = m if top is None else jnp.maximum(top, m)
    return top


def attend(k, vt, q, slabs):
    s = dot(k, q)
    top = scores_top(s, slabs)
    parts, total = [], None
    for start, rows, bias in slabs:
        shift = top if bias is None else top - bias
        p = jnp.exp(s[start : start + rows] - shift)
        t = jnp.sum(p, axis=0, keepdims=True)
        total = t if total is None else total + t
        parts.append(p.astype(BF16))
    o = dot(vt, jnp.concatenate(parts, 0))
    o = jnp.concatenate([o[:HEAD_DIM, :BLOCK], o[HEAD_DIM:, BLOCK:]], 1)
    return top, total, o


def merge(a, b):
    top = jnp.maximum(a[0], b[0])
    fa, fb = jnp.exp(a[0] - top), jnp.exp(b[0] - top)
    return top, a[1] * fa + b[1] * fb, a[2] * fa + b[2] * fb


def kernel(
    devices, heads,
    q_hbm, k_hbm, v_hbm, w_hbm, out_ref,
    q_ref, k_ref, v_ref, w_own, pn, near, near1, g2, g3, g4, g5, g6, s1, s2, s3, s4, s5, s6,
    qbd, ka, vat, kb, vb, vbt, kc, vc, vct, wg, wt, att, got, st_m, st_l, st_o, in_s,
    p1_s, p1_r, p2_s, p2_r, p3_s, p3_r, near_s, near_r, w_s, w_r, att_s, att_r, relay_s, relay_r,
):
    d = lax.axis_index("seq")
    x = lax.axis_index("head")
    core = d % 2
    gathers = {3: g3, 4: g4, 5: g5, 6: g6}
    stages = {2: s2, 3: s3, 4: s4, 5: s5, 6: s6}

    def seq(steps):
        return (d + steps + 2 * devices) % devices

    def group(level):
        return 2 ** (level - 2)

    def far_steps(level, p):
        g = group(level)
        if p == 0:
            return 2 * g
        if p == 1:
            return -2 * g
        return (3 - 6 * ((d // g) % 2)) * g

    def remote(src, dst, send, recv, axis, target):
        return pltpu.make_async_remote_copy(
            src_ref=src, dst_ref=dst, send_sem=send, recv_sem=recv,
            device_id={axis: target}, device_id_type=MESH,
        )

    def far_target(level, p):
        target = seq(far_steps(level, p))
        if level == 4 and p == 2:
            target = target + 2 - 4 * ((target // 2) % 2)
        return target

    def phase1(level, p):
        at = (level - 2, p)
        rank = (d % group(level)) // 2
        if level == 2:
            dst = g2.at[p]
        elif level == 4 and p == 2:
            dst = g4.at[1 - rank, core, p]
        else:
            dst = gathers[level].at[rank, core, p]
        return remote(stages[level], dst, p1_s.at[at], p1_r.at[at], "seq", far_target(level, p))

    odd = (d // 2) % 2

    def phase2_target(level, j):
        if level == 3:
            return seq((1, 5)[j - 1] * 2 * (1 - 2 * odd))
        chips = group(level) // 2
        mine = (d // 2) % chips
        return d - 2 * mine + 2 * ((mine + j) % chips)

    def phase2(level, j):
        slot = {3: 0, 4: 2, 5: 3, 6: 6}[level] + j - 1
        if level == 3:
            src = g3.at[0, core, 2]
            dst = g3.at[0, core, 1 - odd if j == 1 else odd]
        else:
            src = dst = gathers[level].at[(d // 2) % (group(level) // 2), core]
        return remote(src, dst, p2_s.at[slot], p2_r.at[slot], "seq", phase2_target(level, j))

    def phase3(level):
        if level == 2:
            src, dst = g2.at[core], g2.at[2]
        else:
            src = dst = gathers[level].at[:, core]
        slot = level - 2
        return remote(src, dst, p3_s.at[slot], p3_r.at[slot], "seq", d + 1 - 2 * core)

    def neighbour(which, up):
        side = 0 if up else 1
        rows = pl.ds(BLOCK, BLOCK) if up else pl.ds(0, BLOCK)
        src = (k_hbm.at[rows], v_hbm.at[rows], s1.at[side])[which]
        dst = (near.at[0, side], near.at[1, side], near1.at[side])[which]
        at = (which, side)
        return remote(src, dst, near_s.at[at], near_r.at[at], "seq", seq(1 if up else -1))

    def weights(t):
        to = (x + t) % heads
        width = wg.shape[3]
        rows = pl.ds(pl.multiple_of(core * BLOCK, BLOCK), BLOCK)
        src = w_hbm.at[rows, pl.ds(pl.multiple_of(to * width, width), width)]
        return remote(src, wg.at[t - 1, core], w_s.at[t - 1], w_r.at[t - 1], "head", to)

    def weights_swap():
        block = wg.at[:, core]
        slot = heads - 1
        return remote(block, block, w_s.at[slot], w_r.at[slot], "seq", d + 1 - 2 * core)

    def share(b, hp, t):
        at = (b, hp, t // 2)
        rows = pl.ds(pl.multiple_of(hp * BLOCK, BLOCK), BLOCK)
        return remote(
            att.at[b, rows], got.at[t - 1, b, rows], att_s.at[at], att_r.at[at], "head", (x + t) % heads
        )

    def relay(b, hp):
        rows = pl.ds(hp * BLOCK, BLOCK)
        t = 1 + 2 * hp
        src, dst = got.at[t - 1, b, rows], got.at[1, b, rows]
        return remote(src, dst, relay_s.at[b, hp], relay_r.at[b, hp], "head", (x + t) % heads)

    far1 = [(6, 0), (6, 1), (6, 2), (5, 0), (5, 1), (5, 2), (4, 2), (4, 0), (4, 1), (3, 2)]
    two1 = [(2, 0), (2, 1)]
    all1 = far1 + two1
    all2 = [(3, 1), (3, 2)] + [(level, j) for level in (4, 5, 6) for j in range(1, group(level) // 2)]

    def pass_on(level):
        for other, j in all2:
            if other == level:
                phase2(level, j).start()

    def passed(level):
        for other, j in all2:
            if other == level:
                phase2(level, j).wait_recv()

    barrier = pltpu.get_barrier_semaphore()
    targets = [("seq", far_target(level, p)) for level, p in all1]
    targets += [("seq", phase2_target(6, j)) for j in range(1, 8)]
    targets += [("seq", phase2_target(3, 2))]
    targets += [("seq", seq(1)), ("seq", seq(-1))]
    targets += [("head", (x + t) % heads) for t in range(1, heads)]
    for axis, target in targets:
        pl.semaphore_signal(barrier, inc=1, device_id={axis: target}, device_id_type=MESH)
    width = wg.shape[3]
    own = pl.ds(pl.multiple_of(x * width, width), width)
    loads = [
        pltpu.make_async_copy(src, dst, in_s.at[i])
        for i, (src, dst) in enumerate(
            [(k_hbm, k_ref), (v_hbm, v_ref), (q_hbm, q_ref), (w_hbm.at[:, own], w_own)]
        )
    ]
    for load in loads:
        load.start()

    pools = jnp.concatenate(
        [pool(BLOCK, 256, 1, 128), pool(64, 256, 2, 64), pool(32, 256, 3, 32), pool(16, 256, 4, 16),
         pool(32, 256, 5, 8), pool(16, 256, 6, 4)], 0)
    loads[0].wait()
    loads[1].wait()
    k, v = k_ref[...], v_ref[...]
    ck, cv = dot(pools, k), dot(pools, v)
    blocks = [ck[:, :128], ck[:, 128:], cv[:, :128], cv[:, 128:]]
    for level, start, n in ((2, 128, 64), (3, 192, 32), (4, 224, 16)):
        for c in range(4):
            stages[level][c * n : (c + 1) * n, :] = blocks[c][start : start + n].astype(BF16)
    for level, start, n in ((5, 240, 8), (6, 272, 4)):
        owner = iota((4 * n, 128), 0) // n
        packed = blocks[0][start : start + 4 * n]
        for c in range(1, 4):
            packed = jnp.where(owner == c, blocks[c][start : start + 4 * n], packed)
        stages[level][...] = packed.astype(BF16)
    for half in range(2):
        for c in range(4):
            s1[half, c * HALF : (c + 1) * HALF, :] = blocks[c][half * HALF : (half + 1) * HALF].astype(BF16)

    pl.semaphore_wait(barrier, len(targets))
    for level, p in far1:
        phase1(level, p).start()
    for which in range(3):
        neighbour(which, True).start()
        neighbour(which, False).start()
    for level, p in two1:
        phase1(level, p).start()
    for t in range(1, heads):
        weights(t).start()

    loads[2].wait()
    feature = iota((BLOCK, BLOCK), 0)

    def lanes_of(hp):
        return pl.ds(pl.multiple_of(hp * BLOCK, BLOCK), BLOCK)

    def each(count, body):
        def step(i, carry):
            body(i)
            return carry

        lax.fori_loop(0, count, step, 0)

    def lay_own(hp):
        ka[hp] = k_ref[:, lanes_of(hp)]
        vat[hp] = v_ref[:, lanes_of(hp)].T
        qt = (q_ref[:, lanes_of(hp)].astype(F32) * HEAD_DIM**-0.5).T
        for b in range(2):
            part = qt[:, b * BLOCK : (b + 1) * BLOCK]
            low = jnp.where(feature < HEAD_DIM, part, 0.0)
            high = jnp.where(feature < HEAD_DIM, 0.0, part)
            qbd[2 * b + hp] = jnp.concatenate([low, high], 1).astype(BF16)

    each(2, lay_own)

    def keep(u, state):
        st_m[u, 0:1, :], st_l[u, 0:1, :], st_o[u] = state

    def kept(u):
        return st_m[u, 0:1, :], st_l[u, 0:1, :], st_o[u]

    units = [(b, hp) for b in range(2) for hp in range(2)]

    def own_keys(u):
        keep(u, attend(ka[u % 2], vat[u % 2], qbd[u], [(0, 256, None)]))

    each(4, own_keys)

    for level, p in far1:
        phase1(level, p).wait_recv()
        if (level, p) in ((6, 2), (5, 2), (4, 1), (3, 2)):
            pass_on(level)

    for level, p in two1:
        phase1(level, p).wait_recv()
    phase3(2).start()
    for which in range(3):
        neighbour(which, True).wait_recv()
        neighbour(which, False).wait_recv()
    half_pool = pool(HALF, BLOCK, 1, HALF)
    lower_ok = jnp.where(d > 0, 0.0, OFF).astype(F32)
    upper_ok = jnp.where(d < devices - 1, 0.0, OFF).astype(F32)

    def far_bias(level):
        g, out = group(level), []
        e, last = d // g, devices // g - 1
        steps = (-2, 2, 3 - 6 * (e % 2))
        for step in steps:
            there = e + step
            out.append(jnp.where((there >= 0) & (there <= last), 0.0, OFF).astype(F32))
        return out

    bias2 = far_bias(2)
    phase3(2).wait_recv()
    pooled = [[dot(half_pool, near[kind, side]).astype(BF16) for side in range(2)] for kind in range(2)]
    for kind in range(2):
        for side in range(2):
            for hp in range(2):
                pn[kind, side, hp] = pooled[kind][side][:, hp * BLOCK : (hp + 1) * BLOCK]

    def lay_near(hp):
        for kind in range(2):
            rows = pl.ds(pl.multiple_of((2 * kind + hp) * HALF, HALF), HALF)
            for b in range(2):
                u = 2 * b + hp
                to = kb if kind == 0 else vb
                to[u, 0:128, :] = near[kind, b, :, lanes_of(hp)]
                to[u, 128:192, :] = pn[kind, 1 - b, hp]
                to[u, 192:256, :] = near1[0, rows, :]
                to[u, 256:320, :] = near1[1, rows, :]
                for p in range(3):
                    to[u, 320 + 64 * p : 384 + 64 * p, :] = g2[p, rows, :]

    each(2, lay_near)

    def near_keys(u):
        first = jnp.where(u < 2, lower_ok, upper_ok)
        second = jnp.where(u < 2, upper_ok, lower_ok)
        slabs = [(0, 128, first), (128, 64, second), (192, 64, lower_ok), (256, 64, upper_ok)]
        slabs += [(320 + 64 * p, 64, bias2[p]) for p in range(3)]
        vbt[...] = vb[u].T
        keep(u, merge(kept(u), attend(kb[u], vbt[...], qbd[u], slabs)))

    lax.fori_loop(0, 2, lambda u, c: (near_keys(u), c)[1], 0)
    for level in FAR:
        passed(level)
        phase3(level).start()
    lax.fori_loop(2, 4, lambda u, c: (near_keys(u), c)[1], 0)

    for t in range(1, heads):
        weights(t).wait_recv()
    weights_swap().start()
    loads[3].wait()
    wt[0] = w_own[...].T

    def far_chunk(i):
        slabs = []
        for which, level in enumerate(FAR[2 * i : 2 * i + 2]):
            phase3(level).wait_recv()
            n = 256 // 2**level
            g = group(level)
            slabs += [(64 * (3 * which + p), 64, bias) for p, bias in enumerate(far_bias(level))]
            moves = unpack(n) if n < 16 else None

            def lay(p):
                rows = pl.ds(pl.multiple_of(64 * (3 * which + p), 64), 64)
                whole = gathers[level][:, :, p].reshape(g, 4 * n, 128)
                if n >= 16:
                    four = [whole[:, c * n : (c + 1) * n, :].reshape(64, 128) for c in range(4)]
                else:
                    moved = dot(moves, whole.reshape(256, 128)).astype(BF16)
                    four = [moved[c * 64 : (c + 1) * 64] for c in range(4)]
                for hp in range(2):
                    kc[i, hp, rows, :] = four[hp]
                    vc[i, hp, rows, :] = four[2 + hp]

            each(3, lay)

        def turn(hp):
            vct[i, hp] = vc[i, hp].T

        each(2, turn)
        return slabs

    slabs = far_chunk(0)

    def far_keys(u):
        hp = u % 2
        keep(u, merge(kept(u), attend(kc[0, hp], vct[0, hp], qbd[u], slabs)))

    each(4, far_keys)
    weights_swap().wait_recv()

    def turn_weights(t):
        wt[t + 1] = wg[t].reshape(2 * BLOCK, width).T

    each(heads - 1, turn_weights)
    last_slabs = far_chunk(1)

    def last_keys(u):
        b, hp = u // 2, u % 2
        _, total, o = merge(kept(u), attend(kc[1, hp], vct[1, hp], qbd[u], last_slabs))
        o = (o / total).astype(BF16)
        att[b, lanes_of(hp), :] = jnp.concatenate([o[:, :BLOCK], o[:, BLOCK:]], 0)
        share(b, hp, 1).start()
        share(b, hp, 3).start()

    each(4, last_keys)

    for b, hp in units:
        share(b, hp, 1 + 2 * hp).wait_recv()
        relay(b, hp).start()
    total = dot(wt[0], jnp.concatenate([att[0], att[1]], 1))
    for b, hp in units:
        share(b, hp, 3 - 2 * hp).wait_recv()
    for t in (1, 3):
        total = total + dot(wt[t], jnp.concatenate([got[t - 1, 0], got[t - 1, 1]], 1))
    for b, hp in units:
        relay(b, hp).wait_recv()
    total = total + dot(wt[2], jnp.concatenate([got[1, 0], got[1, 1]], 1))
    out_ref[...] = total.astype(BF16)

    for level, p in all1:
        phase1(level, p).wait_send()
    for level, j in all2:
        phase2(level, j).wait_send()
    for level in (2,) + FAR:
        phase3(level).wait_send()
    for which in range(3):
        neighbour(which, True).wait_send()
        neighbour(which, False).wait_send()
    for t in range(1, heads):
        weights(t).wait_send()
    weights_swap().wait_send()
    for b, hp in units:
        share(b, hp, 1).wait_send()
        share(b, hp, 3).wait_send()
        relay(b, hp).wait_send()


def solution(mesh):
    devices, heads = mesh.shape["seq"], mesh.shape["head"]

    def shards(q, k, v, w):
        rows, width = q.shape
        lanes = w.shape[1] // heads
        vmem = pl.BlockSpec(memory_space=pltpu.VMEM)
        dma = pltpu.SemaphoreType.DMA

        def gather(level):
            return pltpu.VMEM((2 ** (level - 3), 2, 3, 4 * (rows >> level), 128), BF16)

        def stage(level):
            return pltpu.VMEM((4 * (rows >> level), 128), BF16)

        return pl.pallas_call(
            functools.partial(kernel, devices, heads),
            out_shape=jax.ShapeDtypeStruct((lanes, rows), BF16),
            in_specs=[pl.BlockSpec(memory_space=pltpu.HBM)] * 4,
            out_specs=vmem,
            scratch_shapes=[
                pltpu.VMEM((rows, width), BF16),
                pltpu.VMEM((rows, width), BF16),
                pltpu.VMEM((rows, width), BF16),
                pltpu.VMEM((width, lanes), BF16),
                pltpu.VMEM((2, 2, 2, HALF, BLOCK), BF16),
                pltpu.VMEM((2, 2, BLOCK, width), BF16),
                pltpu.VMEM((2, 4 * HALF, 128), BF16),
                pltpu.VMEM((3, 4 * HALF, 128), BF16),
                gather(3), gather(4), gather(5), gather(6),
                pltpu.VMEM((2, 4 * HALF, 128), BF16),
                stage(2), stage(3), stage(4), stage(5), stage(6),
                pltpu.VMEM((4, 128, 256), BF16),
                pltpu.VMEM((2, 256, 128), BF16),
                pltpu.VMEM((2, 128, 256), BF16),
                pltpu.VMEM((4, 512, 128), BF16),
                pltpu.VMEM((4, 512, 128), BF16),
                pltpu.VMEM((128, 512), BF16),
                pltpu.VMEM((2, 2, 384, 128), BF16),
                pltpu.VMEM((2, 2, 384, 128), BF16),
                pltpu.VMEM((2, 2, 128, 384), BF16),
                pltpu.VMEM((heads - 1, 2, BLOCK, lanes), BF16),
                pltpu.VMEM((heads, lanes, width), BF16),
                pltpu.VMEM((2, width, BLOCK), BF16),
                pltpu.VMEM((heads - 1, 2, width, BLOCK), BF16),
                pltpu.VMEM((4, 8, 256), F32),
                pltpu.VMEM((4, 8, 256), F32),
                pltpu.VMEM((4, HEAD_DIM, 256), F32),
                dma((4,)),
                dma((5, 3)), dma((5, 3)), dma((13,)), dma((13,)), dma((5,)), dma((5,)),
                dma((3, 2)), dma((3, 2)), dma((heads,)), dma((heads,)),
                dma((2, 2, 2)), dma((2, 2, 2)), dma((2, 2)), dma((2, 2)),
            ],
            compiler_params=pltpu.CompilerParams(
                collective_id=0, has_side_effects=True, vmem_limit_bytes=60 * 1024 * 1024
            ),
            cost_estimate=pl.CostEstimate(
                flops=2_000_000_000, bytes_accessed=1_200_000, transcendentals=1_600_000
            ),
        )(q, k, v, w)

    placed = (P("seq", "head"), P("seq", "head"), P("seq", "head"), P("head", None))
    return jax.shard_map(
        shards, mesh=mesh, in_specs=placed, out_specs=P("head", "seq"), check_vma=False
    )
```

```python
import functools

import jax
import jax.numpy as jnp
from jax import lax
from jax.experimental import pallas as pl
from jax.experimental.pallas import tpu as pltpu
from jax.sharding import PartitionSpec as P

HEAD_DIM = 64
BLOCK = 128
LEVELS = 6
HALF = BLOCK // 2
F32 = jnp.float32
BF16 = jnp.bfloat16
MESH = pl.DeviceIdType.MESH
FAR = (3, 4, 5, 6)
OFF = -1e30


def dot(a, b):
    return jnp.dot(a, b, preferred_element_type=F32)


def iota(shape, dim):
    return lax.broadcasted_iota(jnp.int32, shape, dim)


def pool(rows, fine, level, repeat):
    r, c = iota((rows, fine), 0), iota((rows, fine), 1)
    hit = (c >> level) == (r & (repeat - 1))
    return jnp.where(hit, 2.0**-level, 0.0).astype(BF16)


def unpack(n):
    r, c = iota((256, 256), 0), iota((256, 256), 1)
    group, inside = r >> 6, r & 63
    source, row = inside // n, inside & (n - 1)
    return jnp.where(c == source * (4 * n) + group * n + row, 1.0, 0.0).astype(BF16)


def scores_top(s, slabs):
    top = None
    for start, rows, bias in slabs:
        m = jnp.max(s[start : start + rows], axis=0, keepdims=True)
        if bias is not None:
            m = m + bias
        top = m if top is None else jnp.maximum(top, m)
    return top


def attend(k, vt, q, slabs):
    s = dot(k, q)
    top = scores_top(s, slabs)
    parts, total = [], None
    for start, rows, bias in slabs:
        shift = top if bias is None else top - bias
        p = jnp.exp(s[start : start + rows] - shift)
        t = jnp.sum(p, axis=0, keepdims=True)
        total = t if total is None else total + t
        parts.append(p.astype(BF16))
    o = dot(vt, jnp.concatenate(parts, 0))
    o = jnp.concatenate([o[:HEAD_DIM, :BLOCK], o[HEAD_DIM:, BLOCK:]], 1)
    return top, total, o


def merge(a, b):
    top = jnp.maximum(a[0], b[0])
    fa, fb = jnp.exp(a[0] - top), jnp.exp(b[0] - top)
    return top, a[1] * fa + b[1] * fb, a[2] * fa + b[2] * fb


def kernel(
    devices, heads,
    q_hbm, k_hbm, v_hbm, w_hbm, out_ref,
    q_ref, k_ref, v_ref, w_own, rim, near, g2, g3, g4, g5, g6, s2, s3, s4, s5, s6,
    qbd, kb, vbt, kc, vct, wg, wt, att, got, st_m, st_l, st_o, in_s,
    p1_s, p1_r, p2_s, p2_r, p3_s, p3_r, near_s, near_r, w_s, w_r, att_s, att_r,
):
    d = lax.axis_index("seq")
    x = lax.axis_index("head")
    core = d % 2
    gathers = {3: g3, 4: g4, 5: g5, 6: g6}
    stages = {2: s2, 3: s3, 4: s4, 5: s5, 6: s6}

    def seq(steps):
        return (d + steps + 2 * devices) % devices

    def group(level):
        return 2 ** (level - 2)

    def far_steps(level, p):
        g = group(level)
        if p == 0:
            return 2 * g
        if p == 1:
            return -2 * g
        return (3 - 6 * ((d // g) % 2)) * g

    def remote(src, dst, send, recv, axis, target):
        return pltpu.make_async_remote_copy(
            src_ref=src, dst_ref=dst, send_sem=send, recv_sem=recv,
            device_id={axis: target}, device_id_type=MESH,
        )

    def far_target(level, p):
        target = seq(far_steps(level, p))
        if level == 4 and p == 2:
            target = target + 2 - 4 * ((target // 2) % 2)
        return target

    def phase1(level, p):
        at = (level - 2, p)
        rank = (d % group(level)) // 2
        if level == 2:
            dst = g2.at[p]
        elif level == 4 and p == 2:
            dst = g4.at[1 - rank, core, p]
        else:
            dst = gathers[level].at[rank, core, p]
        return remote(stages[level], dst, p1_s.at[at], p1_r.at[at], "seq", far_target(level, p))

    odd = (d // 2) % 2

    def phase2_target(level, j):
        if level == 3:
            return seq((1, 5)[j - 1] * 2 * (1 - 2 * odd))
        chips = group(level) // 2
        mine = (d // 2) % chips
        return d - 2 * mine + 2 * ((mine + j) % chips)

    def phase2(level, j):
        slot = {3: 0, 4: 2, 5: 3, 6: 6}[level] + j - 1
        if level == 3:
            src = g3.at[0, core, 2]
            dst = g3.at[0, core, 1 - odd if j == 1 else odd]
        else:
            src = dst = gathers[level].at[(d // 2) % (group(level) // 2), core]
        return remote(src, dst, p2_s.at[slot], p2_r.at[slot], "seq", phase2_target(level, j))

    def phase3(level):
        if level == 2:
            src, dst = g2.at[core], g2.at[2]
        else:
            src = dst = gathers[level].at[:, core]
        slot = level - 2
        return remote(src, dst, p3_s.at[slot], p3_r.at[slot], "seq", d + 1 - 2 * core)

    def neighbour(up):
        side = 0 if up else 1
        return remote(
            rim.at[side], near.at[side], near_s.at[side], near_r.at[side], "seq", seq(1 if up else -1)
        )

    def weights(t):
        to = (x + t) % heads
        width = wg.shape[3]
        rows = pl.ds(pl.multiple_of(core * BLOCK, BLOCK), BLOCK)
        src = w_hbm.at[rows, pl.ds(pl.multiple_of(to * width, width), width)]
        return remote(src, wg.at[t - 1, core], w_s.at[t - 1], w_r.at[t - 1], "head", to)

    def weights_swap():
        block = wg.at[:, core]
        slot = heads - 1
        return remote(block, block, w_s.at[slot], w_r.at[slot], "seq", d + 1 - 2 * core)

    def share(b, t):
        at = (b, t - 1)
        return remote(att.at[b], got.at[t - 1, b], att_s.at[at], att_r.at[at], "head", (x + t) % heads)

    far1 = [(6, 0), (6, 1), (6, 2), (5, 0), (5, 1), (5, 2), (4, 2), (4, 0), (4, 1), (3, 2)]
    two1 = [(2, 0), (2, 1)]
    all1 = far1 + two1
    all2 = [(3, 1), (3, 2)] + [(level, j) for level in (4, 5, 6) for j in range(1, group(level) // 2)]

    def pass_on(level):
        for other, j in all2:
            if other == level:
                phase2(level, j).start()

    def passed(level):
        for other, j in all2:
            if other == level:
                phase2(level, j).wait_recv()

    barrier = pltpu.get_barrier_semaphore()
    targets = [("seq", far_target(level, p)) for level, p in all1]
    targets += [("seq", phase2_target(6, j)) for j in range(1, 8)]
    targets += [("seq", phase2_target(3, 2))]
    targets += [("seq", seq(1)), ("seq", seq(-1))]
    targets += [("head", (x + t) % heads) for t in range(1, heads)]
    for axis, target in targets:
        pl.semaphore_signal(barrier, inc=1, device_id={axis: target}, device_id_type=MESH)
    width = wg.shape[3]
    own = pl.ds(pl.multiple_of(x * width, width), width)
    loads = [
        pltpu.make_async_copy(src, dst, in_s.at[i])
        for i, (src, dst) in enumerate(
            [(k_hbm, k_ref), (v_hbm, v_ref), (q_hbm, q_ref), (w_hbm.at[:, own], w_own)]
        )
    ]
    for load in loads:
        load.start()

    pools = jnp.concatenate(
        [pool(BLOCK, 256, 1, 128), pool(64, 256, 2, 64), pool(32, 256, 3, 32), pool(16, 256, 4, 16),
         pool(32, 256, 5, 8), pool(16, 256, 6, 4)], 0)
    loads[0].wait()
    loads[1].wait()
    k, v = k_ref[...], v_ref[...]
    ck, cv = dot(pools, k), dot(pools, v)
    blocks = [ck[:, :128], ck[:, 128:], cv[:, :128], cv[:, 128:]]
    for level, start, n in ((2, 128, 64), (3, 192, 32), (4, 224, 16)):
        for c in range(4):
            stages[level][c * n : (c + 1) * n, :] = blocks[c][start : start + n].astype(BF16)
    for level, start, n in ((5, 240, 8), (6, 272, 4)):
        owner = iota((4 * n, 128), 0) // n
        packed = blocks[0][start : start + 4 * n]
        for c in range(1, 4):
            packed = jnp.where(owner == c, blocks[c][start : start + 4 * n], packed)
        stages[level][...] = packed.astype(BF16)
    fine = [k[:, :128], k[:, 128:], v[:, :128], v[:, 128:]]
    for side in range(2):
        edge = BLOCK * (1 - side)
        for c in range(4):
            rim[side, c * BLOCK : (c + 1) * BLOCK, :] = fine[c][edge : edge + BLOCK]
            rim[side, 512 + c * HALF : 512 + (c + 1) * HALF, :] = blocks[c][side * HALF : (side + 1) * HALF].astype(BF16)

    loads[2].wait()
    qt = (q_ref[...].astype(F32) * HEAD_DIM**-0.5).T
    feature = iota((BLOCK, BLOCK), 0)
    for b in range(2):
        for hp in range(2):
            part = qt[hp * BLOCK : (hp + 1) * BLOCK, b * BLOCK : (b + 1) * BLOCK]
            low = jnp.where(feature < HEAD_DIM, part, 0.0)
            high = jnp.where(feature < HEAD_DIM, 0.0, part)
            qbd[b, hp] = jnp.concatenate([low, high], 1).astype(BF16)

    def keep(u, state):
        st_m[u, 0:1, :], st_l[u, 0:1, :], st_o[u] = state

    def kept(u):
        return st_m[u, 0:1, :], st_l[u, 0:1, :], st_o[u]

    units = [(b, hp) for b in range(2) for hp in range(2)]
    for hp in range(2):
        lanes = slice(hp * BLOCK, (hp + 1) * BLOCK)
        vt = v_ref[:, lanes].T
        kk = k_ref[:, lanes]
        for b in range(2):
            keep(b * 2 + hp, attend(kk, vt, qbd[b, hp], [(0, 256, None)]))

    loads[3].wait()
    wt[0] = w_own[...].T

    pl.semaphore_wait(barrier, len(targets))
    for level, p in far1:
        phase1(level, p).start()
    neighbour(True).start()
    neighbour(False).start()
    for level, p in two1:
        phase1(level, p).start()
    for t in range(1, heads):
        weights(t).start()

    for level, p in far1:
        phase1(level, p).wait_recv()
        if (level, p) in ((6, 2), (5, 2), (4, 1), (3, 2)):
            pass_on(level)

    for level, p in two1:
        phase1(level, p).wait_recv()
    phase3(2).start()
    neighbour(True).wait_recv()
    neighbour(False).wait_recv()
    half_pool = pool(HALF, BLOCK, 1, HALF)
    lower_ok = jnp.where(d > 0, 0.0, OFF).astype(F32)
    upper_ok = jnp.where(d < devices - 1, 0.0, OFF).astype(F32)

    def far_bias(level):
        g, out = group(level), []
        e, last = d // g, devices // g - 1
        steps = (-2, 2, 3 - 6 * (e % 2))
        for step in steps:
            there = e + step
            out.append(jnp.where((there >= 0) & (there <= last), 0.0, OFF).astype(F32))
        return out

    bias2 = far_bias(2)
    phase3(2).wait_recv()
    for c in range(4):
        kind, hp = c // 2, c % 2
        strip = slice(c * BLOCK, (c + 1) * BLOCK)
        rows = slice(c * HALF, (c + 1) * HALF)
        half = slice(512 + c * HALF, 512 + (c + 1) * HALF)
        pooled = [dot(half_pool, near[side, strip, :]).astype(BF16) for side in range(2)]
        common = [near[0, half, :], near[1, half, :]] + [g2[p, rows, :] for p in range(3)]
        for b in range(2):
            full = jnp.concatenate([near[b, strip, :], pooled[1 - b]] + common, 0)
            if kind == 0:
                kb[b, hp] = full
            else:
                vbt[b, hp] = full.T
    for b, hp in units:
        first, second = (lower_ok, upper_ok) if b == 0 else (upper_ok, lower_ok)
        slabs = [(0, 128, first), (128, 64, second), (192, 64, lower_ok), (256, 64, upper_ok)]
        slabs += [(320 + 64 * p, 64, bias2[p]) for p in range(3)]
        u = b * 2 + hp
        keep(u, merge(kept(u), attend(kb[b, hp], vbt[b, hp], qbd[b, hp], slabs)))
        if u in (1, 3):
            for level in FAR[:3] if u == 1 else FAR[3:]:
                passed(level)
                phase3(level).start()

    for t in range(1, heads):
        weights(t).wait_recv()
    weights_swap().start()

    def far_chunk(i):
        slabs, keys, values = [], ([], []), ([], [])
        for level in FAR[2 * i : 2 * i + 2]:
            phase3(level).wait_recv()
            n = 256 // 2**level
            g = group(level)
            for p, bias in enumerate(far_bias(level)):
                slabs.append((64 * len(slabs), 64, bias))
                whole = gathers[level][:, :, p].reshape(g, 4 * n, 128)
                if n >= 16:
                    four = [whole[:, c * n : (c + 1) * n, :].reshape(64, 128) for c in range(4)]
                else:
                    moved = dot(unpack(n), whole.reshape(256, 128)).astype(BF16)
                    four = [moved[c * 64 : (c + 1) * 64] for c in range(4)]
                for hp in range(2):
                    keys[hp].append(four[hp])
                    values[hp].append(four[2 + hp])
        for hp in range(2):
            kc[i, hp] = jnp.concatenate(keys[hp], 0)
            vct[i, hp] = jnp.concatenate(values[hp], 0).T
        return slabs

    slabs = far_chunk(0)
    for b, hp in units:
        u = b * 2 + hp
        keep(u, merge(kept(u), attend(kc[0, hp], vct[0, hp], qbd[b, hp], slabs)))
    weights_swap().wait_recv()
    for t in range(1, heads):
        wt[t] = wg[t - 1].reshape(2 * BLOCK, width).T
    slabs = far_chunk(1)
    for b, hp in units:
        u = b * 2 + hp
        _, total, o = merge(kept(u), attend(kc[1, hp], vct[1, hp], qbd[b, hp], slabs))
        o = (o / total).astype(BF16)
        att[b, hp * BLOCK : (hp + 1) * BLOCK, :] = jnp.concatenate([o[:, :BLOCK], o[:, BLOCK:]], 0)
        if hp == 1:
            for t in (2, 1, 3):
                share(b, t).start()

    total = dot(wt[0], jnp.concatenate([att[0], att[1]], 1))
    for t in (1, 3, 2):
        for b in range(2):
            share(b, t).wait_recv()
        total = total + dot(wt[t], jnp.concatenate([got[t - 1, 0], got[t - 1, 1]], 1))
    out_ref[...] = total.astype(BF16)

    for level, p in all1:
        phase1(level, p).wait_send()
    for level, j in all2:
        phase2(level, j).wait_send()
    for level in (2,) + FAR:
        phase3(level).wait_send()
    neighbour(True).wait_send()
    neighbour(False).wait_send()
    for t in range(1, heads):
        weights(t).wait_send()
    weights_swap().wait_send()
    for b in range(2):
        for t in range(1, heads):
            share(b, t).wait_send()


def solution(mesh):
    devices, heads = mesh.shape["seq"], mesh.shape["head"]

    def shards(q, k, v, w):
        rows, width = q.shape
        lanes = w.shape[1] // heads
        vmem = pl.BlockSpec(memory_space=pltpu.VMEM)
        dma = pltpu.SemaphoreType.DMA

        def gather(level):
            return pltpu.VMEM((2 ** (level - 3), 2, 3, 4 * (rows >> level), 128), BF16)

        def stage(level):
            return pltpu.VMEM((4 * (rows >> level), 128), BF16)

        return pl.pallas_call(
            functools.partial(kernel, devices, heads),
            out_shape=jax.ShapeDtypeStruct((lanes, rows), BF16),
            in_specs=[pl.BlockSpec(memory_space=pltpu.HBM)] * 4,
            out_specs=vmem,
            scratch_shapes=[
                pltpu.VMEM((rows, width), BF16),
                pltpu.VMEM((rows, width), BF16),
                pltpu.VMEM((rows, width), BF16),
                pltpu.VMEM((width, lanes), BF16),
                pltpu.VMEM((2, 4 * (BLOCK + HALF), 128), BF16),
                pltpu.VMEM((2, 4 * (BLOCK + HALF), 128), BF16),
                pltpu.VMEM((3, 4 * HALF, 128), BF16),
                gather(3), gather(4), gather(5), gather(6),
                stage(2), stage(3), stage(4), stage(5), stage(6),
                pltpu.VMEM((2, 2, 128, 256), BF16),
                pltpu.VMEM((2, 2, 512, 128), BF16),
                pltpu.VMEM((2, 2, 128, 512), BF16),
                pltpu.VMEM((2, 2, 384, 128), BF16),
                pltpu.VMEM((2, 2, 128, 384), BF16),
                pltpu.VMEM((heads - 1, 2, BLOCK, lanes), BF16),
                pltpu.VMEM((heads, lanes, width), BF16),
                pltpu.VMEM((2, width, BLOCK), BF16),
                pltpu.VMEM((heads - 1, 2, width, BLOCK), BF16),
                pltpu.VMEM((4, 8, 256), F32),
                pltpu.VMEM((4, 8, 256), F32),
                pltpu.VMEM((4, HEAD_DIM, 256), F32),
                dma((4,)),
                dma((5, 3)), dma((5, 3)), dma((13,)), dma((13,)), dma((5,)), dma((5,)),
                dma((2,)), dma((2,)), dma((heads,)), dma((heads,)),
                dma((2, heads - 1)), dma((2, heads - 1)),
            ],
            compiler_params=pltpu.CompilerParams(
                collective_id=0, has_side_effects=True, vmem_limit_bytes=55040 * 1024
            ),
            cost_estimate=pl.CostEstimate(
                flops=2_000_000_000, bytes_accessed=1_200_000, transcendentals=1_600_000
            ),
        )(q, k, v, w)

    placed = (P("seq", "head"), P("seq", "head"), P("seq", "head"), P("head", None))
    return jax.shard_map(
        shards, mesh=mesh, in_specs=placed, out_specs=P("head", "seq"), check_vma=False
    )
```

```python
import functools

import jax
import jax.numpy as jnp
from jax import lax
from jax.experimental import pallas as pl
from jax.experimental.pallas import tpu as pltpu
from jax.sharding import PartitionSpec as P

HEAD_DIM = 64
BLOCK = 128
LEVELS = 6
HALF = BLOCK // 2
F32 = jnp.float32
BF16 = jnp.bfloat16
MESH = pl.DeviceIdType.MESH
FAR = (3, 4, 5, 6)
OFF = -1e30


def dot(a, b):
    return jnp.dot(a, b, preferred_element_type=F32)


def iota(shape, dim):
    return lax.broadcasted_iota(jnp.int32, shape, dim)


def pool(rows, fine, level, repeat):
    r, c = iota((rows, fine), 0), iota((rows, fine), 1)
    hit = (c >> level) == (r & (repeat - 1))
    return jnp.where(hit, 2.0**-level, 0.0).astype(BF16)


def unpack(n):
    r, c = iota((256, 256), 0), iota((256, 256), 1)
    group, inside = r >> 6, r & 63
    source, row = inside // n, inside & (n - 1)
    return jnp.where(c == source * (4 * n) + group * n + row, 1.0, 0.0).astype(BF16)


def scores_top(s, slabs):
    top = None
    for start, rows, bias in slabs:
        m = jnp.max(s[start : start + rows], axis=0, keepdims=True)
        if bias is not None:
            m = m + bias
        top = m if top is None else jnp.maximum(top, m)
    return top


def attend(k, vt, q, slabs):
    s = dot(k, q)
    top = scores_top(s, slabs)
    parts, total = [], None
    for start, rows, bias in slabs:
        shift = top if bias is None else top - bias
        p = jnp.exp(s[start : start + rows] - shift)
        t = jnp.sum(p, axis=0, keepdims=True)
        total = t if total is None else total + t
        parts.append(p.astype(BF16))
    o = dot(vt, jnp.concatenate(parts, 0))
    o = jnp.concatenate([o[:HEAD_DIM, :BLOCK], o[HEAD_DIM:, BLOCK:]], 1)
    return top, total, o


def merge(a, b):
    top = jnp.maximum(a[0], b[0])
    fa, fb = jnp.exp(a[0] - top), jnp.exp(b[0] - top)
    return top, a[1] * fa + b[1] * fb, a[2] * fa + b[2] * fb


def kernel(
    devices, heads,
    q_hbm, k_hbm, v_hbm, w_hbm, out_ref,
    q_ref, k_ref, v_ref, w_own, rim, near, g2, g3, g4, g5, g6, s2, s3, s4, s5, s6,
    qbd, kb, vbt, kc, vct, wg, wt, att, got, st_m, st_l, st_o, grants, in_s,
    p1_s, p1_r, p2_s, p2_r, p3_s, p3_r, near_s, near_r, w_s, w_r, att_s, att_r,
):
    d = lax.axis_index("seq")
    x = lax.axis_index("head")
    core = d % 2
    gathers = {3: g3, 4: g4, 5: g5, 6: g6}
    stages = {2: s2, 3: s3, 4: s4, 5: s5, 6: s6}

    def seq(steps):
        return (d + steps + 2 * devices) % devices

    def group(level):
        return 2 ** (level - 2)

    def far_steps(level, p):
        g = group(level)
        if p == 0:
            return 2 * g
        if p == 1:
            return -2 * g
        return (3 - 6 * ((d // g) % 2)) * g

    def remote(src, dst, send, recv, axis, target):
        return pltpu.make_async_remote_copy(
            src_ref=src, dst_ref=dst, send_sem=send, recv_sem=recv,
            device_id={axis: target}, device_id_type=MESH,
        )

    def far_target(level, p):
        target = seq(far_steps(level, p))
        if level == 4 and p == 2:
            target = target + 2 - 4 * ((target // 2) % 2)
        return target

    def phase1(level, p):
        at = (level - 2, p)
        rank = (d % group(level)) // 2
        if level == 2:
            dst = g2.at[p]
        elif level == 4 and p == 2:
            dst = g4.at[1 - rank, core, p]
        else:
            dst = gathers[level].at[rank, core, p]
        return remote(stages[level], dst, p1_s.at[at], p1_r.at[at], "seq", far_target(level, p))

    odd = (d // 2) % 2

    def phase2_target(level, j):
        if level == 3:
            return seq((1, 5)[j - 1] * 2 * (1 - 2 * odd))
        chips = group(level) // 2
        mine = (d // 2) % chips
        return d - 2 * mine + 2 * ((mine + j) % chips)

    def phase2(level, j):
        slot = {3: 0, 4: 2, 5: 3, 6: 6}[level] + j - 1
        if level == 3:
            src = g3.at[0, core, 2]
            dst = g3.at[0, core, 1 - odd if j == 1 else odd]
        else:
            src = dst = gathers[level].at[(d // 2) % (group(level) // 2), core]
        return remote(src, dst, p2_s.at[slot], p2_r.at[slot], "seq", phase2_target(level, j))

    def phase3(level):
        if level == 2:
            src, dst = g2.at[core], g2.at[2]
        else:
            src = dst = gathers[level].at[:, core]
        slot = level - 2
        return remote(src, dst, p3_s.at[slot], p3_r.at[slot], "seq", d + 1 - 2 * core)

    def neighbour(up):
        side = 0 if up else 1
        return remote(
            rim.at[side], near.at[side], near_s.at[side], near_r.at[side], "seq", seq(1 if up else -1)
        )

    def weights(t):
        to = (x + t) % heads
        width = wg.shape[3]
        rows = pl.ds(pl.multiple_of(core * BLOCK, BLOCK), BLOCK)
        src = w_hbm.at[rows, pl.ds(pl.multiple_of(to * width, width), width)]
        return remote(src, wg.at[t - 1, core], w_s.at[t - 1], w_r.at[t - 1], "head", to)

    def weights_swap():
        block = wg.at[:, core]
        slot = heads - 1
        return remote(block, block, w_s.at[slot], w_r.at[slot], "seq", d + 1 - 2 * core)

    def share(b, t):
        at = (b, t - 1)
        return remote(att.at[b], got.at[t - 1, b], att_s.at[at], att_r.at[at], "head", (x + t) % heads)

    far1 = [(6, 0), (6, 1), (6, 2), (5, 0), (5, 1), (5, 2), (4, 2), (4, 0), (4, 1), (3, 2)]
    two1 = [(2, 0), (2, 1)]
    all1 = far1 + two1
    all2 = [(3, 1), (3, 2)] + [(level, j) for level in (4, 5, 6) for j in range(1, group(level) // 2)]

    def pass_on(level):
        for other, j in all2:
            if other == level:
                phase2(level, j).start()

    def passed(level):
        for other, j in all2:
            if other == level:
                phase2(level, j).wait_recv()

    other = (1, 0, 2)
    relations = {("far", level, p): ("seq", far_target(level, p), ("far", level, other[p])) for level, p in all1}
    for j in range(1, 8):
        relations["mate", j] = ("seq", phase2_target(6, j), ("mate", 8 - j))
    relations["pass", 2] = ("seq", phase2_target(3, 2), ("pass", 2))
    for up in (True, False):
        relations["near", up] = ("seq", seq(1 if up else -1), ("near", not up))
    for t in range(1, heads):
        relations["head", t] = ("head", (x + t) % heads, ("head", heads - t))
    slots = {name: i for i, name in enumerate(relations)}
    above = {name: target > (d if axis == "seq" else x) for name, (axis, target, _) in relations.items()}

    barrier = pltpu.get_barrier_semaphore()

    def signal(semaphore, name):
        axis, target, _ = relations[name]
        pl.semaphore_signal(semaphore, inc=1, device_id={axis: target}, device_id_type=MESH)

    def on(condition, *steps):
        @pl.when(condition)
        def _():
            for step in steps:
                step()

    def granted(name):
        on(above[name], lambda: pl.semaphore_wait(grants.at[slots[name]], 1))

    def send_below(level, p):
        on(jnp.logical_not(above["far", level, p]), lambda: phase1(level, p).start())

    def send_above(level, p):
        name = ("far", level, p)
        on(above[name], lambda: pl.semaphore_wait(grants.at[slots[name]], 1), lambda: phase1(level, p).start())

    for name in relations:
        on(above[name], lambda: signal(barrier, name))
    width = wg.shape[3]
    own = pl.ds(pl.multiple_of(x * width, width), width)
    loads = [
        pltpu.make_async_copy(src, dst, in_s.at[i])
        for i, (src, dst) in enumerate(
            [(k_hbm, k_ref), (v_hbm, v_ref), (q_hbm, q_ref), (w_hbm.at[:, own], w_own)]
        )
    ]
    for load in loads:
        load.start()

    pools = jnp.concatenate(
        [pool(BLOCK, 256, 1, 128), pool(64, 256, 2, 64), pool(32, 256, 3, 32), pool(16, 256, 4, 16),
         pool(32, 256, 5, 8), pool(16, 256, 6, 4)], 0)
    loads[0].wait()
    loads[1].wait()
    k, v = k_ref[...], v_ref[...]
    ck, cv = dot(pools, k), dot(pools, v)
    blocks = [ck[:, :128], ck[:, 128:], cv[:, :128], cv[:, 128:]]
    for level, start, n in ((2, 128, 64), (3, 192, 32), (4, 224, 16)):
        for c in range(4):
            stages[level][c * n : (c + 1) * n, :] = blocks[c][start : start + n].astype(BF16)
    for level, start, n in ((5, 240, 8), (6, 272, 4)):
        owner = iota((4 * n, 128), 0) // n
        packed = blocks[0][start : start + 4 * n]
        for c in range(1, 4):
            packed = jnp.where(owner == c, blocks[c][start : start + 4 * n], packed)
        stages[level][...] = packed.astype(BF16)
    fine = [k[:, :128], k[:, 128:], v[:, :128], v[:, 128:]]
    for side in range(2):
        edge = BLOCK * (1 - side)
        for c in range(4):
            rim[side, c * BLOCK : (c + 1) * BLOCK, :] = fine[c][edge : edge + BLOCK]
            rim[side, 512 + c * HALF : 512 + (c + 1) * HALF, :] = blocks[c][side * HALF : (side + 1) * HALF].astype(BF16)

    below = sum(jnp.where(above[name], 0, 1) for name in relations)
    on(below > 0, lambda: pl.semaphore_wait(barrier, below))
    for name in relations:
        on(jnp.logical_not(above[name]), lambda: signal(grants.at[slots[relations[name][2]]], name))
    for level, p in all1:
        send_below(level, p)
    granted(("near", True))
    granted(("near", False))
    neighbour(True).start()
    neighbour(False).start()
    for t in range(1, heads):
        granted(("head", t))
        weights(t).start()

    loads[2].wait()
    qt = (q_ref[...].astype(F32) * HEAD_DIM**-0.5).T
    feature = iota((BLOCK, BLOCK), 0)
    for b in range(2):
        for hp in range(2):
            part = qt[hp * BLOCK : (hp + 1) * BLOCK, b * BLOCK : (b + 1) * BLOCK]
            low = jnp.where(feature < HEAD_DIM, part, 0.0)
            high = jnp.where(feature < HEAD_DIM, 0.0, part)
            qbd[b, hp] = jnp.concatenate([low, high], 1).astype(BF16)

    def keep(u, state):
        st_m[u, 0:1, :], st_l[u, 0:1, :], st_o[u] = state

    def kept(u):
        return st_m[u, 0:1, :], st_l[u, 0:1, :], st_o[u]

    units = [(b, hp) for b in range(2) for hp in range(2)]
    for hp in range(2):
        lanes = slice(hp * BLOCK, (hp + 1) * BLOCK)
        vt = v_ref[:, lanes].T
        kk = k_ref[:, lanes]
        for b in range(2):
            keep(b * 2 + hp, attend(kk, vt, qbd[b, hp], [(0, 256, None)]))

    for level, p in two1 + [(3, 2), (4, 2), (4, 0), (4, 1), (5, 0), (5, 1), (5, 2)]:
        send_above(level, p)
    for j in range(1, 8):
        granted(("mate", j))
    granted(("pass", 2))
    loads[3].wait()
    wt[0] = w_own[...].T

    for level, p in two1:
        phase1(level, p).wait_recv()
    phase3(2).start()
    for level, p in ((3, 2), (4, 2), (4, 0), (4, 1)):
        phase1(level, p).wait_recv()
    pass_on(3)
    pass_on(4)
    neighbour(True).wait_recv()
    neighbour(False).wait_recv()
    half_pool = pool(HALF, BLOCK, 1, HALF)
    lower_ok = jnp.where(d > 0, 0.0, OFF).astype(F32)
    upper_ok = jnp.where(d < devices - 1, 0.0, OFF).astype(F32)

    def far_bias(level):
        g, out = group(level), []
        e, last = d // g, devices // g - 1
        steps = (-2, 2, 3 - 6 * (e % 2))
        for step in steps:
            there = e + step
            out.append(jnp.where((there >= 0) & (there <= last), 0.0, OFF).astype(F32))
        return out

    bias2 = far_bias(2)
    phase3(2).wait_recv()
    for c in range(4):
        kind, hp = c // 2, c % 2
        strip = slice(c * BLOCK, (c + 1) * BLOCK)
        rows = slice(c * HALF, (c + 1) * HALF)
        half = slice(512 + c * HALF, 512 + (c + 1) * HALF)
        pooled = [dot(half_pool, near[side, strip, :]).astype(BF16) for side in range(2)]
        common = [near[0, half, :], near[1, half, :]] + [g2[p, rows, :] for p in range(3)]
        for b in range(2):
            full = jnp.concatenate([near[b, strip, :], pooled[1 - b]] + common, 0)
            if kind == 0:
                kb[b, hp] = full
            else:
                vbt[b, hp] = full.T
    for b, hp in units:
        first, second = (lower_ok, upper_ok) if b == 0 else (upper_ok, lower_ok)
        slabs = [(0, 128, first), (128, 64, second), (192, 64, lower_ok), (256, 64, upper_ok)]
        slabs += [(320 + 64 * p, 64, bias2[p]) for p in range(3)]
        u = b * 2 + hp
        keep(u, merge(kept(u), attend(kb[b, hp], vbt[b, hp], qbd[b, hp], slabs)))
        if u == 1:
            for level in (3, 4):
                passed(level)
                phase3(level).start()
            for p in range(3):
                phase1(5, p).wait_recv()
            pass_on(5)

    for t in range(1, heads):
        weights(t).wait_recv()
    weights_swap().start()

    def far_chunk(i):
        slabs, keys, values = [], ([], []), ([], [])
        for level in FAR[2 * i : 2 * i + 2]:
            phase3(level).wait_recv()
            n = 256 // 2**level
            g = group(level)
            for p, bias in enumerate(far_bias(level)):
                slabs.append((64 * len(slabs), 64, bias))
                whole = gathers[level][:, :, p].reshape(g, 4 * n, 128)
                if n >= 16:
                    four = [whole[:, c * n : (c + 1) * n, :].reshape(64, 128) for c in range(4)]
                else:
                    moved = dot(unpack(n), whole.reshape(256, 128)).astype(BF16)
                    four = [moved[c * 64 : (c + 1) * 64] for c in range(4)]
                for hp in range(2):
                    keys[hp].append(four[hp])
                    values[hp].append(four[2 + hp])
        for hp in range(2):
            kc[i, hp] = jnp.concatenate(keys[hp], 0)
            vct[i, hp] = jnp.concatenate(values[hp], 0).T
        return slabs

    slabs = far_chunk(0)
    for b, hp in units:
        u = b * 2 + hp
        keep(u, merge(kept(u), attend(kc[0, hp], vct[0, hp], qbd[b, hp], slabs)))
    for p in range(3):
        send_above(6, p)
    passed(5)
    phase3(5).start()
    for p in range(3):
        phase1(6, p).wait_recv()
    pass_on(6)
    weights_swap().wait_recv()
    for t in range(1, heads):
        wt[t] = wg[t - 1].reshape(2 * BLOCK, width).T
    passed(6)
    phase3(6).start()
    slabs = far_chunk(1)
    for b, hp in units:
        u = b * 2 + hp
        _, total, o = merge(kept(u), attend(kc[1, hp], vct[1, hp], qbd[b, hp], slabs))
        o = (o / total).astype(BF16)
        att[b, hp * BLOCK : (hp + 1) * BLOCK, :] = jnp.concatenate([o[:, :BLOCK], o[:, BLOCK:]], 0)
        if hp == 1:
            for t in (2, 1, 3):
                share(b, t).start()

    total = dot(wt[0], jnp.concatenate([att[0], att[1]], 1))
    for t in (1, 3, 2):
        for b in range(2):
            share(b, t).wait_recv()
        total = total + dot(wt[t], jnp.concatenate([got[t - 1, 0], got[t - 1, 1]], 1))
    out_ref[...] = total.astype(BF16)

    for level, p in all1:
        phase1(level, p).wait_send()
    for level, j in all2:
        phase2(level, j).wait_send()
    for level in (2,) + FAR:
        phase3(level).wait_send()
    neighbour(True).wait_send()
    neighbour(False).wait_send()
    for t in range(1, heads):
        weights(t).wait_send()
    weights_swap().wait_send()
    for b in range(2):
        for t in range(1, heads):
            share(b, t).wait_send()


def solution(mesh):
    devices, heads = mesh.shape["seq"], mesh.shape["head"]

    def shards(q, k, v, w):
        rows, width = q.shape
        lanes = w.shape[1] // heads
        vmem = pl.BlockSpec(memory_space=pltpu.VMEM)
        dma = pltpu.SemaphoreType.DMA

        def gather(level):
            return pltpu.VMEM((2 ** (level - 3), 2, 3, 4 * (rows >> level), 128), BF16)

        def stage(level):
            return pltpu.VMEM((4 * (rows >> level), 128), BF16)

        return pl.pallas_call(
            functools.partial(kernel, devices, heads),
            out_shape=jax.ShapeDtypeStruct((lanes, rows), BF16),
            in_specs=[pl.BlockSpec(memory_space=pltpu.HBM)] * 4,
            out_specs=vmem,
            scratch_shapes=[
                pltpu.VMEM((rows, width), BF16),
                pltpu.VMEM((rows, width), BF16),
                pltpu.VMEM((rows, width), BF16),
                pltpu.VMEM((width, lanes), BF16),
                pltpu.VMEM((2, 4 * (BLOCK + HALF), 128), BF16),
                pltpu.VMEM((2, 4 * (BLOCK + HALF), 128), BF16),
                pltpu.VMEM((3, 4 * HALF, 128), BF16),
                gather(3), gather(4), gather(5), gather(6),
                stage(2), stage(3), stage(4), stage(5), stage(6),
                pltpu.VMEM((2, 2, 128, 256), BF16),
                pltpu.VMEM((2, 2, 512, 128), BF16),
                pltpu.VMEM((2, 2, 128, 512), BF16),
                pltpu.VMEM((2, 2, 384, 128), BF16),
                pltpu.VMEM((2, 2, 128, 384), BF16),
                pltpu.VMEM((heads - 1, 2, BLOCK, lanes), BF16),
                pltpu.VMEM((heads, lanes, width), BF16),
                pltpu.VMEM((2, width, BLOCK), BF16),
                pltpu.VMEM((heads - 1, 2, width, BLOCK), BF16),
                pltpu.VMEM((4, 8, 256), F32),
                pltpu.VMEM((4, 8, 256), F32),
                pltpu.VMEM((4, HEAD_DIM, 256), F32),
                pltpu.SemaphoreType.REGULAR((25,)),
                dma((4,)),
                dma((5, 3)), dma((5, 3)), dma((13,)), dma((13,)), dma((5,)), dma((5,)),
                dma((2,)), dma((2,)), dma((heads,)), dma((heads,)),
                dma((2, heads - 1)), dma((2, heads - 1)),
            ],
            compiler_params=pltpu.CompilerParams(
                collective_id=0, has_side_effects=True, vmem_limit_bytes=55040 * 1024
            ),
            cost_estimate=pl.CostEstimate(
                flops=2_000_000_000, bytes_accessed=1_200_000, transcendentals=1_600_000
            ),
        )(q, k, v, w)

    placed = (P("seq", "head"), P("seq", "head"), P("seq", "head"), P("head", None))
    return jax.shard_map(
        shards, mesh=mesh, in_specs=placed, out_specs=P("head", "seq"), check_vma=False
    )
```

```python
import functools

import jax
import jax.numpy as jnp
from jax import lax
from jax.experimental import pallas as pl
from jax.experimental.pallas import tpu as pltpu
from jax.sharding import PartitionSpec as P

HEAD_DIM = 64
BLOCK = 128
LEVELS = 6
HALF = BLOCK // 2
F32 = jnp.float32
BF16 = jnp.bfloat16
MESH = pl.DeviceIdType.MESH
FAR = (3, 4, 5, 6)
OFF = -1e30


def dot(a, b):
    return jnp.dot(a, b, preferred_element_type=F32)


def iota(shape, dim):
    return lax.broadcasted_iota(jnp.int32, shape, dim)


def pool(rows, fine, level, repeat):
    r, c = iota((rows, fine), 0), iota((rows, fine), 1)
    hit = (c >> level) == (r & (repeat - 1))
    return jnp.where(hit, 2.0**-level, 0.0).astype(BF16)


def unpack(n):
    r, c = iota((256, 256), 0), iota((256, 256), 1)
    group, inside = r >> 6, r & 63
    source, row = inside // n, inside & (n - 1)
    return jnp.where(c == source * (4 * n) + group * n + row, 1.0, 0.0).astype(BF16)


def scores_top(s, slabs):
    top = None
    for start, rows, bias in slabs:
        m = jnp.max(s[start : start + rows], axis=0, keepdims=True)
        if bias is not None:
            m = m + bias
        top = m if top is None else jnp.maximum(top, m)
    return top


def attend(k, vt, q, slabs):
    s = dot(k, q)
    top = scores_top(s, slabs)
    parts, total = [], None
    for start, rows, bias in slabs:
        shift = top if bias is None else top - bias
        p = jnp.exp(s[start : start + rows] - shift)
        t = jnp.sum(p, axis=0, keepdims=True)
        total = t if total is None else total + t
        parts.append(p.astype(BF16))
    o = dot(vt, jnp.concatenate(parts, 0))
    o = jnp.concatenate([o[:HEAD_DIM, :BLOCK], o[HEAD_DIM:, BLOCK:]], 1)
    return top, total, o


def merge(a, b):
    top = jnp.maximum(a[0], b[0])
    fa, fb = jnp.exp(a[0] - top), jnp.exp(b[0] - top)
    return top, a[1] * fa + b[1] * fb, a[2] * fa + b[2] * fb


def kernel(
    devices, heads,
    q_hbm, k_hbm, v_hbm, w_hbm, out_ref,
    q_ref, k_ref, v_ref, w_own, rim, near, g2, g3, g4, g5, g6, s2, s3, s4, s5, s6,
    qbd, kb, vbt, kc, vct, wg, wt, att, got, st_m, st_l, st_o, in_s,
    p1_s, p1_r, p2_s, p2_r, p3_s, p3_r, near_s, near_r, w_s, w_r, att_s, att_r,
):
    d = lax.axis_index("seq")
    x = lax.axis_index("head")
    core = d % 2
    gathers = {3: g3, 4: g4, 5: g5, 6: g6}
    stages = {2: s2, 3: s3, 4: s4, 5: s5, 6: s6}

    def seq(steps):
        return (d + steps + 2 * devices) % devices

    def group(level):
        return 2 ** (level - 2)

    def far_steps(level, p):
        g = group(level)
        if p == 0:
            return 2 * g
        if p == 1:
            return -2 * g
        return (3 - 6 * ((d // g) % 2)) * g

    def remote(src, dst, send, recv, axis, target):
        return pltpu.make_async_remote_copy(
            src_ref=src, dst_ref=dst, send_sem=send, recv_sem=recv,
            device_id={axis: target}, device_id_type=MESH,
        )

    def far_target(level, p):
        target = seq(far_steps(level, p))
        if level == 4 and p == 2:
            target = target + 2 - 4 * ((target // 2) % 2)
        return target

    def phase1(level, p):
        at = (level - 2, p)
        rank = (d % group(level)) // 2
        if level == 2:
            dst = g2.at[p]
        elif level == 4 and p == 2:
            dst = g4.at[1 - rank, core, p]
        else:
            dst = gathers[level].at[rank, core, p]
        return remote(stages[level], dst, p1_s.at[at], p1_r.at[at], "seq", far_target(level, p))

    odd = (d // 2) % 2

    def phase2_target(level, j):
        if level == 3:
            return seq((1, 5)[j - 1] * 2 * (1 - 2 * odd))
        chips = group(level) // 2
        mine = (d // 2) % chips
        return d - 2 * mine + 2 * ((mine + j) % chips)

    def phase2(level, j):
        slot = {3: 0, 4: 2, 5: 3, 6: 6}[level] + j - 1
        if level == 3:
            src = g3.at[0, core, 2]
            dst = g3.at[0, core, 1 - odd if j == 1 else odd]
        else:
            src = dst = gathers[level].at[(d // 2) % (group(level) // 2), core]
        return remote(src, dst, p2_s.at[slot], p2_r.at[slot], "seq", phase2_target(level, j))

    def phase3(level):
        if level == 2:
            src, dst = g2.at[core], g2.at[2]
        else:
            src = dst = gathers[level].at[:, core]
        slot = level - 2
        return remote(src, dst, p3_s.at[slot], p3_r.at[slot], "seq", d + 1 - 2 * core)

    def neighbour(up):
        side = 0 if up else 1
        return remote(
            rim.at[side], near.at[side], near_s.at[side], near_r.at[side], "seq", seq(1 if up else -1)
        )

    def weights(t):
        to = (x + t) % heads
        width = wg.shape[3]
        rows = pl.ds(pl.multiple_of(core * BLOCK, BLOCK), BLOCK)
        src = w_hbm.at[rows, pl.ds(pl.multiple_of(to * width, width), width)]
        return remote(src, wg.at[t - 1, core], w_s.at[t - 1], w_r.at[t - 1], "head", to)

    def weights_swap():
        block = wg.at[:, core]
        slot = heads - 1
        return remote(block, block, w_s.at[slot], w_r.at[slot], "seq", d + 1 - 2 * core)

    def share(b, t):
        at = (b, t - 1)
        return remote(att.at[b], got.at[t - 1, b], att_s.at[at], att_r.at[at], "head", (x + t) % heads)

    far1 = [(6, 0), (6, 1), (6, 2), (5, 0), (5, 1), (5, 2), (4, 2), (4, 0), (4, 1), (3, 2)]
    two1 = [(2, 0), (2, 1)]
    all1 = far1 + two1
    all2 = [(3, 1), (3, 2)] + [(level, j) for level in (4, 5, 6) for j in range(1, group(level) // 2)]

    def pass_on(level):
        for other, j in all2:
            if other == level:
                phase2(level, j).start()

    def passed(level):
        for other, j in all2:
            if other == level:
                phase2(level, j).wait_recv()

    width = wg.shape[3]
    own = pl.ds(pl.multiple_of(x * width, width), width)
    loads = [
        pltpu.make_async_copy(src, dst, in_s.at[i])
        for i, (src, dst) in enumerate(
            [(k_hbm, k_ref), (v_hbm, v_ref), (q_hbm, q_ref), (w_hbm.at[:, own], w_own)]
        )
    ]
    loads[0].start()
    loads[1].start()
    barrier = pltpu.get_barrier_semaphore()
    targets = [("seq", far_target(level, p)) for level, p in all1]
    targets += [("seq", phase2_target(6, j)) for j in range(1, 8)]
    targets += [("seq", phase2_target(3, 2))]
    targets += [("seq", seq(1)), ("seq", seq(-1))]
    targets += [("head", (x + t) % heads) for t in range(1, heads)]
    for axis, target in targets:
        pl.semaphore_signal(barrier, inc=1, device_id={axis: target}, device_id_type=MESH)
    loads[2].start()
    loads[3].start()

    pools = jnp.concatenate(
        [pool(BLOCK, 256, 1, 128), pool(64, 256, 2, 64), pool(32, 256, 3, 32), pool(16, 256, 4, 16),
         pool(32, 256, 5, 8), pool(16, 256, 6, 4)], 0)
    loads[0].wait()
    loads[1].wait()
    k, v = k_ref[...], v_ref[...]
    ck, cv = dot(pools, k), dot(pools, v)
    blocks = [ck[:, :128], ck[:, 128:], cv[:, :128], cv[:, 128:]]
    for level, start, n in ((2, 128, 64), (3, 192, 32), (4, 224, 16)):
        for c in range(4):
            stages[level][c * n : (c + 1) * n, :] = blocks[c][start : start + n].astype(BF16)
    for level, start, n in ((5, 240, 8), (6, 272, 4)):
        owner = iota((4 * n, 128), 0) // n
        packed = blocks[0][start : start + 4 * n]
        for c in range(1, 4):
            packed = jnp.where(owner == c, blocks[c][start : start + 4 * n], packed)
        stages[level][...] = packed.astype(BF16)
    fine = [k[:, :128], k[:, 128:], v[:, :128], v[:, 128:]]
    for side in range(2):
        edge = BLOCK * (1 - side)
        for c in range(4):
            rim[side, c * BLOCK : (c + 1) * BLOCK, :] = fine[c][edge : edge + BLOCK]
            rim[side, 512 + c * HALF : 512 + (c + 1) * HALF, :] = blocks[c][side * HALF : (side + 1) * HALF].astype(BF16)

    pl.semaphore_wait(barrier, len(targets))
    for level, p in far1:
        phase1(level, p).start()
    neighbour(True).start()
    neighbour(False).start()
    for level, p in two1:
        phase1(level, p).start()
    for t in range(1, heads):
        weights(t).start()

    loads[2].wait()
    qt = (q_ref[...].astype(F32) * HEAD_DIM**-0.5).T
    feature = iota((BLOCK, BLOCK), 0)
    for b in range(2):
        for hp in range(2):
            part = qt[hp * BLOCK : (hp + 1) * BLOCK, b * BLOCK : (b + 1) * BLOCK]
            low = jnp.where(feature < HEAD_DIM, part, 0.0)
            high = jnp.where(feature < HEAD_DIM, 0.0, part)
            qbd[b, hp] = jnp.concatenate([low, high], 1).astype(BF16)

    def keep(u, state):
        st_m[u, 0:1, :], st_l[u, 0:1, :], st_o[u] = state

    def kept(u):
        return st_m[u, 0:1, :], st_l[u, 0:1, :], st_o[u]

    units = [(b, hp) for b in range(2) for hp in range(2)]
    for hp in range(2):
        lanes = slice(hp * BLOCK, (hp + 1) * BLOCK)
        vt = v_ref[:, lanes].T
        kk = k_ref[:, lanes]
        for b in range(2):
            keep(b * 2 + hp, attend(kk, vt, qbd[b, hp], [(0, 256, None)]))

    for level, p in far1:
        phase1(level, p).wait_recv()
        if (level, p) in ((6, 2), (5, 2), (4, 1), (3, 2)):
            pass_on(level)

    for level, p in two1:
        phase1(level, p).wait_recv()
    phase3(2).start()
    neighbour(True).wait_recv()
    neighbour(False).wait_recv()
    half_pool = pool(HALF, BLOCK, 1, HALF)
    lower_ok = jnp.where(d > 0, 0.0, OFF).astype(F32)
    upper_ok = jnp.where(d < devices - 1, 0.0, OFF).astype(F32)

    def far_bias(level):
        g, out = group(level), []
        e, last = d // g, devices // g - 1
        steps = (-2, 2, 3 - 6 * (e % 2))
        for step in steps:
            there = e + step
            out.append(jnp.where((there >= 0) & (there <= last), 0.0, OFF).astype(F32))
        return out

    bias2 = far_bias(2)
    phase3(2).wait_recv()
    for c in range(4):
        kind, hp = c // 2, c % 2
        strip = slice(c * BLOCK, (c + 1) * BLOCK)
        rows = slice(c * HALF, (c + 1) * HALF)
        half = slice(512 + c * HALF, 512 + (c + 1) * HALF)
        pooled = [dot(half_pool, near[side, strip, :]).astype(BF16) for side in range(2)]
        common = [near[0, half, :], near[1, half, :]] + [g2[p, rows, :] for p in range(3)]
        for b in range(2):
            full = jnp.concatenate([near[b, strip, :], pooled[1 - b]] + common, 0)
            if kind == 0:
                kb[b, hp] = full
            else:
                vbt[b, hp] = full.T
    for b, hp in units:
        first, second = (lower_ok, upper_ok) if b == 0 else (upper_ok, lower_ok)
        slabs = [(0, 128, first), (128, 64, second), (192, 64, lower_ok), (256, 64, upper_ok)]
        slabs += [(320 + 64 * p, 64, bias2[p]) for p in range(3)]
        u = b * 2 + hp
        keep(u, merge(kept(u), attend(kb[b, hp], vbt[b, hp], qbd[b, hp], slabs)))
        if u in (1, 3):
            for level in FAR[:3] if u == 1 else FAR[3:]:
                passed(level)
                phase3(level).start()

    for t in range(1, heads):
        weights(t).wait_recv()
    weights_swap().start()

    def far_chunk(i):
        slabs, keys, values = [], ([], []), ([], [])
        for level in FAR[2 * i : 2 * i + 2]:
            phase3(level).wait_recv()
            n = 256 // 2**level
            g = group(level)
            for p, bias in enumerate(far_bias(level)):
                slabs.append((64 * len(slabs), 64, bias))
                whole = gathers[level][:, :, p].reshape(g, 4 * n, 128)
                if n >= 16:
                    four = [whole[:, c * n : (c + 1) * n, :].reshape(64, 128) for c in range(4)]
                else:
                    moved = dot(unpack(n), whole.reshape(256, 128)).astype(BF16)
                    four = [moved[c * 64 : (c + 1) * 64] for c in range(4)]
                for hp in range(2):
                    keys[hp].append(four[hp])
                    values[hp].append(four[2 + hp])
        for hp in range(2):
            kc[i, hp] = jnp.concatenate(keys[hp], 0)
            vct[i, hp] = jnp.concatenate(values[hp], 0).T
        return slabs

    slabs = far_chunk(0)
    for b, hp in units:
        u = b * 2 + hp
        keep(u, merge(kept(u), attend(kc[0, hp], vct[0, hp], qbd[b, hp], slabs)))
    slabs = far_chunk(1)
    for b, hp in units:
        u = b * 2 + hp
        _, total, o = merge(kept(u), attend(kc[1, hp], vct[1, hp], qbd[b, hp], slabs))
        o = (o / total).astype(BF16)
        att[b, hp * BLOCK : (hp + 1) * BLOCK, :] = jnp.concatenate([o[:, :BLOCK], o[:, BLOCK:]], 0)
        if hp == 1:
            for t in (2, 1, 3):
                share(b, t).start()

    for level, p in all1:
        phase1(level, p).wait_send()
    for level, j in all2:
        phase2(level, j).wait_send()
    for level in (2,) + FAR:
        phase3(level).wait_send()
    neighbour(True).wait_send()
    neighbour(False).wait_send()
    for t in range(1, heads):
        weights(t).wait_send()
    weights_swap().wait()
    loads[3].wait()
    wt[0] = w_own[...].T
    for t in range(1, heads):
        wt[t] = wg[t - 1].reshape(2 * BLOCK, width).T

    total = dot(wt[0], jnp.concatenate([att[0], att[1]], 1))
    for t in (1, 3, 2):
        for b in range(2):
            share(b, t).wait_recv()
        total = total + dot(wt[t], jnp.concatenate([got[t - 1, 0], got[t - 1, 1]], 1))
    out_ref[...] = total.astype(BF16)

    for b in range(2):
        for t in range(1, heads):
            share(b, t).wait_send()


def solution(mesh):
    devices, heads = mesh.shape["seq"], mesh.shape["head"]

    def shards(q, k, v, w):
        rows, width = q.shape
        lanes = w.shape[1] // heads
        vmem = pl.BlockSpec(memory_space=pltpu.VMEM)
        dma = pltpu.SemaphoreType.DMA

        def gather(level):
            return pltpu.VMEM((2 ** (level - 3), 2, 3, 4 * (rows >> level), 128), BF16)

        def stage(level):
            return pltpu.VMEM((4 * (rows >> level), 128), BF16)

        return pl.pallas_call(
            functools.partial(kernel, devices, heads),
            out_shape=jax.ShapeDtypeStruct((lanes, rows), BF16),
            in_specs=[pl.BlockSpec(memory_space=pltpu.HBM)] * 4,
            out_specs=vmem,
            scratch_shapes=[
                pltpu.VMEM((rows, width), BF16),
                pltpu.VMEM((rows, width), BF16),
                pltpu.VMEM((rows, width), BF16),
                pltpu.VMEM((width, lanes), BF16),
                pltpu.VMEM((2, 4 * (BLOCK + HALF), 128), BF16),
                pltpu.VMEM((2, 4 * (BLOCK + HALF), 128), BF16),
                pltpu.VMEM((3, 4 * HALF, 128), BF16),
                gather(3), gather(4), gather(5), gather(6),
                stage(2), stage(3), stage(4), stage(5), stage(6),
                pltpu.VMEM((2, 2, 128, 256), BF16),
                pltpu.VMEM((2, 2, 512, 128), BF16),
                pltpu.VMEM((2, 2, 128, 512), BF16),
                pltpu.VMEM((2, 2, 384, 128), BF16),
                pltpu.VMEM((2, 2, 128, 384), BF16),
                pltpu.VMEM((heads - 1, 2, BLOCK, lanes), BF16),
                pltpu.VMEM((heads, lanes, width), BF16),
                pltpu.VMEM((2, width, BLOCK), BF16),
                pltpu.VMEM((heads - 1, 2, width, BLOCK), BF16),
                pltpu.VMEM((4, 8, 256), F32),
                pltpu.VMEM((4, 8, 256), F32),
                pltpu.VMEM((4, HEAD_DIM, 256), F32),
                dma((4,)),
                dma((5, 3)), dma((5, 3)), dma((13,)), dma((13,)), dma((5,)), dma((5,)),
                dma((2,)), dma((2,)), dma((heads,)), dma((heads,)),
                dma((2, heads - 1)), dma((2, heads - 1)),
            ],
            compiler_params=pltpu.CompilerParams(
                collective_id=0, has_side_effects=True, vmem_limit_bytes=55040 * 1024
            ),
            cost_estimate=pl.CostEstimate(
                flops=2_000_000_000, bytes_accessed=1_200_000, transcendentals=1_600_000
            ),
        )(q, k, v, w)

    placed = (P("seq", "head"), P("seq", "head"), P("seq", "head"), P("head", None))
    return jax.shard_map(
        shards, mesh=mesh, in_specs=placed, out_specs=P("head", "seq"), check_vma=False
    )
```

```python
import functools

import jax
import jax.numpy as jnp
from jax import lax
from jax.experimental import pallas as pl
from jax.experimental.pallas import tpu as pltpu
from jax.sharding import PartitionSpec as P

HEAD_DIM = 64
BLOCK = 128
LEVELS = 6
HALF = BLOCK // 2
F32 = jnp.float32
BF16 = jnp.bfloat16
MESH = pl.DeviceIdType.MESH
FAR = (3, 4, 5, 6)
OFF = -1e30


def dot(a, b):
    return jnp.dot(a, b, preferred_element_type=F32)


def iota(shape, dim):
    return lax.broadcasted_iota(jnp.int32, shape, dim)


def pool(rows, fine, level, repeat):
    r, c = iota((rows, fine), 0), iota((rows, fine), 1)
    hit = (c >> level) == (r & (repeat - 1))
    return jnp.where(hit, 2.0**-level, 0.0).astype(BF16)


def unpack(n):
    r, c = iota((256, 256), 0), iota((256, 256), 1)
    group, inside = r >> 6, r & 63
    source, row = inside // n, inside & (n - 1)
    return jnp.where(c == source * (4 * n) + group * n + row, 1.0, 0.0).astype(BF16)


def scores_top(s, slabs):
    top = None
    for start, rows, bias in slabs:
        m = jnp.max(s[start : start + rows], axis=0, keepdims=True)
        if bias is not None:
            m = m + bias
        top = m if top is None else jnp.maximum(top, m)
    return top


def attend(k, vt, q, slabs):
    s = dot(k, q)
    top = scores_top(s, slabs)
    parts, total = [], None
    for start, rows, bias in slabs:
        shift = top if bias is None else top - bias
        p = jnp.exp(s[start : start + rows] - shift)
        t = jnp.sum(p, axis=0, keepdims=True)
        total = t if total is None else total + t
        parts.append(p.astype(BF16))
    o = dot(vt, jnp.concatenate(parts, 0))
    o = jnp.concatenate([o[:HEAD_DIM, :BLOCK], o[HEAD_DIM:, BLOCK:]], 1)
    return top, total, o


def merge(a, b):
    top = jnp.maximum(a[0], b[0])
    fa, fb = jnp.exp(a[0] - top), jnp.exp(b[0] - top)
    return top, a[1] * fa + b[1] * fb, a[2] * fa + b[2] * fb


def kernel(
    devices, heads,
    q_hbm, k_hbm, v_hbm, w_hbm, out_ref,
    q_ref, k_ref, v_ref, w_ref, rim, near, g2, g3, g4, g5, g6, s2, s3, s4, s5, s6,
    qbd, kb, vbt, kc, vct, wt, own_part, part, got, st_m, st_l, st_o, in_s,
    p1_s, p1_r, p2_s, p2_r, p3_s, p3_r, near_s, near_r, part_s, part_r,
):
    d = lax.axis_index("seq")
    x = lax.axis_index("head")
    core = d % 2
    gathers = {3: g3, 4: g4, 5: g5, 6: g6}
    stages = {2: s2, 3: s3, 4: s4, 5: s5, 6: s6}

    def seq(steps):
        return (d + steps + 2 * devices) % devices

    def group(level):
        return 2 ** (level - 2)

    def far_steps(level, p):
        g = group(level)
        if p == 0:
            return 2 * g
        if p == 1:
            return -2 * g
        return (3 - 6 * ((d // g) % 2)) * g

    def remote(src, dst, send, recv, axis, target):
        return pltpu.make_async_remote_copy(
            src_ref=src, dst_ref=dst, send_sem=send, recv_sem=recv,
            device_id={axis: target}, device_id_type=MESH,
        )

    def far_target(level, p):
        target = seq(far_steps(level, p))
        if level == 4 and p == 2:
            target = target + 2 - 4 * ((target // 2) % 2)
        return target

    def phase1(level, p):
        at = (level - 2, p)
        rank = (d % group(level)) // 2
        if level == 2:
            dst = g2.at[p]
        elif level == 4 and p == 2:
            dst = g4.at[1 - rank, core, p]
        else:
            dst = gathers[level].at[rank, core, p]
        return remote(stages[level], dst, p1_s.at[at], p1_r.at[at], "seq", far_target(level, p))

    odd = (d // 2) % 2

    def phase2_target(level, j):
        if level == 3:
            return seq((1, 5)[j - 1] * 2 * (1 - 2 * odd))
        chips = group(level) // 2
        mine = (d // 2) % chips
        return d - 2 * mine + 2 * ((mine + j) % chips)

    def phase2(level, j):
        slot = {3: 0, 4: 2, 5: 3, 6: 6}[level] + j - 1
        if level == 3:
            src = g3.at[0, core, 2]
            dst = g3.at[0, core, 1 - odd if j == 1 else odd]
        else:
            src = dst = gathers[level].at[(d // 2) % (group(level) // 2), core]
        return remote(src, dst, p2_s.at[slot], p2_r.at[slot], "seq", phase2_target(level, j))

    def phase3(level):
        if level == 2:
            src, dst = g2.at[core], g2.at[2]
        else:
            src = dst = gathers[level].at[:, core]
        slot = level - 2
        return remote(src, dst, p3_s.at[slot], p3_r.at[slot], "seq", d + 1 - 2 * core)

    def neighbour(up):
        side = 0 if up else 1
        return remote(
            rim.at[side], near.at[side], near_s.at[side], near_r.at[side], "seq", seq(1 if up else -1)
        )

    def share(b, t):
        at = (b, t - 1)
        return remote(part.at[b, t - 1], got.at[t - 1, b], part_s.at[at], part_r.at[at], "head", (x + t) % heads)

    far1 = [(6, 0), (6, 1), (6, 2), (5, 0), (5, 1), (5, 2), (4, 2), (4, 0), (4, 1), (3, 2)]
    two1 = [(2, 0), (2, 1)]
    all1 = far1 + two1
    all2 = [(3, 1), (3, 2)] + [(level, j) for level in (4, 5, 6) for j in range(1, group(level) // 2)]

    def pass_on(level):
        for other, j in all2:
            if other == level:
                phase2(level, j).start()

    def passed(level):
        for other, j in all2:
            if other == level:
                phase2(level, j).wait_recv()

    loads = [
        pltpu.make_async_copy(src, dst, in_s.at[i])
        for i, (src, dst) in enumerate(
            [(k_hbm, k_ref), (v_hbm, v_ref), (q_hbm, q_ref), (w_hbm, w_ref)]
        )
    ]
    loads[0].start()
    loads[1].start()
    barrier = pltpu.get_barrier_semaphore()
    targets = [("seq", far_target(level, p)) for level, p in all1]
    targets += [("seq", phase2_target(6, j)) for j in range(1, 8)]
    targets += [("seq", phase2_target(3, 2))]
    targets += [("seq", seq(1)), ("seq", seq(-1))]
    targets += [("head", (x + t) % heads) for t in range(1, heads)]
    for axis, target in targets:
        pl.semaphore_signal(barrier, inc=1, device_id={axis: target}, device_id_type=MESH)
    loads[2].start()
    loads[3].start()

    pools = jnp.concatenate(
        [pool(BLOCK, 256, 1, 128), pool(64, 256, 2, 64), pool(32, 256, 3, 32), pool(16, 256, 4, 16),
         pool(32, 256, 5, 8), pool(16, 256, 6, 4)], 0)
    loads[0].wait()
    loads[1].wait()
    k, v = k_ref[...], v_ref[...]
    ck, cv = dot(pools, k), dot(pools, v)
    blocks = [ck[:, :128], ck[:, 128:], cv[:, :128], cv[:, 128:]]
    for level, start, n in ((2, 128, 64), (3, 192, 32), (4, 224, 16)):
        for c in range(4):
            stages[level][c * n : (c + 1) * n, :] = blocks[c][start : start + n].astype(BF16)
    for level, start, n in ((5, 240, 8), (6, 272, 4)):
        owner = iota((4 * n, 128), 0) // n
        packed = blocks[0][start : start + 4 * n]
        for c in range(1, 4):
            packed = jnp.where(owner == c, blocks[c][start : start + 4 * n], packed)
        stages[level][...] = packed.astype(BF16)
    fine = [k[:, :128], k[:, 128:], v[:, :128], v[:, 128:]]
    for side in range(2):
        edge = BLOCK * (1 - side)
        for c in range(4):
            rim[side, c * BLOCK : (c + 1) * BLOCK, :] = fine[c][edge : edge + BLOCK]
            rim[side, 512 + c * HALF : 512 + (c + 1) * HALF, :] = blocks[c][side * HALF : (side + 1) * HALF].astype(BF16)

    pl.semaphore_wait(barrier, len(targets))
    for level, p in far1:
        phase1(level, p).start()
    neighbour(True).start()
    neighbour(False).start()
    for level, p in two1:
        phase1(level, p).start()
    loads[2].wait()
    qt = (q_ref[...].astype(F32) * HEAD_DIM**-0.5).T
    feature = iota((BLOCK, BLOCK), 0)
    for b in range(2):
        for hp in range(2):
            piece = qt[hp * BLOCK : (hp + 1) * BLOCK, b * BLOCK : (b + 1) * BLOCK]
            low = jnp.where(feature < HEAD_DIM, piece, 0.0)
            high = jnp.where(feature < HEAD_DIM, 0.0, piece)
            qbd[b, hp] = jnp.concatenate([low, high], 1).astype(BF16)

    def keep(u, state):
        st_m[u, 0:1, :], st_l[u, 0:1, :], st_o[u] = state

    def kept(u):
        return st_m[u, 0:1, :], st_l[u, 0:1, :], st_o[u]

    units = [(b, hp) for b in range(2) for hp in range(2)]
    for hp in range(2):
        lanes = slice(hp * BLOCK, (hp + 1) * BLOCK)
        vt = v_ref[:, lanes].T
        kk = k_ref[:, lanes]
        for b in range(2):
            keep(b * 2 + hp, attend(kk, vt, qbd[b, hp], [(0, 256, None)]))

    loads[3].wait()
    for i in range(heads):
        wt[i] = w_ref[:, i * 256 : (i + 1) * 256].T

    for level, p in far1:
        phase1(level, p).wait_recv()
        if (level, p) in ((6, 2), (5, 2), (4, 1), (3, 2)):
            pass_on(level)

    for level, p in two1:
        phase1(level, p).wait_recv()
    phase3(2).start()
    neighbour(True).wait_recv()
    neighbour(False).wait_recv()
    half_pool = pool(HALF, BLOCK, 1, HALF)
    lower_ok = jnp.where(d > 0, 0.0, OFF).astype(F32)
    upper_ok = jnp.where(d < devices - 1, 0.0, OFF).astype(F32)

    def far_bias(level):
        g, out = group(level), []
        e, last = d // g, devices // g - 1
        steps = (-2, 2, 3 - 6 * (e % 2))
        for step in steps:
            there = e + step
            out.append(jnp.where((there >= 0) & (there <= last), 0.0, OFF).astype(F32))
        return out

    bias2 = far_bias(2)
    phase3(2).wait_recv()
    for c in range(4):
        kind, hp = c // 2, c % 2
        strip = slice(c * BLOCK, (c + 1) * BLOCK)
        rows = slice(c * HALF, (c + 1) * HALF)
        half = slice(512 + c * HALF, 512 + (c + 1) * HALF)
        pooled = [dot(half_pool, near[side, strip, :]).astype(BF16) for side in range(2)]
        common = [near[0, half, :], near[1, half, :]] + [g2[p, rows, :] for p in range(3)]
        for b in range(2):
            full = jnp.concatenate([near[b, strip, :], pooled[1 - b]] + common, 0)
            if kind == 0:
                kb[b, hp] = full
            else:
                vbt[b, hp] = full.T
    for b, hp in units:
        first, second = (lower_ok, upper_ok) if b == 0 else (upper_ok, lower_ok)
        slabs = [(0, 128, first), (128, 64, second), (192, 64, lower_ok), (256, 64, upper_ok)]
        slabs += [(320 + 64 * p, 64, bias2[p]) for p in range(3)]
        u = b * 2 + hp
        keep(u, merge(kept(u), attend(kb[b, hp], vbt[b, hp], qbd[b, hp], slabs)))
        if u in (1, 3):
            for level in FAR[:3] if u == 1 else FAR[3:]:
                passed(level)
                phase3(level).start()

    def far_chunk(i):
        slabs, keys, values = [], ([], []), ([], [])
        for level in FAR[2 * i : 2 * i + 2]:
            phase3(level).wait_recv()
            n = 256 // 2**level
            g = group(level)
            for p, bias in enumerate(far_bias(level)):
                slabs.append((64 * len(slabs), 64, bias))
                whole = gathers[level][:, :, p].reshape(g, 4 * n, 128)
                if n >= 16:
                    four = [whole[:, c * n : (c + 1) * n, :].reshape(64, 128) for c in range(4)]
                else:
                    moved = dot(unpack(n), whole.reshape(256, 128)).astype(BF16)
                    four = [moved[c * 64 : (c + 1) * 64] for c in range(4)]
                for hp in range(2):
                    keys[hp].append(four[hp])
                    values[hp].append(four[2 + hp])
        for hp in range(2):
            kc[i, hp] = jnp.concatenate(keys[hp], 0)
            vct[i, hp] = jnp.concatenate(values[hp], 0).T
        return slabs

    slabs = far_chunk(0)
    for b, hp in units:
        u = b * 2 + hp
        keep(u, merge(kept(u), attend(kc[0, hp], vct[0, hp], qbd[b, hp], slabs)))
    slabs = far_chunk(1)
    for b, hp in units:
        u = b * 2 + hp
        _, total, o = merge(kept(u), attend(kc[1, hp], vct[1, hp], qbd[b, hp], slabs))
        o = (o / total).astype(BF16)
        rows = jnp.concatenate([o[:, :BLOCK], o[:, BLOCK:]], 0)
        if hp == 0:
            upper = rows
            continue
        attended = jnp.concatenate([upper, rows], 0)
        for t in (2, 1, 3):
            part[b, t - 1] = dot(wt[(x + t) % heads], attended).astype(BF16)
            share(b, t).start()
        own_part[b] = dot(wt[x], attended)

    for level, p in all1:
        phase1(level, p).wait_send()
    for level, j in all2:
        phase2(level, j).wait_send()
    for level in (2,) + FAR:
        phase3(level).wait_send()
    neighbour(True).wait_send()
    neighbour(False).wait_send()

    for b in range(2):
        total = own_part[b]
        for t in (1, 3, 2):
            share(b, t).wait_recv()
            total = total + got[t - 1, b].astype(F32)
        out_ref[:, b * BLOCK : (b + 1) * BLOCK] = total.astype(BF16)

    for b in range(2):
        for t in range(1, heads):
            share(b, t).wait_send()


def solution(mesh):
    devices, heads = mesh.shape["seq"], mesh.shape["head"]

    def shards(q, k, v, w):
        rows, width = q.shape
        lanes = w.shape[1] // heads
        vmem = pl.BlockSpec(memory_space=pltpu.VMEM)
        dma = pltpu.SemaphoreType.DMA

        def gather(level):
            return pltpu.VMEM((2 ** (level - 3), 2, 3, 4 * (rows >> level), 128), BF16)

        def stage(level):
            return pltpu.VMEM((4 * (rows >> level), 128), BF16)

        return pl.pallas_call(
            functools.partial(kernel, devices, heads),
            out_shape=jax.ShapeDtypeStruct((lanes, rows), BF16),
            in_specs=[pl.BlockSpec(memory_space=pltpu.HBM)] * 4,
            out_specs=vmem,
            scratch_shapes=[
                pltpu.VMEM((rows, width), BF16),
                pltpu.VMEM((rows, width), BF16),
                pltpu.VMEM((rows, width), BF16),
                pltpu.VMEM((width, heads * lanes), BF16),
                pltpu.VMEM((2, 4 * (BLOCK + HALF), 128), BF16),
                pltpu.VMEM((2, 4 * (BLOCK + HALF), 128), BF16),
                pltpu.VMEM((3, 4 * HALF, 128), BF16),
                gather(3), gather(4), gather(5), gather(6),
                stage(2), stage(3), stage(4), stage(5), stage(6),
                pltpu.VMEM((2, 2, 128, 256), BF16),
                pltpu.VMEM((2, 2, 512, 128), BF16),
                pltpu.VMEM((2, 2, 128, 512), BF16),
                pltpu.VMEM((2, 2, 384, 128), BF16),
                pltpu.VMEM((2, 2, 128, 384), BF16),
                pltpu.VMEM((heads, lanes, width), BF16),
                pltpu.VMEM((2, lanes, BLOCK), F32),
                pltpu.VMEM((2, heads - 1, lanes, BLOCK), BF16),
                pltpu.VMEM((heads - 1, 2, lanes, BLOCK), BF16),
                pltpu.VMEM((4, 8, 256), F32),
                pltpu.VMEM((4, 8, 256), F32),
                pltpu.VMEM((4, HEAD_DIM, 256), F32),
                dma((4,)),
                dma((5, 3)), dma((5, 3)), dma((13,)), dma((13,)), dma((5,)), dma((5,)),
                dma((2,)), dma((2,)),
                dma((2, heads - 1)), dma((2, heads - 1)),
            ],
            compiler_params=pltpu.CompilerParams(
                collective_id=0, has_side_effects=True, vmem_limit_bytes=55040 * 1024
            ),
            cost_estimate=pl.CostEstimate(
                flops=2_000_000_000, bytes_accessed=1_200_000, transcendentals=1_600_000
            ),
        )(q, k, v, w)

    placed = (P("seq", "head"), P("seq", "head"), P("seq", "head"), P("head", None))
    return jax.shard_map(
        shards, mesh=mesh, in_specs=placed, out_specs=P("head", "seq"), check_vma=False
    )
```

```python
import functools

import jax
import jax.numpy as jnp
from jax import lax
from jax.experimental import pallas as pl
from jax.experimental.pallas import tpu as pltpu
from jax.sharding import PartitionSpec as P

HEAD_DIM = 64
BLOCK = 128
LEVELS = 6
HALF = BLOCK // 2
F32 = jnp.float32
BF16 = jnp.bfloat16
MESH = pl.DeviceIdType.MESH
FAR = (3, 4, 5, 6)
OFF = -1e30


def dot(a, b):
    return jnp.dot(a, b, preferred_element_type=F32)


def iota(shape, dim):
    return lax.broadcasted_iota(jnp.int32, shape, dim)


def pool(rows, fine, level, repeat):
    r, c = iota((rows, fine), 0), iota((rows, fine), 1)
    hit = (c >> level) == (r & (repeat - 1))
    return jnp.where(hit, 2.0**-level, 0.0).astype(BF16)


def unpack(n):
    r, c = iota((256, 256), 0), iota((256, 256), 1)
    group, inside = r >> 6, r & 63
    source, row = inside // n, inside & (n - 1)
    return jnp.where(c == source * (4 * n) + group * n + row, 1.0, 0.0).astype(BF16)


def scores_top(s, slabs):
    top = None
    for start, rows, bias in slabs:
        m = jnp.max(s[start : start + rows], axis=0, keepdims=True)
        if bias is not None:
            m = m + bias
        top = m if top is None else jnp.maximum(top, m)
    return top


def attend(k, vt, q, slabs):
    s = dot(k, q)
    top = scores_top(s, slabs)
    parts, total = [], None
    for start, rows, bias in slabs:
        shift = top if bias is None else top - bias
        p = jnp.exp(s[start : start + rows] - shift)
        t = jnp.sum(p, axis=0, keepdims=True)
        total = t if total is None else total + t
        parts.append(p.astype(BF16))
    o = dot(vt, jnp.concatenate(parts, 0))
    o = jnp.concatenate([o[:HEAD_DIM, :BLOCK], o[HEAD_DIM:, BLOCK:]], 1)
    return top, total, o


def merge(a, b):
    top = jnp.maximum(a[0], b[0])
    fa, fb = jnp.exp(a[0] - top), jnp.exp(b[0] - top)
    return top, a[1] * fa + b[1] * fb, a[2] * fa + b[2] * fb


def kernel(
    devices, heads,
    q_hbm, k_hbm, v_hbm, w_hbm, out_ref,
    q_ref, k_ref, v_ref, w_ref, rim, near, g2, g3, g4, g5, g6, s2, s3, s4, s5, s6,
    qbd, kb, vbt, kc, vct, wt, own_part, part, got, st_m, st_l, st_o, grants, in_s,
    p1_s, p1_r, p2_s, p2_r, p3_s, p3_r, near_s, near_r, part_s, part_r,
):
    d = lax.axis_index("seq")
    x = lax.axis_index("head")
    core = d % 2
    gathers = {3: g3, 4: g4, 5: g5, 6: g6}
    stages = {2: s2, 3: s3, 4: s4, 5: s5, 6: s6}

    def seq(steps):
        return (d + steps + 2 * devices) % devices

    def group(level):
        return 2 ** (level - 2)

    def far_steps(level, p):
        g = group(level)
        if p == 0:
            return 2 * g
        if p == 1:
            return -2 * g
        return (3 - 6 * ((d // g) % 2)) * g

    def remote(src, dst, send, recv, axis, target):
        return pltpu.make_async_remote_copy(
            src_ref=src, dst_ref=dst, send_sem=send, recv_sem=recv,
            device_id={axis: target}, device_id_type=MESH,
        )

    def far_target(level, p):
        target = seq(far_steps(level, p))
        if level == 4 and p == 2:
            target = target + 2 - 4 * ((target // 2) % 2)
        return target

    def phase1(level, p):
        at = (level - 2, p)
        rank = (d % group(level)) // 2
        if level == 2:
            dst = g2.at[p]
        elif level == 4 and p == 2:
            dst = g4.at[1 - rank, core, p]
        else:
            dst = gathers[level].at[rank, core, p]
        return remote(stages[level], dst, p1_s.at[at], p1_r.at[at], "seq", far_target(level, p))

    def phase2_target(level, j):
        chips = group(level) // 2
        mine = (d // 2) % chips
        return d - 2 * mine + 2 * ((mine + j) % chips)

    def phase2(level, j):
        slot = {4: 0, 5: 1, 6: 4}[level] + j - 1
        block = gathers[level].at[(d // 2) % (group(level) // 2), core]
        return remote(block, block, p2_s.at[slot], p2_r.at[slot], "seq", phase2_target(level, j))

    def phase3(level):
        if level == 2:
            src, dst = g2.at[core], g2.at[2]
        else:
            src = dst = gathers[level].at[:, core]
        slot = level - 2
        return remote(src, dst, p3_s.at[slot], p3_r.at[slot], "seq", d + 1 - 2 * core)

    def neighbour(up):
        side = 0 if up else 1
        return remote(
            rim.at[side], near.at[side], near_s.at[side], near_r.at[side], "seq", seq(1 if up else -1)
        )

    def share(b, t):
        at = (b, t - 1)
        return remote(part.at[b, t - 1], got.at[t - 1, b], part_s.at[at], part_r.at[at], "head", (x + t) % heads)

    all1 = [(level, p) for level in (6, 5, 4, 3, 2) for p in range(3 if level > 2 else 2)]
    all2 = [(level, j) for level in (4, 5, 6) for j in range(1, group(level) // 2)]

    def pass_on(level):
        for other, j in all2:
            if other == level:
                phase2(level, j).start()

    def passed(level):
        for other, j in all2:
            if other == level:
                phase2(level, j).wait_recv()

    back = (1, 0, 2)
    relations = {}
    for level, p in all1:
        there = d // group(level) + far_steps(level, p) // group(level)
        inside = (there >= 0) & (there < devices // group(level))
        relations["far", level, p] = ("seq", far_target(level, p), ("far", level, back[p]), inside)
    for up in (True, False):
        inside = d < devices - 1 if up else d > 0
        relations["near", up] = ("seq", seq(1 if up else -1), ("near", not up), inside)
    for j in range(1, 8):
        relations["mate", j] = ("seq", phase2_target(6, j), ("mate", 8 - j), True)
    for t in range(1, heads):
        relations["head", t] = ("head", (x + t) % heads, ("head", heads - t), True)
    slots = {name: i for i, name in enumerate(relations)}
    inside = {name: relation[3] for name, relation in relations.items()}
    above, below = {}, {}
    for name, (axis, target, _, valid) in relations.items():
        here = d if axis == "seq" else x
        above[name] = (target > here) & valid
        below[name] = (target < here) & valid

    def on(condition, *steps):
        @pl.when(condition)
        def _():
            for step in steps:
                step()

    def signal(semaphore, name):
        axis, target = relations[name][:2]
        pl.semaphore_signal(semaphore, inc=1, device_id={axis: target}, device_id_type=MESH)

    def granted(name, *steps):
        on(above[name], lambda: pl.semaphore_wait(grants.at[slots[name]], 1), *steps)

    def send_above(level, p):
        granted(("far", level, p), lambda: phase1(level, p).start())

    def arrived(level, p):
        on(inside["far", level, back[p]], lambda: phase1(level, p).wait_recv())

    loads = [
        pltpu.make_async_copy(src, dst, in_s.at[i])
        for i, (src, dst) in enumerate(
            [(k_hbm, k_ref), (v_hbm, v_ref), (q_hbm, q_ref), (w_hbm, w_ref)]
        )
    ]
    loads[0].start()
    loads[1].start()
    barrier = pltpu.get_barrier_semaphore()
    for name in relations:
        on(above[name], lambda: signal(barrier, name))
    loads[2].start()
    loads[3].start()

    pools = jnp.concatenate(
        [pool(BLOCK, 256, 1, 128), pool(64, 256, 2, 64), pool(32, 256, 3, 32), pool(16, 256, 4, 16),
         pool(32, 256, 5, 8), pool(16, 256, 6, 4)], 0)
    loads[0].wait()
    loads[1].wait()
    k, v = k_ref[...], v_ref[...]
    ck, cv = dot(pools, k), dot(pools, v)
    blocks = [ck[:, :128], ck[:, 128:], cv[:, :128], cv[:, 128:]]
    for level, start, n in ((2, 128, 64), (3, 192, 32), (4, 224, 16)):
        for c in range(4):
            stages[level][c * n : (c + 1) * n, :] = blocks[c][start : start + n].astype(BF16)
    for level, start, n in ((5, 240, 8), (6, 272, 4)):
        owner = iota((4 * n, 128), 0) // n
        packed = blocks[0][start : start + 4 * n]
        for c in range(1, 4):
            packed = jnp.where(owner == c, blocks[c][start : start + 4 * n], packed)
        stages[level][...] = packed.astype(BF16)
    fine = [k[:, :128], k[:, 128:], v[:, :128], v[:, 128:]]
    for side in range(2):
        edge = BLOCK * (1 - side)
        for c in range(4):
            rim[side, c * BLOCK : (c + 1) * BLOCK, :] = fine[c][edge : edge + BLOCK]
            rim[side, 512 + c * HALF : 512 + (c + 1) * HALF, :] = blocks[c][side * HALF : (side + 1) * HALF].astype(BF16)

    count = sum(jnp.where(below[name], 1, 0) for name in relations)
    on(count > 0, lambda: pl.semaphore_wait(barrier, count))
    for name in relations:
        on(below[name], lambda: signal(grants.at[slots[relations[name][2]]], name))
    for level, p in all1:
        on(below["far", level, p], lambda: phase1(level, p).start())
    on(below["near", False], lambda: neighbour(False).start())

    def clear(ref):
        ref[...] = jnp.zeros(ref.shape, ref.dtype)

    for level, p in all1:
        slot = g2.at[p] if level == 2 else gathers[level].at[(d % group(level)) // 2, core, p]
        on(jnp.logical_not(inside["far", level, back[p]]), lambda: clear(slot))
    on(d == 0, lambda: clear(near.at[0]))
    on(d == devices - 1, lambda: clear(near.at[1]))
    granted(("near", True), lambda: neighbour(True).start())

    loads[2].wait()
    qt = (q_ref[...].astype(F32) * HEAD_DIM**-0.5).T
    feature = iota((BLOCK, BLOCK), 0)
    for b in range(2):
        for hp in range(2):
            piece = qt[hp * BLOCK : (hp + 1) * BLOCK, b * BLOCK : (b + 1) * BLOCK]
            low = jnp.where(feature < HEAD_DIM, piece, 0.0)
            high = jnp.where(feature < HEAD_DIM, 0.0, piece)
            qbd[b, hp] = jnp.concatenate([low, high], 1).astype(BF16)

    def keep(u, state):
        st_m[u, 0:1, :], st_l[u, 0:1, :], st_o[u] = state

    def kept(u):
        return st_m[u, 0:1, :], st_l[u, 0:1, :], st_o[u]

    units = [(b, hp) for b in range(2) for hp in range(2)]
    for hp in range(2):
        lanes = slice(hp * BLOCK, (hp + 1) * BLOCK)
        vt = v_ref[:, lanes].T
        kk = k_ref[:, lanes]
        for b in range(2):
            keep(b * 2 + hp, attend(kk, vt, qbd[b, hp], [(0, 256, None)]))

    loads[3].wait()
    for i in range(heads):
        wt[i] = w_ref[:, i * 256 : (i + 1) * 256].T

    def exchange(level):
        for p in range(3 if level > 2 else 2):
            send_above(level, p)

    def gathered(level):
        for p in range(3 if level > 2 else 2):
            arrived(level, p)

    for level in (2, 3, 4):
        exchange(level)
    for j in range(1, 8):
        granted(("mate", j))

    gathered(2)
    phase3(2).start()
    gathered(3)
    phase3(3).start()
    gathered(4)
    pass_on(4)
    on(inside["near", False], lambda: neighbour(True).wait_recv())
    on(inside["near", True], lambda: neighbour(False).wait_recv())
    half_pool = pool(HALF, BLOCK, 1, HALF)
    lower_ok = jnp.where(d > 0, 0.0, OFF).astype(F32)
    upper_ok = jnp.where(d < devices - 1, 0.0, OFF).astype(F32)

    def far_bias(level):
        g, out = group(level), []
        e, last = d // g, devices // g - 1
        steps = (-2, 2, 3 - 6 * (e % 2))
        for step in steps:
            there = e + step
            out.append(jnp.where((there >= 0) & (there <= last), 0.0, OFF).astype(F32))
        return out

    bias2 = far_bias(2)
    phase3(2).wait_recv()
    for c in range(4):
        kind, hp = c // 2, c % 2
        strip = slice(c * BLOCK, (c + 1) * BLOCK)
        rows = slice(c * HALF, (c + 1) * HALF)
        half = slice(512 + c * HALF, 512 + (c + 1) * HALF)
        pooled = [dot(half_pool, near[side, strip, :]).astype(BF16) for side in range(2)]
        common = [near[0, half, :], near[1, half, :]] + [g2[p, rows, :] for p in range(3)]
        for b in range(2):
            full = jnp.concatenate([near[b, strip, :], pooled[1 - b]] + common, 0)
            if kind == 0:
                kb[b, hp] = full
            else:
                vbt[b, hp] = full.T
    for b, hp in units:
        first, second = (lower_ok, upper_ok) if b == 0 else (upper_ok, lower_ok)
        slabs = [(0, 128, first), (128, 64, second), (192, 64, lower_ok), (256, 64, upper_ok)]
        slabs += [(320 + 64 * p, 64, bias2[p]) for p in range(3)]
        u = b * 2 + hp
        keep(u, merge(kept(u), attend(kb[b, hp], vbt[b, hp], qbd[b, hp], slabs)))
        if u == 1:
            passed(4)
            phase3(4).start()
    exchange(5)
    gathered(5)
    pass_on(5)

    def far_chunk(i):
        slabs, keys, values = [], ([], []), ([], [])
        for level in FAR[2 * i : 2 * i + 2]:
            phase3(level).wait_recv()
            n = 256 // 2**level
            g = group(level)
            for p, bias in enumerate(far_bias(level)):
                slabs.append((64 * len(slabs), 64, bias))
                whole = gathers[level][:, :, p].reshape(g, 4 * n, 128)
                if n >= 16:
                    four = [whole[:, c * n : (c + 1) * n, :].reshape(64, 128) for c in range(4)]
                else:
                    moved = dot(unpack(n), whole.reshape(256, 128)).astype(BF16)
                    four = [moved[c * 64 : (c + 1) * 64] for c in range(4)]
                for hp in range(2):
                    keys[hp].append(four[hp])
                    values[hp].append(four[2 + hp])
        for hp in range(2):
            kc[i, hp] = jnp.concatenate(keys[hp], 0)
            vct[i, hp] = jnp.concatenate(values[hp], 0).T
        return slabs

    slabs = far_chunk(0)
    for b, hp in units:
        u = b * 2 + hp
        keep(u, merge(kept(u), attend(kc[0, hp], vct[0, hp], qbd[b, hp], slabs)))
    exchange(6)
    passed(5)
    phase3(5).start()
    gathered(6)
    pass_on(6)
    for t in range(1, heads):
        granted(("head", t))
    passed(6)
    phase3(6).start()
    slabs = far_chunk(1)
    for b, hp in units:
        u = b * 2 + hp
        _, total, o = merge(kept(u), attend(kc[1, hp], vct[1, hp], qbd[b, hp], slabs))
        o = (o / total).astype(BF16)
        rows = jnp.concatenate([o[:, :BLOCK], o[:, BLOCK:]], 0)
        if hp == 0:
            upper = rows
            continue
        attended = jnp.concatenate([upper, rows], 0)
        for t in (2, 1, 3):
            part[b, t - 1] = dot(wt[(x + t) % heads], attended).astype(BF16)
            share(b, t).start()
        own_part[b] = dot(wt[x], attended)

    for level, p in all1:
        on(inside["far", level, p], lambda: phase1(level, p).wait_send())
    for level, j in all2:
        phase2(level, j).wait_send()
    for level in (2,) + FAR:
        phase3(level).wait_send()
    for up in (True, False):
        on(inside["near", up], lambda: neighbour(up).wait_send())

    for b in range(2):
        total = own_part[b]
        for t in (1, 3, 2):
            share(b, t).wait_recv()
            total = total + got[t - 1, b].astype(F32)
        out_ref[:, b * BLOCK : (b + 1) * BLOCK] = total.astype(BF16)

    for b in range(2):
        for t in range(1, heads):
            share(b, t).wait_send()


def solution(mesh):
    devices, heads = mesh.shape["seq"], mesh.shape["head"]

    def shards(q, k, v, w):
        rows, width = q.shape
        lanes = w.shape[1] // heads
        vmem = pl.BlockSpec(memory_space=pltpu.VMEM)
        dma = pltpu.SemaphoreType.DMA

        def gather(level):
            return pltpu.VMEM((2 ** (level - 3), 2, 3, 4 * (rows >> level), 128), BF16)

        def stage(level):
            return pltpu.VMEM((4 * (rows >> level), 128), BF16)

        return pl.pallas_call(
            functools.partial(kernel, devices, heads),
            out_shape=jax.ShapeDtypeStruct((lanes, rows), BF16),
            in_specs=[pl.BlockSpec(memory_space=pltpu.HBM)] * 4,
            out_specs=vmem,
            scratch_shapes=[
                pltpu.VMEM((rows, width), BF16),
                pltpu.VMEM((rows, width), BF16),
                pltpu.VMEM((rows, width), BF16),
                pltpu.VMEM((width, heads * lanes), BF16),
                pltpu.VMEM((2, 4 * (BLOCK + HALF), 128), BF16),
                pltpu.VMEM((2, 4 * (BLOCK + HALF), 128), BF16),
                pltpu.VMEM((3, 4 * HALF, 128), BF16),
                gather(3), gather(4), gather(5), gather(6),
                stage(2), stage(3), stage(4), stage(5), stage(6),
                pltpu.VMEM((2, 2, 128, 256), BF16),
                pltpu.VMEM((2, 2, 512, 128), BF16),
                pltpu.VMEM((2, 2, 128, 512), BF16),
                pltpu.VMEM((2, 2, 384, 128), BF16),
                pltpu.VMEM((2, 2, 128, 384), BF16),
                pltpu.VMEM((heads, lanes, width), BF16),
                pltpu.VMEM((2, lanes, BLOCK), F32),
                pltpu.VMEM((2, heads - 1, lanes, BLOCK), BF16),
                pltpu.VMEM((heads - 1, 2, lanes, BLOCK), BF16),
                pltpu.VMEM((4, 8, 256), F32),
                pltpu.VMEM((4, 8, 256), F32),
                pltpu.VMEM((4, HEAD_DIM, 256), F32),
                pltpu.SemaphoreType.REGULAR((26,)),
                dma((4,)),
                dma((5, 3)), dma((5, 3)), dma((11,)), dma((11,)), dma((5,)), dma((5,)),
                dma((2,)), dma((2,)),
                dma((2, heads - 1)), dma((2, heads - 1)),
            ],
            compiler_params=pltpu.CompilerParams(
                collective_id=0, has_side_effects=True, vmem_limit_bytes=55040 * 1024
            ),
            cost_estimate=pl.CostEstimate(
                flops=2_000_000_000, bytes_accessed=1_200_000, transcendentals=1_600_000
            ),
        )(q, k, v, w)

    placed = (P("seq", "head"), P("seq", "head"), P("seq", "head"), P("head", None))
    return jax.shard_map(
        shards, mesh=mesh, in_specs=placed, out_specs=P("head", "seq"), check_vma=False
    )
```

```python
import functools

import jax
import jax.numpy as jnp
from jax import lax
from jax.experimental import pallas as pl
from jax.experimental.pallas import tpu as pltpu
from jax.sharding import PartitionSpec as P

HEAD_DIM = 64
BLOCK = 128
LEVELS = 6
HALF = BLOCK // 2
F32 = jnp.float32
BF16 = jnp.bfloat16
MESH = pl.DeviceIdType.MESH
FAR = (3, 4, 5, 6)
RING = 7
OFF = -1e30


def dot(a, b):
    return jnp.dot(a, b, preferred_element_type=F32)


def iota(shape, dim):
    return lax.broadcasted_iota(jnp.int32, shape, dim)


def pool(rows, fine, level, repeat):
    r, c = iota((rows, fine), 0), iota((rows, fine), 1)
    hit = (c >> level) == (r & (repeat - 1))
    return jnp.where(hit, 2.0**-level, 0.0).astype(BF16)


def unpack(n):
    r, c = iota((256, 256), 0), iota((256, 256), 1)
    group, inside = r >> 6, r & 63
    source, row = inside // n, inside & (n - 1)
    return jnp.where(c == source * (4 * n) + group * n + row, 1.0, 0.0).astype(BF16)


def scores_top(s, slabs):
    top = None
    for start, rows, bias in slabs:
        m = jnp.max(s[start : start + rows], axis=0, keepdims=True)
        if bias is not None:
            m = m + bias
        top = m if top is None else jnp.maximum(top, m)
    return top


def attend(k, vt, q, slabs):
    s = dot(k, q)
    top = scores_top(s, slabs)
    parts, total = [], None
    for start, rows, bias in slabs:
        shift = top if bias is None else top - bias
        p = jnp.exp(s[start : start + rows] - shift)
        t = jnp.sum(p, axis=0, keepdims=True)
        total = t if total is None else total + t
        parts.append(p.astype(BF16))
    o = dot(vt, jnp.concatenate(parts, 0))
    o = jnp.concatenate([o[:HEAD_DIM, :BLOCK], o[HEAD_DIM:, BLOCK:]], 1)
    return top, total, o


def merge(a, b):
    top = jnp.maximum(a[0], b[0])
    fa, fb = jnp.exp(a[0] - top), jnp.exp(b[0] - top)
    return top, a[1] * fa + b[1] * fb, a[2] * fa + b[2] * fb


def kernel(
    devices, heads,
    q_hbm, k_hbm, v_hbm, w_hbm, out_ref,
    q_ref, k_ref, v_ref, w_ref, rim, near, g2, g3, g4, gat, ring, s2, s3, s4, s56,
    qbd, kb, vbt, kc, vct, wt, own_part, part, got, st_m, st_l, st_o, in_s,
    p1_s, p1_r, p2_s, p2_r, p3_s, p3_r, ring_s, ring_r, gat_s, gat_r, near_s, near_r, part_s, part_r,
):
    d = lax.axis_index("seq")
    x = lax.axis_index("head")
    core = d % 2
    y, z = (d // 2) % 4, d // 8
    gathers = {3: g3, 4: g4}
    stages = {2: s2, 3: s3, 4: s4}

    def seq(steps):
        return (d + steps + 2 * devices) % devices

    def group(level):
        return 2 ** (level - 2)

    def far_steps(level, p):
        g = group(level)
        if p == 0:
            return 2 * g
        if p == 1:
            return -2 * g
        return (3 - 6 * ((d // g) % 2)) * g

    def remote(src, dst, send, recv, axis, target):
        return pltpu.make_async_remote_copy(
            src_ref=src, dst_ref=dst, send_sem=send, recv_sem=recv,
            device_id={axis: target}, device_id_type=MESH,
        )

    def far_target(level, p):
        target = seq(far_steps(level, p))
        if level == 4 and p == 2:
            target = target + 2 - 4 * ((target // 2) % 2)
        return target

    def phase1(level, p):
        at = (level - 2, p)
        rank = (d % group(level)) // 2
        if level == 2:
            dst = g2.at[p]
        elif level == 4 and p == 2:
            dst = g4.at[1 - rank, core, p]
        else:
            dst = gathers[level].at[rank, core, p]
        return remote(stages[level], dst, p1_s.at[at], p1_r.at[at], "seq", far_target(level, p))

    def phase2():
        mine = (d // 2) % 2
        block = g4.at[mine, core]
        return remote(block, block, p2_s, p2_r, "seq", d + 2 - 4 * mine)

    def ring_step(up, k):
        rows = pl.ds(0, 48 if k <= 3 else 16)
        sign = -1 if up else 1
        src = s56.at[rows] if k == 1 else ring.at[RING + sign * (k - 1), rows]
        dst = ring.at[RING + sign * k, rows]
        at = (0 if up else 1, k - 1)
        return remote(src, dst, ring_s.at[at], ring_r.at[at], "seq", seq(8 if up else -8))

    def ring_pass(k):
        for up in (True, False):
            ring_step(up, k).wait_recv()
            if k < RING:
                ring_step(up, k + 1).start()

    def plane_gather(j):
        block = gat.at[y, core]
        to = d + 2 * ((y + j) % 4 - y)
        return remote(block, block, gat_s.at[j - 1], gat_r.at[j - 1], "seq", to)

    def phase3(level):
        if level == 2:
            src, dst = g2.at[core], g2.at[2]
        elif level == 5:
            src = dst = gat.at[:, core]
        else:
            src = dst = gathers[level].at[:, core]
        slot = level - 2
        return remote(src, dst, p3_s.at[slot], p3_r.at[slot], "seq", d + 1 - 2 * core)

    def neighbour(up):
        side = 0 if up else 1
        return remote(
            rim.at[side], near.at[side], near_s.at[side], near_r.at[side], "seq", seq(1 if up else -1)
        )

    def share(b, t):
        at = (b, t - 1)
        return remote(part.at[b, t - 1], got.at[t - 1, b], part_s.at[at], part_r.at[at], "head", (x + t) % heads)

    far1 = [(level, p) for level in (4, 3) for p in range(3)]
    two1 = [(2, 0), (2, 1)]
    all1 = far1 + two1

    loads = [
        pltpu.make_async_copy(src, dst, in_s.at[i])
        for i, (src, dst) in enumerate(
            [(k_hbm, k_ref), (v_hbm, v_ref), (q_hbm, q_ref), (w_hbm, w_ref)]
        )
    ]
    loads[0].start()
    loads[1].start()
    barrier = pltpu.get_barrier_semaphore()
    targets = [("seq", far_target(level, p)) for level, p in all1]
    targets += [("seq", d + 2 * ((y + j) % 4 - y)) for j in range(1, 4)]
    targets += [("seq", seq(1)), ("seq", seq(-1))]
    targets += [("head", (x + t) % heads) for t in range(1, heads)]
    for axis, target in targets:
        pl.semaphore_signal(barrier, inc=1, device_id={axis: target}, device_id_type=MESH)
    loads[2].start()
    loads[3].start()

    pools = jnp.concatenate(
        [pool(BLOCK, 256, 1, 128), pool(64, 256, 2, 64), pool(32, 256, 3, 32), pool(16, 256, 4, 16),
         pool(32, 256, 5, 8), pool(16, 256, 6, 4)], 0)
    loads[0].wait()
    loads[1].wait()
    k, v = k_ref[...], v_ref[...]
    ck, cv = dot(pools, k), dot(pools, v)
    blocks = [ck[:, :128], ck[:, 128:], cv[:, :128], cv[:, 128:]]
    for level, start, n in ((2, 128, 64), (3, 192, 32), (4, 224, 16)):
        for c in range(4):
            stages[level][c * n : (c + 1) * n, :] = blocks[c][start : start + n].astype(BF16)
    for level, start, n in ((5, 240, 8), (6, 272, 4)):
        owner = iota((4 * n, 128), 0) // n
        packed = blocks[0][start : start + 4 * n]
        for c in range(1, 4):
            packed = jnp.where(owner == c, blocks[c][start : start + 4 * n], packed)
        s56[0 if level == 6 else 16 : 16 if level == 6 else 48, :] = packed.astype(BF16)
    fine = [k[:, :128], k[:, 128:], v[:, :128], v[:, 128:]]
    for side in range(2):
        edge = BLOCK * (1 - side)
        for c in range(4):
            rim[side, c * BLOCK : (c + 1) * BLOCK, :] = fine[c][edge : edge + BLOCK]
            rim[side, 512 + c * HALF : 512 + (c + 1) * HALF, :] = blocks[c][side * HALF : (side + 1) * HALF].astype(BF16)

    pl.semaphore_wait(barrier, len(targets))
    ring_step(True, 1).start()
    ring_step(False, 1).start()
    for level, p in far1:
        phase1(level, p).start()
    neighbour(True).start()
    neighbour(False).start()
    for level, p in two1:
        phase1(level, p).start()
    loads[2].wait()
    qt = (q_ref[...].astype(F32) * HEAD_DIM**-0.5).T
    feature = iota((BLOCK, BLOCK), 0)
    for b in range(2):
        for hp in range(2):
            piece = qt[hp * BLOCK : (hp + 1) * BLOCK, b * BLOCK : (b + 1) * BLOCK]
            low = jnp.where(feature < HEAD_DIM, piece, 0.0)
            high = jnp.where(feature < HEAD_DIM, 0.0, piece)
            qbd[b, hp] = jnp.concatenate([low, high], 1).astype(BF16)

    def keep(u, state):
        st_m[u, 0:1, :], st_l[u, 0:1, :], st_o[u] = state

    def kept(u):
        return st_m[u, 0:1, :], st_l[u, 0:1, :], st_o[u]

    units = [(b, hp) for b in range(2) for hp in range(2)]
    for hp in range(2):
        lanes = slice(hp * BLOCK, (hp + 1) * BLOCK)
        vt = v_ref[:, lanes].T
        kk = k_ref[:, lanes]
        for b in range(2):
            keep(b * 2 + hp, attend(kk, vt, qbd[b, hp], [(0, 256, None)]))
        ring_pass(1 + hp)

    loads[3].wait()
    for i in range(heads):
        wt[i] = w_ref[:, i * 256 : (i + 1) * 256].T

    for level, p in two1:
        phase1(level, p).wait_recv()
    phase3(2).start()
    for level, p in far1:
        phase1(level, p).wait_recv()
    phase2().start()
    phase3(3).start()
    ring_pass(3)
    neighbour(True).wait_recv()
    neighbour(False).wait_recv()
    half_pool = pool(HALF, BLOCK, 1, HALF)
    lower_ok = jnp.where(d > 0, 0.0, OFF).astype(F32)
    upper_ok = jnp.where(d < devices - 1, 0.0, OFF).astype(F32)

    def far_bias(level):
        g, out = group(level), []
        e, last = d // g, devices // g - 1
        steps = (-2, 2, 3 - 6 * (e % 2))
        for step in steps:
            there = e + step
            out.append(jnp.where((there >= 0) & (there <= last), 0.0, OFF).astype(F32))
        return out

    bias2 = far_bias(2)
    phase3(2).wait_recv()
    for c in range(4):
        kind, hp = c // 2, c % 2
        strip = slice(c * BLOCK, (c + 1) * BLOCK)
        rows = slice(c * HALF, (c + 1) * HALF)
        half = slice(512 + c * HALF, 512 + (c + 1) * HALF)
        pooled = [dot(half_pool, near[side, strip, :]).astype(BF16) for side in range(2)]
        common = [near[0, half, :], near[1, half, :]] + [g2[p, rows, :] for p in range(3)]
        for b in range(2):
            full = jnp.concatenate([near[b, strip, :], pooled[1 - b]] + common, 0)
            if kind == 0:
                kb[b, hp] = full
            else:
                vbt[b, hp] = full.T
    for b, hp in units:
        first, second = (lower_ok, upper_ok) if b == 0 else (upper_ok, lower_ok)
        slabs = [(0, 128, first), (128, 64, second), (192, 64, lower_ok), (256, 64, upper_ok)]
        slabs += [(320 + 64 * p, 64, bias2[p]) for p in range(3)]
        u = b * 2 + hp
        keep(u, merge(kept(u), attend(kb[b, hp], vbt[b, hp], qbd[b, hp], slabs)))
        if u == 0:
            ring_pass(4)
        if u == 1:
            phase2().wait_recv()
            phase3(4).start()
        if u == 2:
            ring_pass(5)
    ring_pass(6)
    ring_pass(7)

    pair = z // 2
    for p, steps in enumerate((-2, 2, 3 - 6 * (pair % 2))):
        for i in range(2):
            slot = 2 * (pair + steps) + i - z + RING
            gat[y, core, 16 * (2 * p + i) : 16 * (2 * p + i + 1), :] = ring[slot, 0:16, :]
    for p, steps in enumerate((-2, 2, 3 - 6 * (z % 2))):
        gat[y, core, 96 + 32 * p : 128 + 32 * p, :] = ring[steps + RING, 16:48, :]
    for j in (2, 1, 3):
        plane_gather(j).start()

    def far_chunk(i):
        slabs, keys, values = [], ([], []), ([], [])
        for level in FAR[2 * i : 2 * i + 2]:
            n = 256 // 2**level
            g = group(level)
            for p, bias in enumerate(far_bias(level)):
                slabs.append((64 * len(slabs), 64, bias))
                if level < 5:
                    whole = gathers[level][:, :, p].reshape(g, 4 * n, 128)
                    four = [whole[:, c * n : (c + 1) * n, :].reshape(64, 128) for c in range(4)]
                else:
                    if level == 5:
                        whole = gat[:, :, 96 + 32 * p : 128 + 32 * p, :].reshape(256, 128)
                    else:
                        planes = [gat[:, :, 16 * q : 16 * q + 16, :].reshape(128, 128) for q in (2 * p, 2 * p + 1)]
                        whole = jnp.concatenate(planes, 0)
                    moved = dot(unpack(n), whole).astype(BF16)
                    four = [moved[c * 64 : (c + 1) * 64] for c in range(4)]
                for hp in range(2):
                    keys[hp].append(four[hp])
                    values[hp].append(four[2 + hp])
        for hp in range(2):
            kc[i, hp] = jnp.concatenate(keys[hp], 0)
            vct[i, hp] = jnp.concatenate(values[hp], 0).T
        return slabs

    phase3(3).wait_recv()
    phase3(4).wait_recv()
    slabs = far_chunk(0)
    for b, hp in units:
        u = b * 2 + hp
        keep(u, merge(kept(u), attend(kc[0, hp], vct[0, hp], qbd[b, hp], slabs)))
        if u == 1:
            for j in range(1, 4):
                plane_gather(j).wait_recv()
            phase3(5).start()
    phase3(5).wait_recv()
    slabs = far_chunk(1)
    for b, hp in units:
        u = b * 2 + hp
        _, total, o = merge(kept(u), attend(kc[1, hp], vct[1, hp], qbd[b, hp], slabs))
        o = (o / total).astype(BF16)
        rows = jnp.concatenate([o[:, :BLOCK], o[:, BLOCK:]], 0)
        if hp == 0:
            upper = rows
            continue
        attended = jnp.concatenate([upper, rows], 0)
        for t in (2, 1, 3):
            part[b, t - 1] = dot(wt[(x + t) % heads], attended).astype(BF16)
            share(b, t).start()
        own_part[b] = dot(wt[x], attended)

    for level, p in all1:
        phase1(level, p).wait_send()
    phase2().wait_send()
    for level in (2, 3, 4, 5):
        phase3(level).wait_send()
    for up in (True, False):
        for k in range(1, RING + 1):
            ring_step(up, k).wait_send()
    for j in range(1, 4):
        plane_gather(j).wait_send()
    neighbour(True).wait_send()
    neighbour(False).wait_send()

    for b in range(2):
        total = own_part[b]
        for t in (1, 3, 2):
            share(b, t).wait_recv()
            total = total + got[t - 1, b].astype(F32)
        out_ref[:, b * BLOCK : (b + 1) * BLOCK] = total.astype(BF16)

    for b in range(2):
        for t in range(1, heads):
            share(b, t).wait_send()


def solution(mesh):
    devices, heads = mesh.shape["seq"], mesh.shape["head"]

    def shards(q, k, v, w):
        rows, width = q.shape
        lanes = w.shape[1] // heads
        vmem = pl.BlockSpec(memory_space=pltpu.VMEM)
        dma = pltpu.SemaphoreType.DMA

        def gather(level):
            return pltpu.VMEM((2 ** (level - 3), 2, 3, 4 * (rows >> level), 128), BF16)

        def stage(level):
            return pltpu.VMEM((4 * (rows >> level), 128), BF16)

        return pl.pallas_call(
            functools.partial(kernel, devices, heads),
            out_shape=jax.ShapeDtypeStruct((lanes, rows), BF16),
            in_specs=[pl.BlockSpec(memory_space=pltpu.HBM)] * 4,
            out_specs=vmem,
            scratch_shapes=[
                pltpu.VMEM((rows, width), BF16),
                pltpu.VMEM((rows, width), BF16),
                pltpu.VMEM((rows, width), BF16),
                pltpu.VMEM((width, heads * lanes), BF16),
                pltpu.VMEM((2, 4 * (BLOCK + HALF), 128), BF16),
                pltpu.VMEM((2, 4 * (BLOCK + HALF), 128), BF16),
                pltpu.VMEM((3, 4 * HALF, 128), BF16),
                gather(3), gather(4),
                pltpu.VMEM((4, 2, 192, 128), BF16),
                pltpu.VMEM((2 * RING + 1, 48, 128), BF16),
                stage(2), stage(3), stage(4),
                pltpu.VMEM((48, 128), BF16),
                pltpu.VMEM((2, 2, 128, 256), BF16),
                pltpu.VMEM((2, 2, 512, 128), BF16),
                pltpu.VMEM((2, 2, 128, 512), BF16),
                pltpu.VMEM((2, 2, 384, 128), BF16),
                pltpu.VMEM((2, 2, 128, 384), BF16),
                pltpu.VMEM((heads, lanes, width), BF16),
                pltpu.VMEM((2, lanes, BLOCK), F32),
                pltpu.VMEM((2, heads - 1, lanes, BLOCK), BF16),
                pltpu.VMEM((heads - 1, 2, lanes, BLOCK), BF16),
                pltpu.VMEM((4, 8, 256), F32),
                pltpu.VMEM((4, 8, 256), F32),
                pltpu.VMEM((4, HEAD_DIM, 256), F32),
                dma((4,)),
                dma((3, 3)), dma((3, 3)), dma(()), dma(()), dma((4,)), dma((4,)),
                dma((2, RING)), dma((2, RING)), dma((3,)), dma((3,)),
                dma((2,)), dma((2,)),
                dma((2, heads - 1)), dma((2, heads - 1)),
            ],
            compiler_params=pltpu.CompilerParams(
                collective_id=0, has_side_effects=True, vmem_limit_bytes=55040 * 1024
            ),
            cost_estimate=pl.CostEstimate(
                flops=2_000_000_000, bytes_accessed=1_200_000, transcendentals=1_600_000
            ),
        )(q, k, v, w)

    placed = (P("seq", "head"), P("seq", "head"), P("seq", "head"), P("head", None))
    return jax.shard_map(
        shards, mesh=mesh, in_specs=placed, out_specs=P("head", "seq"), check_vma=False
    )
```

```python
import functools

import jax
import jax.numpy as jnp
from jax import lax
from jax.experimental import pallas as pl
from jax.experimental.pallas import tpu as pltpu
from jax.sharding import PartitionSpec as P

HEAD_DIM = 64
BLOCK = 128
LEVELS = 6
HALF = BLOCK // 2
F32 = jnp.float32
BF16 = jnp.bfloat16
MESH = pl.DeviceIdType.MESH
FAR = (3, 4, 5, 6)
OFF = -1e30


def dot(a, b):
    return jnp.dot(a, b, preferred_element_type=F32)


def iota(shape, dim):
    return lax.broadcasted_iota(jnp.int32, shape, dim)


def pool(rows, fine, level, repeat):
    r, c = iota((rows, fine), 0), iota((rows, fine), 1)
    hit = (c >> level) == (r & (repeat - 1))
    return jnp.where(hit, 2.0**-level, 0.0).astype(BF16)


def unpack(n):
    r, c = iota((256, 256), 0), iota((256, 256), 1)
    group, inside = r >> 6, r & 63
    source, row = inside // n, inside & (n - 1)
    return jnp.where(c == source * (4 * n) + group * n + row, 1.0, 0.0).astype(BF16)


def scores_top(s, slabs):
    top = None
    for start, rows, bias in slabs:
        m = jnp.max(s[start : start + rows], axis=0, keepdims=True)
        if bias is not None:
            m = m + bias
        top = m if top is None else jnp.maximum(top, m)
    return top


def attend(k, vt, q, slabs):
    s = dot(k, q)
    top = scores_top(s, slabs)
    parts, total = [], None
    for start, rows, bias in slabs:
        shift = top if bias is None else top - bias
        p = jnp.exp(s[start : start + rows] - shift)
        t = jnp.sum(p, axis=0, keepdims=True)
        total = t if total is None else total + t
        parts.append(p.astype(BF16))
    o = dot(vt, jnp.concatenate(parts, 0))
    o = jnp.concatenate([o[:HEAD_DIM, :BLOCK], o[HEAD_DIM:, BLOCK:]], 1)
    return top, total, o


def merge(a, b):
    top = jnp.maximum(a[0], b[0])
    fa, fb = jnp.exp(a[0] - top), jnp.exp(b[0] - top)
    return top, a[1] * fa + b[1] * fb, a[2] * fa + b[2] * fb


def kernel(
    devices, heads,
    q_hbm, k_hbm, v_hbm, w_hbm, out_ref,
    q_ref, k_ref, v_ref, w_ref, rim, near, g2, g3, g4, g5, g6, s2, s3, s4, s5, s6,
    qbd, kb, vbt, kc, vct, wt, own_part, part, got, st_m, st_l, st_o, in_s,
    p1_s, p1_r, p2_s, p2_r, near_s, near_r, part_s, part_r,
):
    d = lax.axis_index("seq")
    x = lax.axis_index("head")
    core = d % 2
    gathers = {3: g3, 4: g4, 5: g5, 6: g6}
    stages = {2: s2, 3: s3, 4: s4, 5: s5, 6: s6}

    def seq(steps):
        return (d + steps + 2 * devices) % devices

    def group(level):
        return 2 ** (level - 2)

    def far_steps(level, p):
        g = group(level)
        if p == 0:
            return 2 * g
        if p == 1:
            return -2 * g
        return (3 - 6 * ((d // g) % 2)) * g

    def remote(src, dst, send, recv, axis, target):
        return pltpu.make_async_remote_copy(
            src_ref=src, dst_ref=dst, send_sem=send, recv_sem=recv,
            device_id={axis: target}, device_id_type=MESH,
        )

    def far_target(level, p):
        target = seq(far_steps(level, p))
        if level == 4 and p == 2:
            target = target + 2 - 4 * ((target // 2) % 2)
        return target

    def phase1(level, p):
        at = (level - 2, p)
        rank = (d % group(level)) // 2
        if level == 2:
            dst = g2.at[p]
        elif level == 4 and p == 2:
            dst = g4.at[1 - rank, core, p]
        else:
            dst = gathers[level].at[rank, core, p]
        return remote(stages[level], dst, p1_s.at[at], p1_r.at[at], "seq", far_target(level, p))

    def across(target, flip):
        return target + flip * (1 - 2 * core)

    def phase1_across():
        return remote(
            s3, g3.at[0, core, 2], p1_s.at[1, 0], p1_r.at[1, 0], "seq", across(far_target(3, 2), 1)
        )

    odd = (d // 2) % 2

    def phase2_target(level, j):
        if level == 3:
            which, flip = divmod(j - 1, 2)
            return across(seq((1, 5)[which] * 2 * (1 - 2 * odd)), flip)
        g = group(level)
        return d - d % g + (d % g + j) % g

    def phase2(level, j):
        slot = {3: 0, 4: 4, 5: 7, 6: 14}[level] + j - 1
        if level == 3:
            src = g3.at[0, core, 2]
            dst = g3.at[0, core, 1 - odd if j <= 2 else odd]
        else:
            src = dst = gathers[level].at[(d % group(level)) // 2, core]
        return remote(src, dst, p2_s.at[slot], p2_r.at[slot], "seq", phase2_target(level, j))

    def neighbour(up):
        side = 0 if up else 1
        return remote(
            rim.at[side], near.at[side], near_s.at[side], near_r.at[side], "seq", seq(1 if up else -1)
        )

    def share(b, t):
        at = (b, t - 1)
        return remote(part.at[b, t - 1], got.at[t - 1, b], part_s.at[at], part_r.at[at], "head", (x + t) % heads)

    far1 = [(6, 0), (6, 1), (6, 2), (5, 0), (5, 1), (5, 2), (4, 2), (4, 0), (4, 1), (3, 2)]
    two1 = [(2, 0), (2, 1), (2, 2)]
    all1 = far1 + two1
    all2 = [(3, j) for j in range(1, 5)] + [(level, j) for level in (4, 5, 6) for j in range(1, group(level))]

    def pass_on(level):
        for other, j in all2:
            if other == level:
                phase2(level, j).start()

    def passed(level):
        for other, j in all2:
            if other == level:
                phase2(level, j).wait_recv()

    loads = [
        pltpu.make_async_copy(src, dst, in_s.at[i])
        for i, (src, dst) in enumerate(
            [(k_hbm, k_ref), (v_hbm, v_ref), (q_hbm, q_ref), (w_hbm, w_ref)]
        )
    ]
    loads[0].start()
    loads[1].start()
    barrier = pltpu.get_barrier_semaphore()
    targets = [("seq", far_target(level, p)) for level, p in all1]
    targets += [("seq", phase2_target(6, j)) for j in range(1, 16)]
    targets += [("seq", phase2_target(3, j)) for j in (3, 4)]
    targets += [("seq", across(far_target(3, 2), 1)), ("seq", seq(1)), ("seq", seq(-1))]
    targets += [("head", (x + t) % heads) for t in range(1, heads)]
    for axis, target in targets:
        pl.semaphore_signal(barrier, inc=1, device_id={axis: target}, device_id_type=MESH)
    loads[2].start()
    loads[3].start()

    pools = jnp.concatenate(
        [pool(BLOCK, 256, 1, 128), pool(64, 256, 2, 64), pool(32, 256, 3, 32), pool(16, 256, 4, 16),
         pool(32, 256, 5, 8), pool(16, 256, 6, 4)], 0)
    loads[0].wait()
    loads[1].wait()
    k, v = k_ref[...], v_ref[...]
    ck, cv = dot(pools, k), dot(pools, v)
    blocks = [ck[:, :128], ck[:, 128:], cv[:, :128], cv[:, 128:]]
    for level, start, n in ((2, 128, 64), (3, 192, 32), (4, 224, 16)):
        for c in range(4):
            stages[level][c * n : (c + 1) * n, :] = blocks[c][start : start + n].astype(BF16)
    for level, start, n in ((5, 240, 8), (6, 272, 4)):
        owner = iota((4 * n, 128), 0) // n
        packed = blocks[0][start : start + 4 * n]
        for c in range(1, 4):
            packed = jnp.where(owner == c, blocks[c][start : start + 4 * n], packed)
        stages[level][...] = packed.astype(BF16)
    fine = [k[:, :128], k[:, 128:], v[:, :128], v[:, 128:]]
    for side in range(2):
        edge = BLOCK * (1 - side)
        for c in range(4):
            rim[side, c * BLOCK : (c + 1) * BLOCK, :] = fine[c][edge : edge + BLOCK]
            rim[side, 512 + c * HALF : 512 + (c + 1) * HALF, :] = blocks[c][side * HALF : (side + 1) * HALF].astype(BF16)

    pl.semaphore_wait(barrier, len(targets))
    for level, p in far1:
        phase1(level, p).start()
    phase1_across().start()
    neighbour(True).start()
    neighbour(False).start()
    for level, p in two1:
        phase1(level, p).start()
    loads[2].wait()
    qt = (q_ref[...].astype(F32) * HEAD_DIM**-0.5).T
    feature = iota((BLOCK, BLOCK), 0)
    for b in range(2):
        for hp in range(2):
            piece = qt[hp * BLOCK : (hp + 1) * BLOCK, b * BLOCK : (b + 1) * BLOCK]
            low = jnp.where(feature < HEAD_DIM, piece, 0.0)
            high = jnp.where(feature < HEAD_DIM, 0.0, piece)
            qbd[b, hp] = jnp.concatenate([low, high], 1).astype(BF16)

    def keep(u, state):
        st_m[u, 0:1, :], st_l[u, 0:1, :], st_o[u] = state

    def kept(u):
        return st_m[u, 0:1, :], st_l[u, 0:1, :], st_o[u]

    units = [(b, hp) for b in range(2) for hp in range(2)]
    for hp in range(2):
        lanes = slice(hp * BLOCK, (hp + 1) * BLOCK)
        vt = v_ref[:, lanes].T
        kk = k_ref[:, lanes]
        for b in range(2):
            keep(b * 2 + hp, attend(kk, vt, qbd[b, hp], [(0, 256, None)]))

    loads[3].wait()
    for i in range(heads):
        wt[i] = w_ref[:, i * 256 : (i + 1) * 256].T

    for level, p in far1:
        phase1(level, p).wait_recv()
        if (level, p) in ((6, 2), (5, 2), (4, 1), (3, 2)):
            pass_on(level)
    phase1_across().wait_recv()

    for level, p in two1:
        phase1(level, p).wait_recv()
    neighbour(True).wait_recv()
    neighbour(False).wait_recv()
    half_pool = pool(HALF, BLOCK, 1, HALF)
    lower_ok = jnp.where(d > 0, 0.0, OFF).astype(F32)
    upper_ok = jnp.where(d < devices - 1, 0.0, OFF).astype(F32)

    def far_bias(level):
        g, out = group(level), []
        e, last = d // g, devices // g - 1
        steps = (-2, 2, 3 - 6 * (e % 2))
        for step in steps:
            there = e + step
            out.append(jnp.where((there >= 0) & (there <= last), 0.0, OFF).astype(F32))
        return out

    bias2 = far_bias(2)
    for c in range(4):
        kind, hp = c // 2, c % 2
        strip = slice(c * BLOCK, (c + 1) * BLOCK)
        rows = slice(c * HALF, (c + 1) * HALF)
        half = slice(512 + c * HALF, 512 + (c + 1) * HALF)
        pooled = [dot(half_pool, near[side, strip, :]).astype(BF16) for side in range(2)]
        common = [near[0, half, :], near[1, half, :]] + [g2[p, rows, :] for p in range(3)]
        for b in range(2):
            full = jnp.concatenate([near[b, strip, :], pooled[1 - b]] + common, 0)
            if kind == 0:
                kb[b, hp] = full
            else:
                vbt[b, hp] = full.T
    for b, hp in units:
        first, second = (lower_ok, upper_ok) if b == 0 else (upper_ok, lower_ok)
        slabs = [(0, 128, first), (128, 64, second), (192, 64, lower_ok), (256, 64, upper_ok)]
        slabs += [(320 + 64 * p, 64, bias2[p]) for p in range(3)]
        u = b * 2 + hp
        keep(u, merge(kept(u), attend(kb[b, hp], vbt[b, hp], qbd[b, hp], slabs)))

    def far_chunk(i):
        slabs, keys, values = [], ([], []), ([], [])
        for level in FAR[2 * i : 2 * i + 2]:
            passed(level)
            n = 256 // 2**level
            g = group(level)
            for p, bias in enumerate(far_bias(level)):
                slabs.append((64 * len(slabs), 64, bias))
                whole = gathers[level][:, :, p].reshape(g, 4 * n, 128)
                if n >= 16:
                    four = [whole[:, c * n : (c + 1) * n, :].reshape(64, 128) for c in range(4)]
                else:
                    moved = dot(unpack(n), whole.reshape(256, 128)).astype(BF16)
                    four = [moved[c * 64 : (c + 1) * 64] for c in range(4)]
                for hp in range(2):
                    keys[hp].append(four[hp])
                    values[hp].append(four[2 + hp])
        for hp in range(2):
            kc[i, hp] = jnp.concatenate(keys[hp], 0)
            vct[i, hp] = jnp.concatenate(values[hp], 0).T
        return slabs

    slabs = far_chunk(0)
    for b, hp in units:
        u = b * 2 + hp
        keep(u, merge(kept(u), attend(kc[0, hp], vct[0, hp], qbd[b, hp], slabs)))
    slabs = far_chunk(1)
    for b, hp in units:
        u = b * 2 + hp
        _, total, o = merge(kept(u), attend(kc[1, hp], vct[1, hp], qbd[b, hp], slabs))
        o = (o / total).astype(BF16)
        rows = jnp.concatenate([o[:, :BLOCK], o[:, BLOCK:]], 0)
        if hp == 0:
            upper = rows
            continue
        attended = jnp.concatenate([upper, rows], 0)
        for t in (2, 1, 3):
            part[b, t - 1] = dot(wt[(x + t) % heads], attended).astype(BF16)
            share(b, t).start()
        own_part[b] = dot(wt[x], attended)

    for level, p in all1:
        phase1(level, p).wait_send()
    for level, j in all2:
        phase2(level, j).wait_send()
    phase1_across().wait_send()
    neighbour(True).wait_send()
    neighbour(False).wait_send()

    for b in range(2):
        total = own_part[b]
        for t in (1, 3, 2):
            share(b, t).wait_recv()
            total = total + got[t - 1, b].astype(F32)
        out_ref[:, b * BLOCK : (b + 1) * BLOCK] = total.astype(BF16)

    for b in range(2):
        for t in range(1, heads):
            share(b, t).wait_send()


def solution(mesh):
    devices, heads = mesh.shape["seq"], mesh.shape["head"]

    def shards(q, k, v, w):
        rows, width = q.shape
        lanes = w.shape[1] // heads
        vmem = pl.BlockSpec(memory_space=pltpu.VMEM)
        dma = pltpu.SemaphoreType.DMA

        def gather(level):
            return pltpu.VMEM((2 ** (level - 3), 2, 3, 4 * (rows >> level), 128), BF16)

        def stage(level):
            return pltpu.VMEM((4 * (rows >> level), 128), BF16)

        return pl.pallas_call(
            functools.partial(kernel, devices, heads),
            out_shape=jax.ShapeDtypeStruct((lanes, rows), BF16),
            in_specs=[pl.BlockSpec(memory_space=pltpu.HBM)] * 4,
            out_specs=vmem,
            scratch_shapes=[
                pltpu.VMEM((rows, width), BF16),
                pltpu.VMEM((rows, width), BF16),
                pltpu.VMEM((rows, width), BF16),
                pltpu.VMEM((width, heads * lanes), BF16),
                pltpu.VMEM((2, 4 * (BLOCK + HALF), 128), BF16),
                pltpu.VMEM((2, 4 * (BLOCK + HALF), 128), BF16),
                pltpu.VMEM((3, 4 * HALF, 128), BF16),
                gather(3), gather(4), gather(5), gather(6),
                stage(2), stage(3), stage(4), stage(5), stage(6),
                pltpu.VMEM((2, 2, 128, 256), BF16),
                pltpu.VMEM((2, 2, 512, 128), BF16),
                pltpu.VMEM((2, 2, 128, 512), BF16),
                pltpu.VMEM((2, 2, 384, 128), BF16),
                pltpu.VMEM((2, 2, 128, 384), BF16),
                pltpu.VMEM((heads, lanes, width), BF16),
                pltpu.VMEM((2, lanes, BLOCK), F32),
                pltpu.VMEM((2, heads - 1, lanes, BLOCK), BF16),
                pltpu.VMEM((heads - 1, 2, lanes, BLOCK), BF16),
                pltpu.VMEM((4, 8, 256), F32),
                pltpu.VMEM((4, 8, 256), F32),
                pltpu.VMEM((4, HEAD_DIM, 256), F32),
                dma((4,)),
                dma((5, 3)), dma((5, 3)), dma((29,)), dma((29,)),
                dma((2,)), dma((2,)),
                dma((2, heads - 1)), dma((2, heads - 1)),
            ],
            compiler_params=pltpu.CompilerParams(
                collective_id=0, has_side_effects=True, vmem_limit_bytes=55040 * 1024
            ),
            cost_estimate=pl.CostEstimate(
                flops=2_000_000_000, bytes_accessed=1_200_000, transcendentals=1_600_000
            ),
        )(q, k, v, w)

    placed = (P("seq", "head"), P("seq", "head"), P("seq", "head"), P("head", None))
    return jax.shard_map(
        shards, mesh=mesh, in_specs=placed, out_specs=P("head", "seq"), check_vma=False
    )
```

```python
import functools

import jax
import jax.numpy as jnp
from jax import lax
from jax.experimental import pallas as pl
from jax.experimental.pallas import tpu as pltpu
from jax.sharding import PartitionSpec as P

HEAD_DIM = 64
BLOCK = 128
LEVELS = 6
HALF = BLOCK // 2
F32 = jnp.float32
BF16 = jnp.bfloat16
MESH = pl.DeviceIdType.MESH
FAR = (3, 4, 5, 6)
OFF = -1e30
EARLY = 4


def dot(a, b):
    return jnp.dot(a, b, preferred_element_type=F32)


def iota(shape, dim):
    return lax.broadcasted_iota(jnp.int32, shape, dim)


def pool(rows, fine, level, repeat):
    r, c = iota((rows, fine), 0), iota((rows, fine), 1)
    hit = (c >> level) == (r & (repeat - 1))
    return jnp.where(hit, 2.0**-level, 0.0).astype(BF16)


def unpack(n):
    r, c = iota((256, 256), 0), iota((256, 256), 1)
    group, inside = r >> 6, r & 63
    source, row = inside // n, inside & (n - 1)
    return jnp.where(c == source * (4 * n) + group * n + row, 1.0, 0.0).astype(BF16)


def scores_top(s, slabs):
    top = None
    for start, rows, bias in slabs:
        m = jnp.max(s[start : start + rows], axis=0, keepdims=True)
        if bias is not None:
            m = m + bias
        top = m if top is None else jnp.maximum(top, m)
    return top


def attend(k, vt, q, slabs):
    s = dot(k, q)
    top = scores_top(s, slabs)
    parts, total = [], None
    for start, rows, bias in slabs:
        shift = top if bias is None else top - bias
        p = jnp.exp(s[start : start + rows] - shift)
        t = jnp.sum(p, axis=0, keepdims=True)
        total = t if total is None else total + t
        parts.append(p.astype(BF16))
    o = dot(vt, jnp.concatenate(parts, 0))
    o = jnp.concatenate([o[:HEAD_DIM, :BLOCK], o[HEAD_DIM:, BLOCK:]], 1)
    return top, total, o


def merge(a, b):
    top = jnp.maximum(a[0], b[0])
    fa, fb = jnp.exp(a[0] - top), jnp.exp(b[0] - top)
    return top, a[1] * fa + b[1] * fb, a[2] * fa + b[2] * fb


def kernel(
    devices, heads,
    q_hbm, k_hbm, v_hbm, w_hbm, out_ref,
    q_ref, k_ref, v_ref, w_ref, rim, near, g2, g3, g4, g5, g6, s2, s3, s4, s5, s6,
    qbd, kb, vbt, kc, vct, wt, own_part, part, got, st_m, st_l, st_o, grants, in_s,
    p1_s, p1_r, p2_s, p2_r, p3_s, p3_r, near_s, near_r, part_s, part_r,
):
    d = lax.axis_index("seq")
    x = lax.axis_index("head")
    core = d % 2
    gathers = {3: g3, 4: g4, 5: g5, 6: g6}
    stages = {2: s2, 3: s3, 4: s4, 5: s5, 6: s6}

    def seq(steps):
        return (d + steps + 2 * devices) % devices

    def group(level):
        return 2 ** (level - 2)

    def far_steps(level, p):
        g = group(level)
        if p == 0:
            return 2 * g
        if p == 1:
            return -2 * g
        return (3 - 6 * ((d // g) % 2)) * g

    def remote(src, dst, send, recv, axis, target):
        return pltpu.make_async_remote_copy(
            src_ref=src, dst_ref=dst, send_sem=send, recv_sem=recv,
            device_id={axis: target}, device_id_type=MESH,
        )

    def far_target(level, p):
        target = seq(far_steps(level, p))
        if level == 4 and p == 2:
            target = target + 2 - 4 * ((target // 2) % 2)
        return target

    def phase1(level, p):
        at = (level - 2, p)
        rank = (d % group(level)) // 2
        if level == 2:
            dst = g2.at[p]
        elif level == 4 and p == 2:
            dst = g4.at[1 - rank, core, p]
        else:
            dst = gathers[level].at[rank, core, p]
        return remote(stages[level], dst, p1_s.at[at], p1_r.at[at], "seq", far_target(level, p))

    def phase2_target(level, j):
        chips = group(level) // 2
        mine = (d // 2) % chips
        return d - 2 * mine + 2 * ((mine + j) % chips)

    def phase2(level, j):
        slot = {4: 0, 5: 1, 6: 4}[level] + j - 1
        block = gathers[level].at[(d // 2) % (group(level) // 2), core]
        return remote(block, block, p2_s.at[slot], p2_r.at[slot], "seq", phase2_target(level, j))

    def phase3(level):
        if level == 2:
            src, dst = g2.at[core], g2.at[2]
        else:
            src = dst = gathers[level].at[:, core]
        slot = level - 2
        return remote(src, dst, p3_s.at[slot], p3_r.at[slot], "seq", d + 1 - 2 * core)

    def neighbour(up):
        side = 0 if up else 1
        return remote(
            rim.at[side], near.at[side], near_s.at[side], near_r.at[side], "seq", seq(1 if up else -1)
        )

    def share(b, t):
        at = (b, t - 1)
        return remote(part.at[b, t - 1], got.at[t - 1, b], part_s.at[at], part_r.at[at], "head", (x + t) % heads)

    all1 = [(level, p) for level in (6, 5, 4, 3, 2) for p in range(3 if level > 2 else 2)]
    all2 = [(level, j) for level in (4, 5, 6) for j in range(1, group(level) // 2)]

    def pass_on(level):
        for other, j in all2:
            if other == level:
                phase2(level, j).start()

    def passed(level):
        for other, j in all2:
            if other == level:
                phase2(level, j).wait_recv()

    back = (1, 0, 2)
    relations = {}
    for level, p in all1:
        there = d // group(level) + far_steps(level, p) // group(level)
        inside = (there >= 0) & (there < devices // group(level))
        relations["far", level, p] = ("seq", far_target(level, p), ("far", level, back[p]), inside)
    for up in (True, False):
        inside = d < devices - 1 if up else d > 0
        relations["near", up] = ("seq", seq(1 if up else -1), ("near", not up), inside)
    for j in range(1, 8):
        relations["mate", j] = ("seq", phase2_target(6, j), ("mate", 8 - j), True)
    for t in range(1, heads):
        relations["head", t] = ("head", (x + t) % heads, ("head", heads - t), True)
    slots = {name: i for i, name in enumerate(relations)}
    inside = {name: relation[3] for name, relation in relations.items()}
    above, below = {}, {}
    for name, (axis, target, _, valid) in relations.items():
        here = d if axis == "seq" else x
        above[name] = (target > here) & valid
        below[name] = (target < here) & valid

    def on(condition, *steps):
        @pl.when(condition)
        def _():
            for step in steps:
                step()

    def signal(semaphore, name):
        axis, target = relations[name][:2]
        pl.semaphore_signal(semaphore, inc=1, device_id={axis: target}, device_id_type=MESH)

    def granted(name, *steps):
        on(above[name], lambda: pl.semaphore_wait(grants.at[slots[name]], 1), *steps)

    def send_above(level, p):
        granted(("far", level, p), lambda: phase1(level, p).start())

    def arrived(level, p):
        on(inside["far", level, back[p]], lambda: phase1(level, p).wait_recv())

    loads = [
        pltpu.make_async_copy(src, dst, in_s.at[i])
        for i, (src, dst) in enumerate(
            [(k_hbm, k_ref), (v_hbm, v_ref), (q_hbm, q_ref), (w_hbm, w_ref)]
        )
    ]
    loads[0].start()
    loads[1].start()
    barrier = pltpu.get_barrier_semaphore()
    for name in relations:
        on(above[name], lambda: signal(barrier, name))
    loads[2].start()
    loads[3].start()

    pools = jnp.concatenate(
        [pool(BLOCK, 256, 1, 128), pool(64, 256, 2, 64), pool(32, 256, 3, 32), pool(16, 256, 4, 16),
         pool(32, 256, 5, 8), pool(16, 256, 6, 4)], 0)
    loads[0].wait()
    loads[1].wait()
    k, v = k_ref[...], v_ref[...]
    ck, cv = dot(pools, k), dot(pools, v)
    blocks = [ck[:, :128], ck[:, 128:], cv[:, :128], cv[:, 128:]]
    for level, start, n in ((2, 128, 64), (3, 192, 32), (4, 224, 16)):
        for c in range(4):
            stages[level][c * n : (c + 1) * n, :] = blocks[c][start : start + n].astype(BF16)
    for level, start, n in ((5, 240, 8), (6, 272, 4)):
        owner = iota((4 * n, 128), 0) // n
        packed = blocks[0][start : start + 4 * n]
        for c in range(1, 4):
            packed = jnp.where(owner == c, blocks[c][start : start + 4 * n], packed)
        stages[level][...] = packed.astype(BF16)
    fine = [k[:, :128], k[:, 128:], v[:, :128], v[:, 128:]]
    for side in range(2):
        edge = BLOCK * (1 - side)
        for c in range(4):
            rim[side, c * BLOCK : (c + 1) * BLOCK, :] = fine[c][edge : edge + BLOCK]
            rim[side, 512 + c * HALF : 512 + (c + 1) * HALF, :] = blocks[c][side * HALF : (side + 1) * HALF].astype(BF16)

    count = sum(jnp.where(below[name], 1, 0) for name in relations)
    on(count > 0, lambda: pl.semaphore_wait(barrier, count))
    for name in relations:
        on(below[name], lambda: signal(grants.at[slots[relations[name][2]]], name))
    for level, p in all1:
        on(below["far", level, p], lambda: phase1(level, p).start())
    on(below["near", False], lambda: neighbour(False).start())

    def clear(ref):
        ref[...] = jnp.zeros(ref.shape, ref.dtype)

    for level, p in all1:
        slot = g2.at[p] if level == 2 else gathers[level].at[(d % group(level)) // 2, core, p]
        on(jnp.logical_not(inside["far", level, back[p]]), lambda: clear(slot))
    on(d == 0, lambda: clear(near.at[0]))
    on(d == devices - 1, lambda: clear(near.at[1]))
    granted(("near", True), lambda: neighbour(True).start())

    loads[2].wait()
    qt = (q_ref[...].astype(F32) * HEAD_DIM**-0.5).T
    feature = iota((BLOCK, BLOCK), 0)
    for b in range(2):
        for hp in range(2):
            piece = qt[hp * BLOCK : (hp + 1) * BLOCK, b * BLOCK : (b + 1) * BLOCK]
            low = jnp.where(feature < HEAD_DIM, piece, 0.0)
            high = jnp.where(feature < HEAD_DIM, 0.0, piece)
            qbd[b, hp] = jnp.concatenate([low, high], 1).astype(BF16)

    def keep(u, state):
        st_m[u, 0:1, :], st_l[u, 0:1, :], st_o[u] = state

    def kept(u):
        return st_m[u, 0:1, :], st_l[u, 0:1, :], st_o[u]

    units = [(b, hp) for b in range(2) for hp in range(2)]
    for hp in range(2):
        lanes = slice(hp * BLOCK, (hp + 1) * BLOCK)
        vt = v_ref[:, lanes].T
        kk = k_ref[:, lanes]
        for b in range(2):
            keep(b * 2 + hp, attend(kk, vt, qbd[b, hp], [(0, 256, None)]))

    loads[3].wait()
    for i in range(heads):
        wt[i] = w_ref[:, i * 256 : (i + 1) * 256].T

    def exchange(level):
        for p in range(3 if level > 2 else 2):
            send_above(level, p)

    def gathered(level):
        for p in range(3 if level > 2 else 2):
            arrived(level, p)

    late = d // 8 >= EARLY

    def exchange6(condition):
        for p in range(3):
            name = ("far", 6, p)
            on(
                above[name] & condition,
                lambda: pl.semaphore_wait(grants.at[slots[name]], 1),
                lambda: phase1(6, p).start(),
            )

    def gather6(condition):
        for p in range(3):
            on(inside["far", 6, back[p]] & condition, lambda: phase1(6, p).wait_recv())
        on(condition, lambda: pass_on(6))

    for level in (2, 3, 4, 5):
        exchange(level)
    exchange6(late)
    for j in range(1, 8):
        granted(("mate", j))

    gathered(2)
    phase3(2).start()
    gathered(3)
    phase3(3).start()
    gathered(4)
    pass_on(4)
    gathered(5)
    pass_on(5)
    on(inside["near", False], lambda: neighbour(True).wait_recv())
    on(inside["near", True], lambda: neighbour(False).wait_recv())
    half_pool = pool(HALF, BLOCK, 1, HALF)
    lower_ok = jnp.where(d > 0, 0.0, OFF).astype(F32)
    upper_ok = jnp.where(d < devices - 1, 0.0, OFF).astype(F32)

    def far_bias(level):
        g, out = group(level), []
        e, last = d // g, devices // g - 1
        steps = (-2, 2, 3 - 6 * (e % 2))
        for step in steps:
            there = e + step
            out.append(jnp.where((there >= 0) & (there <= last), 0.0, OFF).astype(F32))
        return out

    bias2 = far_bias(2)
    phase3(2).wait_recv()
    for c in range(4):
        kind, hp = c // 2, c % 2
        strip = slice(c * BLOCK, (c + 1) * BLOCK)
        rows = slice(c * HALF, (c + 1) * HALF)
        half = slice(512 + c * HALF, 512 + (c + 1) * HALF)
        pooled = [dot(half_pool, near[side, strip, :]).astype(BF16) for side in range(2)]
        common = [near[0, half, :], near[1, half, :]] + [g2[p, rows, :] for p in range(3)]
        for b in range(2):
            full = jnp.concatenate([near[b, strip, :], pooled[1 - b]] + common, 0)
            if kind == 0:
                kb[b, hp] = full
            else:
                vbt[b, hp] = full.T
    for b, hp in units:
        first, second = (lower_ok, upper_ok) if b == 0 else (upper_ok, lower_ok)
        slabs = [(0, 128, first), (128, 64, second), (192, 64, lower_ok), (256, 64, upper_ok)]
        slabs += [(320 + 64 * p, 64, bias2[p]) for p in range(3)]
        u = b * 2 + hp
        keep(u, merge(kept(u), attend(kb[b, hp], vbt[b, hp], qbd[b, hp], slabs)))
        if u == 1:
            passed(4)
            phase3(4).start()
    passed(5)
    phase3(5).start()
    gather6(late)

    def far_chunk(i):
        slabs, keys, values = [], ([], []), ([], [])
        for level in FAR[2 * i : 2 * i + 2]:
            phase3(level).wait_recv()
            n = 256 // 2**level
            g = group(level)
            for p, bias in enumerate(far_bias(level)):
                slabs.append((64 * len(slabs), 64, bias))
                whole = gathers[level][:, :, p].reshape(g, 4 * n, 128)
                if n >= 16:
                    four = [whole[:, c * n : (c + 1) * n, :].reshape(64, 128) for c in range(4)]
                else:
                    moved = dot(unpack(n), whole.reshape(256, 128)).astype(BF16)
                    four = [moved[c * 64 : (c + 1) * 64] for c in range(4)]
                for hp in range(2):
                    keys[hp].append(four[hp])
                    values[hp].append(four[2 + hp])
        for hp in range(2):
            kc[i, hp] = jnp.concatenate(keys[hp], 0)
            vct[i, hp] = jnp.concatenate(values[hp], 0).T
        return slabs

    slabs = far_chunk(0)
    for b, hp in units:
        u = b * 2 + hp
        keep(u, merge(kept(u), attend(kc[0, hp], vct[0, hp], qbd[b, hp], slabs)))
    early = jnp.logical_not(late)
    exchange6(early)
    gather6(early)
    for t in range(1, heads):
        granted(("head", t))
    passed(6)
    phase3(6).start()
    slabs = far_chunk(1)
    for b, hp in units:
        u = b * 2 + hp
        _, total, o = merge(kept(u), attend(kc[1, hp], vct[1, hp], qbd[b, hp], slabs))
        o = (o / total).astype(BF16)
        rows = jnp.concatenate([o[:, :BLOCK], o[:, BLOCK:]], 0)
        if hp == 0:
            upper = rows
            continue
        attended = jnp.concatenate([upper, rows], 0)
        for t in (2, 1, 3):
            part[b, t - 1] = dot(wt[(x + t) % heads], attended).astype(BF16)
            share(b, t).start()
        own_part[b] = dot(wt[x], attended)

    for level, p in all1:
        on(inside["far", level, p], lambda: phase1(level, p).wait_send())
    for level, j in all2:
        phase2(level, j).wait_send()
    for level in (2,) + FAR:
        phase3(level).wait_send()
    for up in (True, False):
        on(inside["near", up], lambda: neighbour(up).wait_send())

    for b in range(2):
        total = own_part[b]
        for t in (1, 3, 2):
            share(b, t).wait_recv()
            total = total + got[t - 1, b].astype(F32)
        out_ref[:, b * BLOCK : (b + 1) * BLOCK] = total.astype(BF16)

    for b in range(2):
        for t in range(1, heads):
            share(b, t).wait_send()


def solution(mesh):
    devices, heads = mesh.shape["seq"], mesh.shape["head"]

    def shards(q, k, v, w):
        rows, width = q.shape
        lanes = w.shape[1] // heads
        vmem = pl.BlockSpec(memory_space=pltpu.VMEM)
        dma = pltpu.SemaphoreType.DMA

        def gather(level):
            return pltpu.VMEM((2 ** (level - 3), 2, 3, 4 * (rows >> level), 128), BF16)

        def stage(level):
            return pltpu.VMEM((4 * (rows >> level), 128), BF16)

        return pl.pallas_call(
            functools.partial(kernel, devices, heads),
            out_shape=jax.ShapeDtypeStruct((lanes, rows), BF16),
            in_specs=[pl.BlockSpec(memory_space=pltpu.HBM)] * 4,
            out_specs=vmem,
            scratch_shapes=[
                pltpu.VMEM((rows, width), BF16),
                pltpu.VMEM((rows, width), BF16),
                pltpu.VMEM((rows, width), BF16),
                pltpu.VMEM((width, heads * lanes), BF16),
                pltpu.VMEM((2, 4 * (BLOCK + HALF), 128), BF16),
                pltpu.VMEM((2, 4 * (BLOCK + HALF), 128), BF16),
                pltpu.VMEM((3, 4 * HALF, 128), BF16),
                gather(3), gather(4), gather(5), gather(6),
                stage(2), stage(3), stage(4), stage(5), stage(6),
                pltpu.VMEM((2, 2, 128, 256), BF16),
                pltpu.VMEM((2, 2, 512, 128), BF16),
                pltpu.VMEM((2, 2, 128, 512), BF16),
                pltpu.VMEM((2, 2, 384, 128), BF16),
                pltpu.VMEM((2, 2, 128, 384), BF16),
                pltpu.VMEM((heads, lanes, width), BF16),
                pltpu.VMEM((2, lanes, BLOCK), F32),
                pltpu.VMEM((2, heads - 1, lanes, BLOCK), BF16),
                pltpu.VMEM((heads - 1, 2, lanes, BLOCK), BF16),
                pltpu.VMEM((4, 8, 256), F32),
                pltpu.VMEM((4, 8, 256), F32),
                pltpu.VMEM((4, HEAD_DIM, 256), F32),
                pltpu.SemaphoreType.REGULAR((26,)),
                dma((4,)),
                dma((5, 3)), dma((5, 3)), dma((11,)), dma((11,)), dma((5,)), dma((5,)),
                dma((2,)), dma((2,)),
                dma((2, heads - 1)), dma((2, heads - 1)),
            ],
            compiler_params=pltpu.CompilerParams(
                collective_id=0, has_side_effects=True, vmem_limit_bytes=55040 * 1024
            ),
            cost_estimate=pl.CostEstimate(
                flops=2_000_000_000, bytes_accessed=1_200_000, transcendentals=1_600_000
            ),
        )(q, k, v, w)

    placed = (P("seq", "head"), P("seq", "head"), P("seq", "head"), P("head", None))
    return jax.shard_map(
        shards, mesh=mesh, in_specs=placed, out_specs=P("head", "seq"), check_vma=False
    )
```

```python
import functools

import jax
import jax.numpy as jnp
from jax import lax
from jax.experimental import pallas as pl
from jax.experimental.pallas import tpu as pltpu
from jax.sharding import PartitionSpec as P

HEAD_DIM = 64
BLOCK = 128
LEVELS = 6
HALF = BLOCK // 2
F32 = jnp.float32
BF16 = jnp.bfloat16
MESH = pl.DeviceIdType.MESH
FAR = (3, 4, 5, 6)
OFF = -1e30
EARLY = 8


def dot(a, b):
    return jnp.dot(a, b, preferred_element_type=F32)


def iota(shape, dim):
    return lax.broadcasted_iota(jnp.int32, shape, dim)


def pool(rows, fine, level, repeat):
    r, c = iota((rows, fine), 0), iota((rows, fine), 1)
    hit = (c >> level) == (r & (repeat - 1))
    return jnp.where(hit, 2.0**-level, 0.0).astype(BF16)


def unpack(n):
    r, c = iota((256, 256), 0), iota((256, 256), 1)
    group, inside = r >> 6, r & 63
    source, row = inside // n, inside & (n - 1)
    return jnp.where(c == source * (4 * n) + group * n + row, 1.0, 0.0).astype(BF16)


def scores_top(s, slabs):
    top = None
    for start, rows, bias in slabs:
        m = jnp.max(s[start : start + rows], axis=0, keepdims=True)
        if bias is not None:
            m = m + bias
        top = m if top is None else jnp.maximum(top, m)
    return top


def attend(k, vt, q, slabs):
    s = dot(k, q)
    top = scores_top(s, slabs)
    parts, total = [], None
    for start, rows, bias in slabs:
        shift = top if bias is None else top - bias
        p = jnp.exp(s[start : start + rows] - shift)
        t = jnp.sum(p, axis=0, keepdims=True)
        total = t if total is None else total + t
        parts.append(p.astype(BF16))
    o = dot(vt, jnp.concatenate(parts, 0))
    o = jnp.concatenate([o[:HEAD_DIM, :BLOCK], o[HEAD_DIM:, BLOCK:]], 1)
    return top, total, o


def merge(a, b):
    top = jnp.maximum(a[0], b[0])
    fa, fb = jnp.exp(a[0] - top), jnp.exp(b[0] - top)
    return top, a[1] * fa + b[1] * fb, a[2] * fa + b[2] * fb


def kernel(
    devices, heads,
    q_hbm, k_hbm, v_hbm, w_hbm, out_ref,
    q_ref, k_ref, v_ref, w_ref, rim, near, g2, g3, g4, g5, g6, s2, s3, s4, s5, s6,
    qbd, kb, vbt, kc, vct, wt, own_part, part, got, st_m, st_l, st_o, grants, in_s,
    p1_s, p1_r, p2_s, p2_r, p3_s, p3_r, near_s, near_r, part_s, part_r,
):
    d = lax.axis_index("seq")
    x = lax.axis_index("head")
    core = d % 2
    gathers = {3: g3, 4: g4, 5: g5, 6: g6}
    stages = {2: s2, 3: s3, 4: s4, 5: s5, 6: s6}

    def seq(steps):
        return (d + steps + 2 * devices) % devices

    def group(level):
        return 2 ** (level - 2)

    def far_steps(level, p):
        g = group(level)
        if p == 0:
            return 2 * g
        if p == 1:
            return -2 * g
        return (3 - 6 * ((d // g) % 2)) * g

    def remote(src, dst, send, recv, axis, target):
        return pltpu.make_async_remote_copy(
            src_ref=src, dst_ref=dst, send_sem=send, recv_sem=recv,
            device_id={axis: target}, device_id_type=MESH,
        )

    def far_target(level, p):
        target = seq(far_steps(level, p))
        if level == 4 and p == 2:
            target = target + 2 - 4 * ((target // 2) % 2)
        return target

    def phase1(level, p):
        at = (level - 2, p)
        rank = (d % group(level)) // 2
        if level == 2:
            dst = g2.at[p]
        elif level == 4 and p == 2:
            dst = g4.at[1 - rank, core, p]
        else:
            dst = gathers[level].at[rank, core, p]
        return remote(stages[level], dst, p1_s.at[at], p1_r.at[at], "seq", far_target(level, p))

    def phase2_target(level, j):
        chips = group(level) // 2
        mine = (d // 2) % chips
        return d - 2 * mine + 2 * ((mine + j) % chips)

    def phase2(level, j):
        slot = {4: 0, 5: 1, 6: 4}[level] + j - 1
        block = gathers[level].at[(d // 2) % (group(level) // 2), core]
        return remote(block, block, p2_s.at[slot], p2_r.at[slot], "seq", phase2_target(level, j))

    def phase3(level):
        if level == 2:
            src, dst = g2.at[core], g2.at[2]
        else:
            src = dst = gathers[level].at[:, core]
        slot = level - 2
        return remote(src, dst, p3_s.at[slot], p3_r.at[slot], "seq", d + 1 - 2 * core)

    def neighbour(up):
        side = 0 if up else 1
        return remote(
            rim.at[side], near.at[side], near_s.at[side], near_r.at[side], "seq", seq(1 if up else -1)
        )

    def share(b, t):
        at = (b, t - 1)
        return remote(part.at[b, t - 1], got.at[t - 1, b], part_s.at[at], part_r.at[at], "head", (x + t) % heads)

    all1 = [(level, p) for level in (6, 5, 4, 3, 2) for p in range(3 if level > 2 else 2)]
    all2 = [(level, j) for level in (4, 5, 6) for j in range(1, group(level) // 2)]

    def pass_on(level):
        for other, j in all2:
            if other == level:
                phase2(level, j).start()

    def passed(level):
        for other, j in all2:
            if other == level:
                phase2(level, j).wait_recv()

    back = (1, 0, 2)
    relations = {}
    for level, p in all1:
        there = d // group(level) + far_steps(level, p) // group(level)
        inside = (there >= 0) & (there < devices // group(level))
        relations["far", level, p] = ("seq", far_target(level, p), ("far", level, back[p]), inside)
    for up in (True, False):
        inside = d < devices - 1 if up else d > 0
        relations["near", up] = ("seq", seq(1 if up else -1), ("near", not up), inside)
    for j in range(1, 8):
        relations["mate", j] = ("seq", phase2_target(6, j), ("mate", 8 - j), True)
    for t in range(1, heads):
        relations["head", t] = ("head", (x + t) % heads, ("head", heads - t), True)
    slots = {name: i for i, name in enumerate(relations)}
    inside = {name: relation[3] for name, relation in relations.items()}
    above, below = {}, {}
    for name, (axis, target, _, valid) in relations.items():
        here = d if axis == "seq" else x
        above[name] = (target > here) & valid
        below[name] = (target < here) & valid

    def on(condition, *steps):
        @pl.when(condition)
        def _():
            for step in steps:
                step()

    def signal(semaphore, name):
        axis, target = relations[name][:2]
        pl.semaphore_signal(semaphore, inc=1, device_id={axis: target}, device_id_type=MESH)

    def granted(name, *steps):
        on(above[name], lambda: pl.semaphore_wait(grants.at[slots[name]], 1), *steps)

    def send_above(level, p):
        granted(("far", level, p), lambda: phase1(level, p).start())

    def arrived(level, p):
        on(inside["far", level, back[p]], lambda: phase1(level, p).wait_recv())

    loads = [
        pltpu.make_async_copy(src, dst, in_s.at[i])
        for i, (src, dst) in enumerate(
            [(k_hbm, k_ref), (v_hbm, v_ref), (q_hbm, q_ref), (w_hbm, w_ref)]
        )
    ]
    loads[0].start()
    loads[1].start()
    barrier = pltpu.get_barrier_semaphore()
    for name in relations:
        on(above[name], lambda: signal(barrier, name))
    loads[2].start()
    loads[3].start()
    count = sum(jnp.where(below[name], 1, 0) for name in relations)
    on(count > 0, lambda: pl.semaphore_wait(barrier, count))
    for name in relations:
        on(below[name], lambda: signal(grants.at[slots[relations[name][2]]], name))

    pools = jnp.concatenate(
        [pool(BLOCK, 256, 1, 128), pool(64, 256, 2, 64), pool(32, 256, 3, 32), pool(16, 256, 4, 16),
         pool(32, 256, 5, 8), pool(16, 256, 6, 4)], 0)
    loads[0].wait()
    loads[1].wait()
    k, v = k_ref[...], v_ref[...]
    ck, cv = dot(pools, k), dot(pools, v)
    blocks = [ck[:, :128], ck[:, 128:], cv[:, :128], cv[:, 128:]]
    for level, start, n in ((2, 128, 64), (3, 192, 32), (4, 224, 16)):
        for c in range(4):
            stages[level][c * n : (c + 1) * n, :] = blocks[c][start : start + n].astype(BF16)
    for level, start, n in ((5, 240, 8), (6, 272, 4)):
        owner = iota((4 * n, 128), 0) // n
        packed = blocks[0][start : start + 4 * n]
        for c in range(1, 4):
            packed = jnp.where(owner == c, blocks[c][start : start + 4 * n], packed)
        stages[level][...] = packed.astype(BF16)
    fine = [k[:, :128], k[:, 128:], v[:, :128], v[:, 128:]]
    for side in range(2):
        edge = BLOCK * (1 - side)
        for c in range(4):
            rim[side, c * BLOCK : (c + 1) * BLOCK, :] = fine[c][edge : edge + BLOCK]
            rim[side, 512 + c * HALF : 512 + (c + 1) * HALF, :] = blocks[c][side * HALF : (side + 1) * HALF].astype(BF16)

    for level, p in all1:
        on(below["far", level, p], lambda: phase1(level, p).start())
    on(below["near", False], lambda: neighbour(False).start())

    def clear(ref):
        ref[...] = jnp.zeros(ref.shape, ref.dtype)

    for level, p in all1:
        slot = g2.at[p] if level == 2 else gathers[level].at[(d % group(level)) // 2, core, p]
        on(jnp.logical_not(inside["far", level, back[p]]), lambda: clear(slot))
    on(d == 0, lambda: clear(near.at[0]))
    on(d == devices - 1, lambda: clear(near.at[1]))
    granted(("near", True), lambda: neighbour(True).start())

    loads[2].wait()
    qt = (q_ref[...].astype(F32) * HEAD_DIM**-0.5).T
    feature = iota((BLOCK, BLOCK), 0)
    for b in range(2):
        for hp in range(2):
            piece = qt[hp * BLOCK : (hp + 1) * BLOCK, b * BLOCK : (b + 1) * BLOCK]
            low = jnp.where(feature < HEAD_DIM, piece, 0.0)
            high = jnp.where(feature < HEAD_DIM, 0.0, piece)
            qbd[b, hp] = jnp.concatenate([low, high], 1).astype(BF16)

    def keep(u, state):
        st_m[u, 0:1, :], st_l[u, 0:1, :], st_o[u] = state

    def kept(u):
        return st_m[u, 0:1, :], st_l[u, 0:1, :], st_o[u]

    units = [(b, hp) for b in range(2) for hp in range(2)]
    for hp in range(2):
        lanes = slice(hp * BLOCK, (hp + 1) * BLOCK)
        vt = v_ref[:, lanes].T
        kk = k_ref[:, lanes]
        for b in range(2):
            keep(b * 2 + hp, attend(kk, vt, qbd[b, hp], [(0, 256, None)]))

    loads[3].wait()
    for i in range(heads):
        wt[i] = w_ref[:, i * 256 : (i + 1) * 256].T

    def exchange(level):
        for p in range(3 if level > 2 else 2):
            send_above(level, p)

    def gathered(level):
        for p in range(3 if level > 2 else 2):
            arrived(level, p)

    late = d // 8 >= EARLY

    def exchange_if(level, condition):
        for p in range(3):
            name = ("far", level, p)
            on(
                above[name] & condition,
                lambda: pl.semaphore_wait(grants.at[slots[name]], 1),
                lambda: phase1(level, p).start(),
            )

    for level in (2, 3, 4):
        exchange(level)
    exchange_if(5, late)
    exchange_if(6, late)
    for j in range(1, 8):
        granted(("mate", j))

    gathered(2)
    phase3(2).start()
    gathered(3)
    phase3(3).start()
    gathered(4)
    pass_on(4)
    on(inside["near", False], lambda: neighbour(True).wait_recv())
    on(inside["near", True], lambda: neighbour(False).wait_recv())
    half_pool = pool(HALF, BLOCK, 1, HALF)
    lower_ok = jnp.where(d > 0, 0.0, OFF).astype(F32)
    upper_ok = jnp.where(d < devices - 1, 0.0, OFF).astype(F32)

    def far_bias(level):
        g, out = group(level), []
        e, last = d // g, devices // g - 1
        steps = (-2, 2, 3 - 6 * (e % 2))
        for step in steps:
            there = e + step
            out.append(jnp.where((there >= 0) & (there <= last), 0.0, OFF).astype(F32))
        return out

    bias2 = far_bias(2)
    phase3(2).wait_recv()
    for c in range(4):
        kind, hp = c // 2, c % 2
        strip = slice(c * BLOCK, (c + 1) * BLOCK)
        rows = slice(c * HALF, (c + 1) * HALF)
        half = slice(512 + c * HALF, 512 + (c + 1) * HALF)
        pooled = [dot(half_pool, near[side, strip, :]).astype(BF16) for side in range(2)]
        common = [near[0, half, :], near[1, half, :]] + [g2[p, rows, :] for p in range(3)]
        for b in range(2):
            full = jnp.concatenate([near[b, strip, :], pooled[1 - b]] + common, 0)
            if kind == 0:
                kb[b, hp] = full
            else:
                vbt[b, hp] = full.T
    for b, hp in units:
        first, second = (lower_ok, upper_ok) if b == 0 else (upper_ok, lower_ok)
        slabs = [(0, 128, first), (128, 64, second), (192, 64, lower_ok), (256, 64, upper_ok)]
        slabs += [(320 + 64 * p, 64, bias2[p]) for p in range(3)]
        u = b * 2 + hp
        keep(u, merge(kept(u), attend(kb[b, hp], vbt[b, hp], qbd[b, hp], slabs)))
        if u == 1:
            passed(4)
            phase3(4).start()
            exchange_if(5, jnp.logical_not(late))
            gathered(5)
            pass_on(5)
    exchange_if(6, jnp.logical_not(late))
    gathered(6)
    pass_on(6)
    passed(5)
    phase3(5).start()

    def far_chunk(i):
        slabs, keys, values = [], ([], []), ([], [])
        for level in FAR[2 * i : 2 * i + 2]:
            phase3(level).wait_recv()
            n = 256 // 2**level
            g = group(level)
            for p, bias in enumerate(far_bias(level)):
                slabs.append((64 * len(slabs), 64, bias))
                whole = gathers[level][:, :, p].reshape(g, 4 * n, 128)
                if n >= 16:
                    four = [whole[:, c * n : (c + 1) * n, :].reshape(64, 128) for c in range(4)]
                else:
                    moved = dot(unpack(n), whole.reshape(256, 128)).astype(BF16)
                    four = [moved[c * 64 : (c + 1) * 64] for c in range(4)]
                for hp in range(2):
                    keys[hp].append(four[hp])
                    values[hp].append(four[2 + hp])
        for hp in range(2):
            kc[i, hp] = jnp.concatenate(keys[hp], 0)
            vct[i, hp] = jnp.concatenate(values[hp], 0).T
        return slabs

    slabs = far_chunk(0)
    for b, hp in units:
        u = b * 2 + hp
        keep(u, merge(kept(u), attend(kc[0, hp], vct[0, hp], qbd[b, hp], slabs)))
        if u == 1:
            passed(6)
            phase3(6).start()
    for t in range(1, heads):
        granted(("head", t))
    slabs = far_chunk(1)
    for b, hp in units:
        u = b * 2 + hp
        _, total, o = merge(kept(u), attend(kc[1, hp], vct[1, hp], qbd[b, hp], slabs))
        o = (o / total).astype(BF16)
        rows = jnp.concatenate([o[:, :BLOCK], o[:, BLOCK:]], 0)
        if hp == 0:
            upper = rows
            continue
        attended = jnp.concatenate([upper, rows], 0)
        for t in (2, 1, 3):
            part[b, t - 1] = dot(wt[(x + t) % heads], attended).astype(BF16)
            share(b, t).start()
        own_part[b] = dot(wt[x], attended)

    for level, p in all1:
        on(inside["far", level, p], lambda: phase1(level, p).wait_send())
    for level, j in all2:
        phase2(level, j).wait_send()
    for level in (2,) + FAR:
        phase3(level).wait_send()
    for up in (True, False):
        on(inside["near", up], lambda: neighbour(up).wait_send())

    for b in range(2):
        total = own_part[b]
        for t in (1, 3, 2):
            share(b, t).wait_recv()
            total = total + got[t - 1, b].astype(F32)
        out_ref[:, b * BLOCK : (b + 1) * BLOCK] = total.astype(BF16)

    for b in range(2):
        for t in range(1, heads):
            share(b, t).wait_send()


def solution(mesh):
    devices, heads = mesh.shape["seq"], mesh.shape["head"]

    def shards(q, k, v, w):
        rows, width = q.shape
        lanes = w.shape[1] // heads
        vmem = pl.BlockSpec(memory_space=pltpu.VMEM)
        dma = pltpu.SemaphoreType.DMA

        def gather(level):
            return pltpu.VMEM((2 ** (level - 3), 2, 3, 4 * (rows >> level), 128), BF16)

        def stage(level):
            return pltpu.VMEM((4 * (rows >> level), 128), BF16)

        return pl.pallas_call(
            functools.partial(kernel, devices, heads),
            out_shape=jax.ShapeDtypeStruct((lanes, rows), BF16),
            in_specs=[pl.BlockSpec(memory_space=pltpu.HBM)] * 4,
            out_specs=vmem,
            scratch_shapes=[
                pltpu.VMEM((rows, width), BF16),
                pltpu.VMEM((rows, width), BF16),
                pltpu.VMEM((rows, width), BF16),
                pltpu.VMEM((width, heads * lanes), BF16),
                pltpu.VMEM((2, 4 * (BLOCK + HALF), 128), BF16),
                pltpu.VMEM((2, 4 * (BLOCK + HALF), 128), BF16),
                pltpu.VMEM((3, 4 * HALF, 128), BF16),
                gather(3), gather(4), gather(5), gather(6),
                stage(2), stage(3), stage(4), stage(5), stage(6),
                pltpu.VMEM((2, 2, 128, 256), BF16),
                pltpu.VMEM((2, 2, 512, 128), BF16),
                pltpu.VMEM((2, 2, 128, 512), BF16),
                pltpu.VMEM((2, 2, 384, 128), BF16),
                pltpu.VMEM((2, 2, 128, 384), BF16),
                pltpu.VMEM((heads, lanes, width), BF16),
                pltpu.VMEM((2, lanes, BLOCK), F32),
                pltpu.VMEM((2, heads - 1, lanes, BLOCK), BF16),
                pltpu.VMEM((heads - 1, 2, lanes, BLOCK), BF16),
                pltpu.VMEM((4, 8, 256), F32),
                pltpu.VMEM((4, 8, 256), F32),
                pltpu.VMEM((4, HEAD_DIM, 256), F32),
                pltpu.SemaphoreType.REGULAR((26,)),
                dma((4,)),
                dma((5, 3)), dma((5, 3)), dma((11,)), dma((11,)), dma((5,)), dma((5,)),
                dma((2,)), dma((2,)),
                dma((2, heads - 1)), dma((2, heads - 1)),
            ],
            compiler_params=pltpu.CompilerParams(
                collective_id=0, has_side_effects=True, vmem_limit_bytes=55040 * 1024
            ),
            cost_estimate=pl.CostEstimate(
                flops=2_000_000_000, bytes_accessed=1_200_000, transcendentals=1_600_000
            ),
        )(q, k, v, w)

    placed = (P("seq", "head"), P("seq", "head"), P("seq", "head"), P("head", None))
    return jax.shard_map(
        shards, mesh=mesh, in_specs=placed, out_specs=P("head", "seq"), check_vma=False
    )
```

```python
import functools

import jax
import jax.numpy as jnp
from jax import lax
from jax.experimental import pallas as pl
from jax.experimental.pallas import tpu as pltpu
from jax.sharding import PartitionSpec as P

HEAD_DIM = 64
BLOCK = 128
LEVELS = 6
HALF = BLOCK // 2
F32 = jnp.float32
BF16 = jnp.bfloat16
MESH = pl.DeviceIdType.MESH
FAR = (3, 4, 5, 6)
OFF = -1e30
MIDDLE, LATE = 4, 8


def dot(a, b):
    return jnp.dot(a, b, preferred_element_type=F32)


def iota(shape, dim):
    return lax.broadcasted_iota(jnp.int32, shape, dim)


def pool(rows, fine, level, repeat):
    r, c = iota((rows, fine), 0), iota((rows, fine), 1)
    hit = (c >> level) == (r & (repeat - 1))
    return jnp.where(hit, 2.0**-level, 0.0).astype(BF16)


def unpack(n):
    r, c = iota((256, 256), 0), iota((256, 256), 1)
    group, inside = r >> 6, r & 63
    source, row = inside // n, inside & (n - 1)
    return jnp.where(c == source * (4 * n) + group * n + row, 1.0, 0.0).astype(BF16)


def scores_top(s, slabs):
    top = None
    for start, rows, bias in slabs:
        m = jnp.max(s[start : start + rows], axis=0, keepdims=True)
        if bias is not None:
            m = m + bias
        top = m if top is None else jnp.maximum(top, m)
    return top


def attend(k, vt, q, slabs):
    s = dot(k, q)
    top = scores_top(s, slabs)
    parts, total = [], None
    for start, rows, bias in slabs:
        shift = top if bias is None else top - bias
        p = jnp.exp(s[start : start + rows] - shift)
        t = jnp.sum(p, axis=0, keepdims=True)
        total = t if total is None else total + t
        parts.append(p.astype(BF16))
    o = dot(vt, jnp.concatenate(parts, 0))
    o = jnp.concatenate([o[:HEAD_DIM, :BLOCK], o[HEAD_DIM:, BLOCK:]], 1)
    return top, total, o


def merge(a, b):
    top = jnp.maximum(a[0], b[0])
    fa, fb = jnp.exp(a[0] - top), jnp.exp(b[0] - top)
    return top, a[1] * fa + b[1] * fb, a[2] * fa + b[2] * fb


def kernel(
    devices, heads,
    q_hbm, k_hbm, v_hbm, w_hbm, out_ref,
    q_ref, k_ref, v_ref, w_ref, rim, near, g2, g3, g4, g5, g6, s2, s3, s4, s5, s6,
    qbd, kb, vbt, kc, vct, wt, own_part, part, got, st_m, st_l, st_o, grants, in_s,
    p1_s, p1_r, p2_s, p2_r, p3_s, p3_r, near_s, near_r, part_s, part_r,
):
    d = lax.axis_index("seq")
    x = lax.axis_index("head")
    core = d % 2
    gathers = {3: g3, 4: g4, 5: g5, 6: g6}
    stages = {2: s2, 3: s3, 4: s4, 5: s5, 6: s6}

    def seq(steps):
        return (d + steps + 2 * devices) % devices

    def group(level):
        return 2 ** (level - 2)

    def far_steps(level, p):
        g = group(level)
        if p == 0:
            return 2 * g
        if p == 1:
            return -2 * g
        return (3 - 6 * ((d // g) % 2)) * g

    def remote(src, dst, send, recv, axis, target):
        return pltpu.make_async_remote_copy(
            src_ref=src, dst_ref=dst, send_sem=send, recv_sem=recv,
            device_id={axis: target}, device_id_type=MESH,
        )

    def far_target(level, p):
        target = seq(far_steps(level, p))
        if level == 4 and p == 2:
            target = target + 2 - 4 * ((target // 2) % 2)
        return target

    def phase1(level, p):
        at = (level - 2, p)
        rank = (d % group(level)) // 2
        if level == 2:
            dst = g2.at[p]
        elif level == 4 and p == 2:
            dst = g4.at[1 - rank, core, p]
        else:
            dst = gathers[level].at[rank, core, p]
        return remote(stages[level], dst, p1_s.at[at], p1_r.at[at], "seq", far_target(level, p))

    def phase2_target(level, j):
        chips = group(level) // 2
        mine = (d // 2) % chips
        return d - 2 * mine + 2 * ((mine + j) % chips)

    def phase2(level, j):
        slot = {4: 0, 5: 1, 6: 4}[level] + j - 1
        block = gathers[level].at[(d // 2) % (group(level) // 2), core]
        return remote(block, block, p2_s.at[slot], p2_r.at[slot], "seq", phase2_target(level, j))

    def phase3(level):
        if level == 2:
            src, dst = g2.at[core], g2.at[2]
        else:
            src = dst = gathers[level].at[:, core]
        slot = level - 2
        return remote(src, dst, p3_s.at[slot], p3_r.at[slot], "seq", d + 1 - 2 * core)

    def neighbour(up):
        side = 0 if up else 1
        return remote(
            rim.at[side], near.at[side], near_s.at[side], near_r.at[side], "seq", seq(1 if up else -1)
        )

    def share(b, t):
        at = (b, t - 1)
        return remote(part.at[b, t - 1], got.at[t - 1, b], part_s.at[at], part_r.at[at], "head", (x + t) % heads)

    all1 = [(level, p) for level in (6, 5, 4, 3, 2) for p in range(3 if level > 2 else 2)]
    all2 = [(level, j) for level in (4, 5, 6) for j in range(1, group(level) // 2)]

    def pass_on(level):
        for other, j in all2:
            if other == level:
                phase2(level, j).start()

    def passed(level):
        for other, j in all2:
            if other == level:
                phase2(level, j).wait_recv()

    back = (1, 0, 2)
    relations = {}
    for level, p in all1:
        there = d // group(level) + far_steps(level, p) // group(level)
        inside = (there >= 0) & (there < devices // group(level))
        relations["far", level, p] = ("seq", far_target(level, p), ("far", level, back[p]), inside)
    for up in (True, False):
        inside = d < devices - 1 if up else d > 0
        relations["near", up] = ("seq", seq(1 if up else -1), ("near", not up), inside)
    for j in range(1, 8):
        relations["mate", j] = ("seq", phase2_target(6, j), ("mate", 8 - j), True)
    for t in range(1, heads):
        relations["head", t] = ("head", (x + t) % heads, ("head", heads - t), True)
    slots = {name: i for i, name in enumerate(relations)}
    inside = {name: relation[3] for name, relation in relations.items()}
    above, below = {}, {}
    for name, (axis, target, _, valid) in relations.items():
        here = d if axis == "seq" else x
        above[name] = (target > here) & valid
        below[name] = (target < here) & valid

    def on(condition, *steps):
        @pl.when(condition)
        def _():
            for step in steps:
                step()

    def signal(semaphore, name):
        axis, target = relations[name][:2]
        pl.semaphore_signal(semaphore, inc=1, device_id={axis: target}, device_id_type=MESH)

    def granted(name, *steps):
        on(above[name], lambda: pl.semaphore_wait(grants.at[slots[name]], 1), *steps)

    def arrived(level, p):
        on(inside["far", level, back[p]], lambda: phase1(level, p).wait_recv())

    loads = [
        pltpu.make_async_copy(src, dst, in_s.at[i])
        for i, (src, dst) in enumerate(
            [(k_hbm, k_ref), (v_hbm, v_ref), (q_hbm, q_ref), (w_hbm, w_ref)]
        )
    ]
    loads[0].start()
    loads[1].start()
    barrier = pltpu.get_barrier_semaphore()
    for name in relations:
        on(above[name], lambda: signal(barrier, name))
    loads[2].start()
    loads[3].start()
    count = sum(jnp.where(below[name], 1, 0) for name in relations)
    on(count > 0, lambda: pl.semaphore_wait(barrier, count))
    for name in relations:
        on(below[name], lambda: signal(grants.at[slots[relations[name][2]]], name))

    pools = jnp.concatenate(
        [pool(BLOCK, 256, 1, 128), pool(64, 256, 2, 64), pool(32, 256, 3, 32), pool(16, 256, 4, 16),
         pool(32, 256, 5, 8), pool(16, 256, 6, 4)], 0)
    loads[0].wait()
    loads[1].wait()
    k, v = k_ref[...], v_ref[...]
    ck, cv = dot(pools, k), dot(pools, v)
    blocks = [ck[:, :128], ck[:, 128:], cv[:, :128], cv[:, 128:]]
    for level, start, n in ((2, 128, 64), (3, 192, 32), (4, 224, 16)):
        for c in range(4):
            stages[level][c * n : (c + 1) * n, :] = blocks[c][start : start + n].astype(BF16)
    for level, start, n in ((5, 240, 8), (6, 272, 4)):
        owner = iota((4 * n, 128), 0) // n
        packed = blocks[0][start : start + 4 * n]
        for c in range(1, 4):
            packed = jnp.where(owner == c, blocks[c][start : start + 4 * n], packed)
        stages[level][...] = packed.astype(BF16)
    fine = [k[:, :128], k[:, 128:], v[:, :128], v[:, 128:]]
    for side in range(2):
        edge = BLOCK * (1 - side)
        for c in range(4):
            rim[side, c * BLOCK : (c + 1) * BLOCK, :] = fine[c][edge : edge + BLOCK]
            rim[side, 512 + c * HALF : 512 + (c + 1) * HALF, :] = blocks[c][side * HALF : (side + 1) * HALF].astype(BF16)

    for level, p in all1:
        on(below["far", level, p], lambda: phase1(level, p).start())
    on(below["near", False], lambda: neighbour(False).start())

    def clear(ref):
        ref[...] = jnp.zeros(ref.shape, ref.dtype)

    for level, p in all1:
        slot = g2.at[p] if level == 2 else gathers[level].at[(d % group(level)) // 2, core, p]
        on(jnp.logical_not(inside["far", level, back[p]]), lambda: clear(slot))
    on(d == 0, lambda: clear(near.at[0]))
    on(d == devices - 1, lambda: clear(near.at[1]))
    granted(("near", True), lambda: neighbour(True).start())

    plane = d // 8
    soon, middle, last = plane < MIDDLE, (plane >= MIDDLE) & (plane < LATE), plane >= LATE

    def exchange_if(level, condition):
        for p in range(3 if level > 2 else 2):
            name = ("far", level, p)
            on(
                above[name] & condition,
                lambda: pl.semaphore_wait(grants.at[slots[name]], 1),
                lambda: phase1(level, p).start(),
            )

    for level in (6, 5, 4, 3, 2):
        exchange_if(level, last)

    loads[2].wait()
    qt = (q_ref[...].astype(F32) * HEAD_DIM**-0.5).T
    feature = iota((BLOCK, BLOCK), 0)
    for b in range(2):
        for hp in range(2):
            piece = qt[hp * BLOCK : (hp + 1) * BLOCK, b * BLOCK : (b + 1) * BLOCK]
            low = jnp.where(feature < HEAD_DIM, piece, 0.0)
            high = jnp.where(feature < HEAD_DIM, 0.0, piece)
            qbd[b, hp] = jnp.concatenate([low, high], 1).astype(BF16)

    def keep(u, state):
        st_m[u, 0:1, :], st_l[u, 0:1, :], st_o[u] = state

    def kept(u):
        return st_m[u, 0:1, :], st_l[u, 0:1, :], st_o[u]

    units = [(b, hp) for b in range(2) for hp in range(2)]
    for hp in range(2):
        lanes = slice(hp * BLOCK, (hp + 1) * BLOCK)
        vt = v_ref[:, lanes].T
        kk = k_ref[:, lanes]
        for b in range(2):
            keep(b * 2 + hp, attend(kk, vt, qbd[b, hp], [(0, 256, None)]))

    loads[3].wait()
    for i in range(heads):
        wt[i] = w_ref[:, i * 256 : (i + 1) * 256].T

    def gathered(level):
        for p in range(3 if level > 2 else 2):
            arrived(level, p)

    for level in (2, 3, 4):
        exchange_if(level, jnp.logical_not(last))
    exchange_if(5, middle)
    exchange_if(6, middle)
    for j in range(1, 8):
        granted(("mate", j))

    gathered(2)
    phase3(2).start()
    gathered(3)
    phase3(3).start()
    gathered(4)
    pass_on(4)
    on(inside["near", False], lambda: neighbour(True).wait_recv())
    on(inside["near", True], lambda: neighbour(False).wait_recv())
    half_pool = pool(HALF, BLOCK, 1, HALF)
    lower_ok = jnp.where(d > 0, 0.0, OFF).astype(F32)
    upper_ok = jnp.where(d < devices - 1, 0.0, OFF).astype(F32)

    def far_bias(level):
        g, out = group(level), []
        e, last = d // g, devices // g - 1
        steps = (-2, 2, 3 - 6 * (e % 2))
        for step in steps:
            there = e + step
            out.append(jnp.where((there >= 0) & (there <= last), 0.0, OFF).astype(F32))
        return out

    bias2 = far_bias(2)
    phase3(2).wait_recv()
    for c in range(4):
        kind, hp = c // 2, c % 2
        strip = slice(c * BLOCK, (c + 1) * BLOCK)
        rows = slice(c * HALF, (c + 1) * HALF)
        half = slice(512 + c * HALF, 512 + (c + 1) * HALF)
        pooled = [dot(half_pool, near[side, strip, :]).astype(BF16) for side in range(2)]
        common = [near[0, half, :], near[1, half, :]] + [g2[p, rows, :] for p in range(3)]
        for b in range(2):
            full = jnp.concatenate([near[b, strip, :], pooled[1 - b]] + common, 0)
            if kind == 0:
                kb[b, hp] = full
            else:
                vbt[b, hp] = full.T
    for b, hp in units:
        first, second = (lower_ok, upper_ok) if b == 0 else (upper_ok, lower_ok)
        slabs = [(0, 128, first), (128, 64, second), (192, 64, lower_ok), (256, 64, upper_ok)]
        slabs += [(320 + 64 * p, 64, bias2[p]) for p in range(3)]
        u = b * 2 + hp
        keep(u, merge(kept(u), attend(kb[b, hp], vbt[b, hp], qbd[b, hp], slabs)))
        if u == 1:
            passed(4)
            phase3(4).start()
            exchange_if(5, soon)
            gathered(5)
            pass_on(5)
    exchange_if(6, soon)
    gathered(6)
    pass_on(6)
    passed(5)
    phase3(5).start()

    def far_chunk(i):
        slabs, keys, values = [], ([], []), ([], [])
        for level in FAR[2 * i : 2 * i + 2]:
            phase3(level).wait_recv()
            n = 256 // 2**level
            g = group(level)
            for p, bias in enumerate(far_bias(level)):
                slabs.append((64 * len(slabs), 64, bias))
                whole = gathers[level][:, :, p].reshape(g, 4 * n, 128)
                if n >= 16:
                    four = [whole[:, c * n : (c + 1) * n, :].reshape(64, 128) for c in range(4)]
                else:
                    moved = dot(unpack(n), whole.reshape(256, 128)).astype(BF16)
                    four = [moved[c * 64 : (c + 1) * 64] for c in range(4)]
                for hp in range(2):
                    keys[hp].append(four[hp])
                    values[hp].append(four[2 + hp])
        for hp in range(2):
            kc[i, hp] = jnp.concatenate(keys[hp], 0)
            vct[i, hp] = jnp.concatenate(values[hp], 0).T
        return slabs

    slabs = far_chunk(0)
    for b, hp in units:
        u = b * 2 + hp
        keep(u, merge(kept(u), attend(kc[0, hp], vct[0, hp], qbd[b, hp], slabs)))
        if u == 1:
            passed(6)
            phase3(6).start()
    for t in range(1, heads):
        granted(("head", t))
    slabs = far_chunk(1)
    for b, hp in units:
        u = b * 2 + hp
        _, total, o = merge(kept(u), attend(kc[1, hp], vct[1, hp], qbd[b, hp], slabs))
        o = (o / total).astype(BF16)
        rows = jnp.concatenate([o[:, :BLOCK], o[:, BLOCK:]], 0)
        if hp == 0:
            upper = rows
            continue
        attended = jnp.concatenate([upper, rows], 0)
        for t in (2, 1, 3):
            part[b, t - 1] = dot(wt[(x + t) % heads], attended).astype(BF16)
            share(b, t).start()
        own_part[b] = dot(wt[x], attended)

    for level, p in all1:
        on(inside["far", level, p], lambda: phase1(level, p).wait_send())
    for level, j in all2:
        phase2(level, j).wait_send()
    for level in (2,) + FAR:
        phase3(level).wait_send()
    for up in (True, False):
        on(inside["near", up], lambda: neighbour(up).wait_send())

    for b in range(2):
        total = own_part[b]
        for t in (1, 3, 2):
            share(b, t).wait_recv()
            total = total + got[t - 1, b].astype(F32)
        out_ref[:, b * BLOCK : (b + 1) * BLOCK] = total.astype(BF16)

    for b in range(2):
        for t in range(1, heads):
            share(b, t).wait_send()


def solution(mesh):
    devices, heads = mesh.shape["seq"], mesh.shape["head"]

    def shards(q, k, v, w):
        rows, width = q.shape
        lanes = w.shape[1] // heads
        vmem = pl.BlockSpec(memory_space=pltpu.VMEM)
        dma = pltpu.SemaphoreType.DMA

        def gather(level):
            return pltpu.VMEM((2 ** (level - 3), 2, 3, 4 * (rows >> level), 128), BF16)

        def stage(level):
            return pltpu.VMEM((4 * (rows >> level), 128), BF16)

        return pl.pallas_call(
            functools.partial(kernel, devices, heads),
            out_shape=jax.ShapeDtypeStruct((lanes, rows), BF16),
            in_specs=[pl.BlockSpec(memory_space=pltpu.HBM)] * 4,
            out_specs=vmem,
            scratch_shapes=[
                pltpu.VMEM((rows, width), BF16),
                pltpu.VMEM((rows, width), BF16),
                pltpu.VMEM((rows, width), BF16),
                pltpu.VMEM((width, heads * lanes), BF16),
                pltpu.VMEM((2, 4 * (BLOCK + HALF), 128), BF16),
                pltpu.VMEM((2, 4 * (BLOCK + HALF), 128), BF16),
                pltpu.VMEM((3, 4 * HALF, 128), BF16),
                gather(3), gather(4), gather(5), gather(6),
                stage(2), stage(3), stage(4), stage(5), stage(6),
                pltpu.VMEM((2, 2, 128, 256), BF16),
                pltpu.VMEM((2, 2, 512, 128), BF16),
                pltpu.VMEM((2, 2, 128, 512), BF16),
                pltpu.VMEM((2, 2, 384, 128), BF16),
                pltpu.VMEM((2, 2, 128, 384), BF16),
                pltpu.VMEM((heads, lanes, width), BF16),
                pltpu.VMEM((2, lanes, BLOCK), F32),
                pltpu.VMEM((2, heads - 1, lanes, BLOCK), BF16),
                pltpu.VMEM((heads - 1, 2, lanes, BLOCK), BF16),
                pltpu.VMEM((4, 8, 256), F32),
                pltpu.VMEM((4, 8, 256), F32),
                pltpu.VMEM((4, HEAD_DIM, 256), F32),
                pltpu.SemaphoreType.REGULAR((26,)),
                dma((4,)),
                dma((5, 3)), dma((5, 3)), dma((11,)), dma((11,)), dma((5,)), dma((5,)),
                dma((2,)), dma((2,)),
                dma((2, heads - 1)), dma((2, heads - 1)),
            ],
            compiler_params=pltpu.CompilerParams(
                collective_id=0, has_side_effects=True, vmem_limit_bytes=55040 * 1024
            ),
            cost_estimate=pl.CostEstimate(
                flops=2_000_000_000, bytes_accessed=1_200_000, transcendentals=1_600_000
            ),
        )(q, k, v, w)

    placed = (P("seq", "head"), P("seq", "head"), P("seq", "head"), P("head", None))
    return jax.shard_map(
        shards, mesh=mesh, in_specs=placed, out_specs=P("head", "seq"), check_vma=False
    )
```

```python
import functools

import jax
import jax.numpy as jnp
from jax import lax
from jax.experimental import pallas as pl
from jax.experimental.pallas import tpu as pltpu
from jax.sharding import PartitionSpec as P

HEAD_DIM = 64
BLOCK = 128
LEVELS = 6
HALF = BLOCK // 2
F32 = jnp.float32
BF16 = jnp.bfloat16
MESH = pl.DeviceIdType.MESH
FAR = (3, 4, 5, 6)
OFF = -1e30
MIDDLE, LATE = 6, 8


def dot(a, b):
    return jnp.dot(a, b, preferred_element_type=F32)


def iota(shape, dim):
    return lax.broadcasted_iota(jnp.int32, shape, dim)


def pool(rows, fine, level, repeat):
    r, c = iota((rows, fine), 0), iota((rows, fine), 1)
    hit = (c >> level) == (r & (repeat - 1))
    return jnp.where(hit, 2.0**-level, 0.0).astype(BF16)


def unpack(n):
    r, c = iota((256, 256), 0), iota((256, 256), 1)
    group, inside = r >> 6, r & 63
    source, row = inside // n, inside & (n - 1)
    return jnp.where(c == source * (4 * n) + group * n + row, 1.0, 0.0).astype(BF16)


def scores_top(s, slabs):
    top = None
    for start, rows, bias in slabs:
        m = jnp.max(s[start : start + rows], axis=0, keepdims=True)
        if bias is not None:
            m = m + bias
        top = m if top is None else jnp.maximum(top, m)
    return top


def attend(k, vt, q, slabs):
    s = dot(k, q)
    top = scores_top(s, slabs)
    parts, total = [], None
    for start, rows, bias in slabs:
        shift = top if bias is None else top - bias
        p = jnp.exp(s[start : start + rows] - shift)
        t = jnp.sum(p, axis=0, keepdims=True)
        total = t if total is None else total + t
        parts.append(p.astype(BF16))
    o = dot(vt, jnp.concatenate(parts, 0))
    o = jnp.concatenate([o[:HEAD_DIM, :BLOCK], o[HEAD_DIM:, BLOCK:]], 1)
    return top, total, o


def merge(a, b):
    top = jnp.maximum(a[0], b[0])
    fa, fb = jnp.exp(a[0] - top), jnp.exp(b[0] - top)
    return top, a[1] * fa + b[1] * fb, a[2] * fa + b[2] * fb


def kernel(
    devices, heads,
    q_hbm, k_hbm, v_hbm, w_hbm, out_ref,
    q_ref, k_ref, v_ref, w_ref, rim, near, g2, g3, g4, g5, g6, s2, s3, s4, s5, s6,
    qbd, kb, vbt, kc, vct, kd, vdt, wt, own_part, part, got, st_m, st_l, st_o, grants, in_s,
    p1_s, p1_r, p2_s, p2_r, p3_s, p3_r, near_s, near_r, part_s, part_r,
):
    d = lax.axis_index("seq")
    x = lax.axis_index("head")
    core = d % 2
    gathers = {3: g3, 4: g4, 5: g5, 6: g6}
    stages = {2: s2, 3: s3, 4: s4, 5: s5, 6: s6}

    def seq(steps):
        return (d + steps + 2 * devices) % devices

    def group(level):
        return 2 ** (level - 2)

    def far_steps(level, p):
        g = group(level)
        if p == 0:
            return 2 * g
        if p == 1:
            return -2 * g
        return (3 - 6 * ((d // g) % 2)) * g

    def remote(src, dst, send, recv, axis, target):
        return pltpu.make_async_remote_copy(
            src_ref=src, dst_ref=dst, send_sem=send, recv_sem=recv,
            device_id={axis: target}, device_id_type=MESH,
        )

    def far_target(level, p):
        target = seq(far_steps(level, p))
        if level == 4 and p == 2:
            target = target + 2 - 4 * ((target // 2) % 2)
        return target

    def phase1(level, p):
        at = (level - 2, p)
        rank = (d % group(level)) // 2
        if level == 2:
            dst = g2.at[p]
        elif level == 4 and p == 2:
            dst = g4.at[1 - rank, core, p]
        else:
            dst = gathers[level].at[rank, core, p]
        return remote(stages[level], dst, p1_s.at[at], p1_r.at[at], "seq", far_target(level, p))

    def phase2_target(level, j):
        chips = group(level) // 2
        mine = (d // 2) % chips
        return d - 2 * mine + 2 * ((mine + j) % chips)

    def phase2(level, j):
        slot = {4: 0, 5: 1, 6: 4}[level] + j - 1
        block = gathers[level].at[(d // 2) % (group(level) // 2), core]
        return remote(block, block, p2_s.at[slot], p2_r.at[slot], "seq", phase2_target(level, j))

    def phase3(level):
        if level == 2:
            src, dst = g2.at[core], g2.at[2]
        else:
            src = dst = gathers[level].at[:, core]
        slot = level - 2
        return remote(src, dst, p3_s.at[slot], p3_r.at[slot], "seq", d + 1 - 2 * core)

    def neighbour(up):
        side = 0 if up else 1
        return remote(
            rim.at[side], near.at[side], near_s.at[side], near_r.at[side], "seq", seq(1 if up else -1)
        )

    def share(b, t):
        at = (b, t - 1)
        return remote(part.at[b, t - 1], got.at[t - 1, b], part_s.at[at], part_r.at[at], "head", (x + t) % heads)

    all1 = [(level, p) for level in (6, 5, 4, 3, 2) for p in range(3 if level > 2 else 2)]
    all2 = [(level, j) for level in (4, 5, 6) for j in range(1, group(level) // 2)]

    def pass_on(level):
        for other, j in all2:
            if other == level:
                phase2(level, j).start()

    def passed(level):
        for other, j in all2:
            if other == level:
                phase2(level, j).wait_recv()

    back = (1, 0, 2)
    relations = {}
    for level, p in all1:
        there = d // group(level) + far_steps(level, p) // group(level)
        inside = (there >= 0) & (there < devices // group(level))
        relations["far", level, p] = ("seq", far_target(level, p), ("far", level, back[p]), inside)
    for up in (True, False):
        inside = d < devices - 1 if up else d > 0
        relations["near", up] = ("seq", seq(1 if up else -1), ("near", not up), inside)
    for j in range(1, 8):
        relations["mate", j] = ("seq", phase2_target(6, j), ("mate", 8 - j), True)
    for t in range(1, heads):
        relations["head", t] = ("head", (x + t) % heads, ("head", heads - t), True)
    slots = {name: i for i, name in enumerate(relations)}
    inside = {name: relation[3] for name, relation in relations.items()}
    above, below = {}, {}
    for name, (axis, target, _, valid) in relations.items():
        here = d if axis == "seq" else x
        above[name] = (target > here) & valid
        below[name] = (target < here) & valid

    def on(condition, *steps):
        @pl.when(condition)
        def _():
            for step in steps:
                step()

    def signal(semaphore, name):
        axis, target = relations[name][:2]
        pl.semaphore_signal(semaphore, inc=1, device_id={axis: target}, device_id_type=MESH)

    def granted(name, *steps):
        on(above[name], lambda: pl.semaphore_wait(grants.at[slots[name]], 1), *steps)

    def arrived(level, p):
        on(inside["far", level, back[p]], lambda: phase1(level, p).wait_recv())

    loads = [
        pltpu.make_async_copy(src, dst, in_s.at[i])
        for i, (src, dst) in enumerate(
            [(k_hbm, k_ref), (v_hbm, v_ref), (q_hbm, q_ref), (w_hbm, w_ref)]
        )
    ]
    loads[0].start()
    loads[1].start()
    barrier = pltpu.get_barrier_semaphore()
    for name in relations:
        on(above[name], lambda: signal(barrier, name))
    loads[2].start()
    loads[3].start()
    count = sum(jnp.where(below[name], 1, 0) for name in relations)
    on(count > 0, lambda: pl.semaphore_wait(barrier, count))
    for name in relations:
        on(below[name], lambda: signal(grants.at[slots[relations[name][2]]], name))

    pools = jnp.concatenate(
        [pool(BLOCK, 256, 1, 128), pool(64, 256, 2, 64), pool(32, 256, 3, 32), pool(16, 256, 4, 16),
         pool(32, 256, 5, 8), pool(16, 256, 6, 4)], 0)
    loads[0].wait()
    loads[1].wait()
    k, v = k_ref[...], v_ref[...]
    ck, cv = dot(pools, k), dot(pools, v)
    blocks = [ck[:, :128], ck[:, 128:], cv[:, :128], cv[:, 128:]]
    for level, start, n in ((2, 128, 64), (3, 192, 32), (4, 224, 16)):
        for c in range(4):
            stages[level][c * n : (c + 1) * n, :] = blocks[c][start : start + n].astype(BF16)
    for level, start, n in ((5, 240, 8), (6, 272, 4)):
        owner = iota((4 * n, 128), 0) // n
        packed = blocks[0][start : start + 4 * n]
        for c in range(1, 4):
            packed = jnp.where(owner == c, blocks[c][start : start + 4 * n], packed)
        stages[level][...] = packed.astype(BF16)
    fine = [k[:, :128], k[:, 128:], v[:, :128], v[:, 128:]]
    for side in range(2):
        edge = BLOCK * (1 - side)
        for c in range(4):
            rim[side, c * BLOCK : (c + 1) * BLOCK, :] = fine[c][edge : edge + BLOCK]
            rim[side, 512 + c * HALF : 512 + (c + 1) * HALF, :] = blocks[c][side * HALF : (side + 1) * HALF].astype(BF16)

    for level, p in all1:
        on(below["far", level, p], lambda: phase1(level, p).start())
    on(below["near", False], lambda: neighbour(False).start())

    def clear(ref):
        ref[...] = jnp.zeros(ref.shape, ref.dtype)

    for level, p in all1:
        slot = g2.at[p] if level == 2 else gathers[level].at[(d % group(level)) // 2, core, p]
        on(jnp.logical_not(inside["far", level, back[p]]), lambda: clear(slot))
    on(d == 0, lambda: clear(near.at[0]))
    on(d == devices - 1, lambda: clear(near.at[1]))
    granted(("near", True), lambda: neighbour(True).start())

    plane = d // 8
    soon, middle, last = plane < MIDDLE, (plane >= MIDDLE) & (plane < LATE), plane >= LATE

    def exchange_if(level, condition):
        for p in range(3 if level > 2 else 2):
            name = ("far", level, p)
            on(
                above[name] & condition,
                lambda: pl.semaphore_wait(grants.at[slots[name]], 1),
                lambda: phase1(level, p).start(),
            )

    for level in (6, 5, 4, 3, 2):
        exchange_if(level, last)

    loads[2].wait()
    qt = (q_ref[...].astype(F32) * HEAD_DIM**-0.5).T
    feature = iota((BLOCK, BLOCK), 0)
    for b in range(2):
        for hp in range(2):
            piece = qt[hp * BLOCK : (hp + 1) * BLOCK, b * BLOCK : (b + 1) * BLOCK]
            low = jnp.where(feature < HEAD_DIM, piece, 0.0)
            high = jnp.where(feature < HEAD_DIM, 0.0, piece)
            qbd[b, hp] = jnp.concatenate([low, high], 1).astype(BF16)

    def keep(u, state):
        st_m[u, 0:1, :], st_l[u, 0:1, :], st_o[u] = state

    def kept(u):
        return st_m[u, 0:1, :], st_l[u, 0:1, :], st_o[u]

    units = [(b, hp) for b in range(2) for hp in range(2)]
    for hp in range(2):
        lanes = slice(hp * BLOCK, (hp + 1) * BLOCK)
        vt = v_ref[:, lanes].T
        kk = k_ref[:, lanes]
        for b in range(2):
            keep(b * 2 + hp, attend(kk, vt, qbd[b, hp], [(0, 256, None)]))

    loads[3].wait()
    for i in range(heads):
        wt[i] = w_ref[:, i * 256 : (i + 1) * 256].T

    def gathered(level):
        for p in range(3 if level > 2 else 2):
            arrived(level, p)

    for level in (2, 3, 4):
        exchange_if(level, jnp.logical_not(last))
    exchange_if(5, middle)
    exchange_if(6, middle)
    for j in range(1, 8):
        granted(("mate", j))

    gathered(2)
    phase3(2).start()
    gathered(3)
    phase3(3).start()
    gathered(4)
    pass_on(4)
    on(inside["near", False], lambda: neighbour(True).wait_recv())
    on(inside["near", True], lambda: neighbour(False).wait_recv())
    half_pool = pool(HALF, BLOCK, 1, HALF)
    lower_ok = jnp.where(d > 0, 0.0, OFF).astype(F32)
    upper_ok = jnp.where(d < devices - 1, 0.0, OFF).astype(F32)

    def far_bias(level):
        g, out = group(level), []
        e, last = d // g, devices // g - 1
        steps = (-2, 2, 3 - 6 * (e % 2))
        for step in steps:
            there = e + step
            out.append(jnp.where((there >= 0) & (there <= last), 0.0, OFF).astype(F32))
        return out

    bias2 = far_bias(2)
    phase3(2).wait_recv()
    for c in range(4):
        kind, hp = c // 2, c % 2
        strip = slice(c * BLOCK, (c + 1) * BLOCK)
        rows = slice(c * HALF, (c + 1) * HALF)
        half = slice(512 + c * HALF, 512 + (c + 1) * HALF)
        pooled = [dot(half_pool, near[side, strip, :]).astype(BF16) for side in range(2)]
        common = [near[0, half, :], near[1, half, :]] + [g2[p, rows, :] for p in range(3)]
        for b in range(2):
            full = jnp.concatenate([near[b, strip, :], pooled[1 - b]] + common, 0)
            if kind == 0:
                kb[b, hp] = full
            else:
                vbt[b, hp] = full.T
    for b, hp in units:
        first, second = (lower_ok, upper_ok) if b == 0 else (upper_ok, lower_ok)
        slabs = [(0, 128, first), (128, 64, second), (192, 64, lower_ok), (256, 64, upper_ok)]
        slabs += [(320 + 64 * p, 64, bias2[p]) for p in range(3)]
        u = b * 2 + hp
        keep(u, merge(kept(u), attend(kb[b, hp], vbt[b, hp], qbd[b, hp], slabs)))
        if u == 1:
            passed(4)
            phase3(4).start()
            exchange_if(5, soon)
            gathered(5)
            pass_on(5)
    exchange_if(6, soon)
    gathered(6)
    pass_on(6)
    passed(5)
    phase3(5).start()

    def far_chunk(levels, k_to, vt_to):
        slabs, keys, values = [], ([], []), ([], [])
        for level in levels:
            phase3(level).wait_recv()
            n = 256 // 2**level
            g = group(level)
            for p, bias in enumerate(far_bias(level)):
                slabs.append((64 * len(slabs), 64, bias))
                whole = gathers[level][:, :, p].reshape(g, 4 * n, 128)
                if n >= 16:
                    four = [whole[:, c * n : (c + 1) * n, :].reshape(64, 128) for c in range(4)]
                else:
                    moved = dot(unpack(n), whole.reshape(256, 128)).astype(BF16)
                    four = [moved[c * 64 : (c + 1) * 64] for c in range(4)]
                for hp in range(2):
                    keys[hp].append(four[hp])
                    values[hp].append(four[2 + hp])
        for hp in range(2):
            k_to[hp] = jnp.concatenate(keys[hp], 0)
            vt_to[hp] = jnp.concatenate(values[hp], 0).T
        return slabs

    slabs = far_chunk((3, 4), kc, vct)
    for b, hp in units:
        u = b * 2 + hp
        keep(u, merge(kept(u), attend(kc[hp], vct[hp], qbd[b, hp], slabs)))
        if u == 1:
            passed(6)
            phase3(6).start()
    slabs = far_chunk((5,), kd.at[0], vdt.at[0])
    for b, hp in units:
        u = b * 2 + hp
        keep(u, merge(kept(u), attend(kd[0, hp], vdt[0, hp], qbd[b, hp], slabs)))
    for t in range(1, heads):
        granted(("head", t))
    slabs = far_chunk((6,), kd.at[1], vdt.at[1])
    for b, hp in units:
        u = b * 2 + hp
        _, total, o = merge(kept(u), attend(kd[1, hp], vdt[1, hp], qbd[b, hp], slabs))
        o = (o / total).astype(BF16)
        rows = jnp.concatenate([o[:, :BLOCK], o[:, BLOCK:]], 0)
        if hp == 0:
            upper = rows
            continue
        attended = jnp.concatenate([upper, rows], 0)
        for t in (2, 1, 3):
            part[b, t - 1] = dot(wt[(x + t) % heads], attended).astype(BF16)
            share(b, t).start()
        own_part[b] = dot(wt[x], attended)

    for level, p in all1:
        on(inside["far", level, p], lambda: phase1(level, p).wait_send())
    for level, j in all2:
        phase2(level, j).wait_send()
    for level in (2,) + FAR:
        phase3(level).wait_send()
    for up in (True, False):
        on(inside["near", up], lambda: neighbour(up).wait_send())

    for b in range(2):
        total = own_part[b]
        for t in (1, 3, 2):
            share(b, t).wait_recv()
            total = total + got[t - 1, b].astype(F32)
        out_ref[:, b * BLOCK : (b + 1) * BLOCK] = total.astype(BF16)

    for b in range(2):
        for t in range(1, heads):
            share(b, t).wait_send()


def solution(mesh):
    devices, heads = mesh.shape["seq"], mesh.shape["head"]

    def shards(q, k, v, w):
        rows, width = q.shape
        lanes = w.shape[1] // heads
        vmem = pl.BlockSpec(memory_space=pltpu.VMEM)
        dma = pltpu.SemaphoreType.DMA

        def gather(level):
            return pltpu.VMEM((2 ** (level - 3), 2, 3, 4 * (rows >> level), 128), BF16)

        def stage(level):
            return pltpu.VMEM((4 * (rows >> level), 128), BF16)

        return pl.pallas_call(
            functools.partial(kernel, devices, heads),
            out_shape=jax.ShapeDtypeStruct((lanes, rows), BF16),
            in_specs=[pl.BlockSpec(memory_space=pltpu.HBM)] * 4,
            out_specs=vmem,
            scratch_shapes=[
                pltpu.VMEM((rows, width), BF16),
                pltpu.VMEM((rows, width), BF16),
                pltpu.VMEM((rows, width), BF16),
                pltpu.VMEM((width, heads * lanes), BF16),
                pltpu.VMEM((2, 4 * (BLOCK + HALF), 128), BF16),
                pltpu.VMEM((2, 4 * (BLOCK + HALF), 128), BF16),
                pltpu.VMEM((3, 4 * HALF, 128), BF16),
                gather(3), gather(4), gather(5), gather(6),
                stage(2), stage(3), stage(4), stage(5), stage(6),
                pltpu.VMEM((2, 2, 128, 256), BF16),
                pltpu.VMEM((2, 2, 512, 128), BF16),
                pltpu.VMEM((2, 2, 128, 512), BF16),
                pltpu.VMEM((2, 384, 128), BF16),
                pltpu.VMEM((2, 128, 384), BF16),
                pltpu.VMEM((2, 2, 192, 128), BF16),
                pltpu.VMEM((2, 2, 128, 192), BF16),
                pltpu.VMEM((heads, lanes, width), BF16),
                pltpu.VMEM((2, lanes, BLOCK), F32),
                pltpu.VMEM((2, heads - 1, lanes, BLOCK), BF16),
                pltpu.VMEM((heads - 1, 2, lanes, BLOCK), BF16),
                pltpu.VMEM((4, 8, 256), F32),
                pltpu.VMEM((4, 8, 256), F32),
                pltpu.VMEM((4, HEAD_DIM, 256), F32),
                pltpu.SemaphoreType.REGULAR((26,)),
                dma((4,)),
                dma((5, 3)), dma((5, 3)), dma((11,)), dma((11,)), dma((5,)), dma((5,)),
                dma((2,)), dma((2,)),
                dma((2, heads - 1)), dma((2, heads - 1)),
            ],
            compiler_params=pltpu.CompilerParams(
                collective_id=0, has_side_effects=True, vmem_limit_bytes=55040 * 1024
            ),
            cost_estimate=pl.CostEstimate(
                flops=2_000_000_000, bytes_accessed=1_200_000, transcendentals=1_600_000
            ),
        )(q, k, v, w)

    placed = (P("seq", "head"), P("seq", "head"), P("seq", "head"), P("head", None))
    return jax.shard_map(
        shards, mesh=mesh, in_specs=placed, out_specs=P("head", "seq"), check_vma=False
    )
```

```python
import functools

import jax
import jax.numpy as jnp
from jax import lax
from jax.experimental import pallas as pl
from jax.experimental.pallas import tpu as pltpu
from jax.sharding import PartitionSpec as P

HEAD_DIM = 64
BLOCK = 128
LEVELS = 6
HALF = BLOCK // 2
F32 = jnp.float32
BF16 = jnp.bfloat16
MESH = pl.DeviceIdType.MESH
FAR = (3, 4, 5, 6)
OFF = -1e30
EARLY, MIDDLE, LATE = 4, 6, 8


def dot(a, b):
    return jnp.dot(a, b, preferred_element_type=F32)


def iota(shape, dim):
    return lax.broadcasted_iota(jnp.int32, shape, dim)


def pool(rows, fine, level, repeat):
    r, c = iota((rows, fine), 0), iota((rows, fine), 1)
    hit = (c >> level) == (r & (repeat - 1))
    return jnp.where(hit, 2.0**-level, 0.0).astype(BF16)


def unpack(n):
    r, c = iota((256, 256), 0), iota((256, 256), 1)
    group, inside = r >> 6, r & 63
    source, row = inside // n, inside & (n - 1)
    return jnp.where(c == source * (4 * n) + group * n + row, 1.0, 0.0).astype(BF16)


def scores_top(s, slabs):
    top = None
    for start, rows, bias in slabs:
        m = jnp.max(s[start : start + rows], axis=0, keepdims=True)
        if bias is not None:
            m = m + bias
        top = m if top is None else jnp.maximum(top, m)
    return top


def attend(k, vt, q, slabs):
    s = dot(k, q)
    top = scores_top(s, slabs)
    parts, total = [], None
    for start, rows, bias in slabs:
        shift = top if bias is None else top - bias
        p = jnp.exp(s[start : start + rows] - shift)
        t = jnp.sum(p, axis=0, keepdims=True)
        total = t if total is None else total + t
        parts.append(p.astype(BF16))
    o = dot(vt, jnp.concatenate(parts, 0))
    o = jnp.concatenate([o[:HEAD_DIM, :BLOCK], o[HEAD_DIM:, BLOCK:]], 1)
    return top, total, o


def merge(a, b):
    top = jnp.maximum(a[0], b[0])
    fa, fb = jnp.exp(a[0] - top), jnp.exp(b[0] - top)
    return top, a[1] * fa + b[1] * fb, a[2] * fa + b[2] * fb


def kernel(
    devices, heads,
    q_hbm, k_hbm, v_hbm, w_hbm, out_ref,
    q_ref, k_ref, v_ref, w_ref, rim, near, g2, g3, g4, g5, g6, s2, s3, s4, s5, s6,
    qbd, kb, vbt, kc, vct, kd, vdt, wt, own_part, part, got, st_m, st_l, st_o, grants, in_s,
    p1_s, p1_r, p2_s, p2_r, p3_s, p3_r, near_s, near_r, part_s, part_r,
):
    d = lax.axis_index("seq")
    x = lax.axis_index("head")
    core = d % 2
    gathers = {3: g3, 4: g4, 5: g5, 6: g6}
    stages = {2: s2, 3: s3, 4: s4, 5: s5, 6: s6}

    def seq(steps):
        return (d + steps + 2 * devices) % devices

    def group(level):
        return 2 ** (level - 2)

    def far_steps(level, p):
        g = group(level)
        if p == 0:
            return 2 * g
        if p == 1:
            return -2 * g
        return (3 - 6 * ((d // g) % 2)) * g

    def remote(src, dst, send, recv, axis, target):
        return pltpu.make_async_remote_copy(
            src_ref=src, dst_ref=dst, send_sem=send, recv_sem=recv,
            device_id={axis: target}, device_id_type=MESH,
        )

    def far_target(level, p):
        target = seq(far_steps(level, p))
        if level == 4 and p == 2:
            target = target + 2 - 4 * ((target // 2) % 2)
        return target

    def phase1(level, p):
        at = (level - 2, p)
        rank = (d % group(level)) // 2
        if level == 2:
            dst = g2.at[p]
        elif level == 4 and p == 2:
            dst = g4.at[1 - rank, core, p]
        else:
            dst = gathers[level].at[rank, core, p]
        return remote(stages[level], dst, p1_s.at[at], p1_r.at[at], "seq", far_target(level, p))

    def phase2_target(level, j):
        chips = group(level) // 2
        mine = (d // 2) % chips
        return d - 2 * mine + 2 * ((mine + j) % chips)

    def phase2(level, j):
        slot = {4: 0, 5: 1, 6: 4}[level] + j - 1
        block = gathers[level].at[(d // 2) % (group(level) // 2), core]
        return remote(block, block, p2_s.at[slot], p2_r.at[slot], "seq", phase2_target(level, j))

    def phase3(level):
        if level == 2:
            src, dst = g2.at[core], g2.at[2]
        else:
            src = dst = gathers[level].at[:, core]
        slot = level - 2
        return remote(src, dst, p3_s.at[slot], p3_r.at[slot], "seq", d + 1 - 2 * core)

    def neighbour(up):
        side = 0 if up else 1
        return remote(
            rim.at[side], near.at[side], near_s.at[side], near_r.at[side], "seq", seq(1 if up else -1)
        )

    def share(b, t):
        at = (b, t - 1)
        return remote(part.at[b, t - 1], got.at[t - 1, b], part_s.at[at], part_r.at[at], "head", (x + t) % heads)

    all1 = [(level, p) for level in (6, 5, 4, 3, 2) for p in range(3 if level > 2 else 2)]
    all2 = [(level, j) for level in (4, 5, 6) for j in range(1, group(level) // 2)]

    def pass_on(level):
        for other, j in all2:
            if other == level:
                phase2(level, j).start()

    def passed(level):
        for other, j in all2:
            if other == level:
                phase2(level, j).wait_recv()

    back = (1, 0, 2)
    relations = {}
    for level, p in all1:
        there = d // group(level) + far_steps(level, p) // group(level)
        inside = (there >= 0) & (there < devices // group(level))
        relations["far", level, p] = ("seq", far_target(level, p), ("far", level, back[p]), inside)
    for up in (True, False):
        inside = d < devices - 1 if up else d > 0
        relations["near", up] = ("seq", seq(1 if up else -1), ("near", not up), inside)
    for j in range(1, 8):
        relations["mate", j] = ("seq", phase2_target(6, j), ("mate", 8 - j), True)
    for t in range(1, heads):
        relations["head", t] = ("head", (x + t) % heads, ("head", heads - t), True)
    slots = {name: i for i, name in enumerate(relations)}
    inside = {name: relation[3] for name, relation in relations.items()}
    above, below = {}, {}
    for name, (axis, target, _, valid) in relations.items():
        here = d if axis == "seq" else x
        above[name] = (target > here) & valid
        below[name] = (target < here) & valid

    def on(condition, *steps):
        @pl.when(condition)
        def _():
            for step in steps:
                step()

    def signal(semaphore, name):
        axis, target = relations[name][:2]
        pl.semaphore_signal(semaphore, inc=1, device_id={axis: target}, device_id_type=MESH)

    def granted(name, *steps):
        on(above[name], lambda: pl.semaphore_wait(grants.at[slots[name]], 1), *steps)

    def arrived(level, p):
        on(inside["far", level, back[p]], lambda: phase1(level, p).wait_recv())

    loads = [
        pltpu.make_async_copy(src, dst, in_s.at[i])
        for i, (src, dst) in enumerate(
            [(k_hbm, k_ref), (v_hbm, v_ref), (q_hbm, q_ref), (w_hbm, w_ref)]
        )
    ]
    loads[0].start()
    loads[1].start()
    barrier = pltpu.get_barrier_semaphore()
    for name in relations:
        on(above[name], lambda: signal(barrier, name))
    loads[2].start()
    loads[3].start()
    count = sum(jnp.where(below[name], 1, 0) for name in relations)
    on(count > 0, lambda: pl.semaphore_wait(barrier, count))
    for name in relations:
        on(below[name], lambda: signal(grants.at[slots[relations[name][2]]], name))

    pools = jnp.concatenate(
        [pool(BLOCK, 256, 1, 128), pool(64, 256, 2, 64), pool(32, 256, 3, 32), pool(16, 256, 4, 16),
         pool(32, 256, 5, 8), pool(16, 256, 6, 4)], 0)
    loads[0].wait()
    loads[1].wait()
    k, v = k_ref[...], v_ref[...]
    ck, cv = dot(pools, k), dot(pools, v)
    blocks = [ck[:, :128], ck[:, 128:], cv[:, :128], cv[:, 128:]]
    for level, start, n in ((2, 128, 64), (3, 192, 32), (4, 224, 16)):
        for c in range(4):
            stages[level][c * n : (c + 1) * n, :] = blocks[c][start : start + n].astype(BF16)
    for level, start, n in ((5, 240, 8), (6, 272, 4)):
        owner = iota((4 * n, 128), 0) // n
        packed = blocks[0][start : start + 4 * n]
        for c in range(1, 4):
            packed = jnp.where(owner == c, blocks[c][start : start + 4 * n], packed)
        stages[level][...] = packed.astype(BF16)
    fine = [k[:, :128], k[:, 128:], v[:, :128], v[:, 128:]]
    for side in range(2):
        edge = BLOCK * (1 - side)
        for c in range(4):
            rim[side, c * BLOCK : (c + 1) * BLOCK, :] = fine[c][edge : edge + BLOCK]
            rim[side, 512 + c * HALF : 512 + (c + 1) * HALF, :] = blocks[c][side * HALF : (side + 1) * HALF].astype(BF16)

    for level, p in all1:
        on(below["far", level, p], lambda: phase1(level, p).start())
    on(below["near", False], lambda: neighbour(False).start())

    def clear(ref):
        ref[...] = jnp.zeros(ref.shape, ref.dtype)

    for level, p in all1:
        slot = g2.at[p] if level == 2 else gathers[level].at[(d % group(level)) // 2, core, p]
        on(jnp.logical_not(inside["far", level, back[p]]), lambda: clear(slot))
    on(d == 0, lambda: clear(near.at[0]))
    on(d == devices - 1, lambda: clear(near.at[1]))
    granted(("near", True), lambda: neighbour(True).start())

    plane = d // 8
    soon, middle, last = plane < MIDDLE, (plane >= MIDDLE) & (plane < LATE), plane >= LATE

    def exchange_if(level, condition):
        for p in range(3 if level > 2 else 2):
            name = ("far", level, p)
            on(
                above[name] & condition,
                lambda: pl.semaphore_wait(grants.at[slots[name]], 1),
                lambda: phase1(level, p).start(),
            )

    for level in (6, 5, 4, 3, 2):
        exchange_if(level, last)

    loads[2].wait()
    qt = (q_ref[...].astype(F32) * HEAD_DIM**-0.5).T
    feature = iota((BLOCK, BLOCK), 0)
    for b in range(2):
        for hp in range(2):
            piece = qt[hp * BLOCK : (hp + 1) * BLOCK, b * BLOCK : (b + 1) * BLOCK]
            low = jnp.where(feature < HEAD_DIM, piece, 0.0)
            high = jnp.where(feature < HEAD_DIM, 0.0, piece)
            qbd[b, hp] = jnp.concatenate([low, high], 1).astype(BF16)

    def keep(u, state):
        st_m[u, 0:1, :], st_l[u, 0:1, :], st_o[u] = state

    def kept(u):
        return st_m[u, 0:1, :], st_l[u, 0:1, :], st_o[u]

    units = [(b, hp) for b in range(2) for hp in range(2)]
    for hp in range(2):
        lanes = slice(hp * BLOCK, (hp + 1) * BLOCK)
        vt = v_ref[:, lanes].T
        kk = k_ref[:, lanes]
        for b in range(2):
            keep(b * 2 + hp, attend(kk, vt, qbd[b, hp], [(0, 256, None)]))

    loads[3].wait()
    for i in range(heads):
        wt[i] = w_ref[:, i * 256 : (i + 1) * 256].T

    def gathered(level):
        for p in range(3 if level > 2 else 2):
            arrived(level, p)

    for level in (2, 3, 4):
        exchange_if(level, jnp.logical_not(last))
    exchange_if(5, middle)
    exchange_if(6, middle)
    for j in range(1, 8):
        granted(("mate", j))

    gathered(2)
    phase3(2).start()
    gathered(3)
    phase3(3).start()
    gathered(4)
    pass_on(4)
    on(inside["near", False], lambda: neighbour(True).wait_recv())
    on(inside["near", True], lambda: neighbour(False).wait_recv())
    half_pool = pool(HALF, BLOCK, 1, HALF)
    lower_ok = jnp.where(d > 0, 0.0, OFF).astype(F32)
    upper_ok = jnp.where(d < devices - 1, 0.0, OFF).astype(F32)

    def far_bias(level):
        g, out = group(level), []
        e, last = d // g, devices // g - 1
        steps = (-2, 2, 3 - 6 * (e % 2))
        for step in steps:
            there = e + step
            out.append(jnp.where((there >= 0) & (there <= last), 0.0, OFF).astype(F32))
        return out

    bias2 = far_bias(2)
    phase3(2).wait_recv()
    for c in range(4):
        kind, hp = c // 2, c % 2
        strip = slice(c * BLOCK, (c + 1) * BLOCK)
        rows = slice(c * HALF, (c + 1) * HALF)
        half = slice(512 + c * HALF, 512 + (c + 1) * HALF)
        pooled = [dot(half_pool, near[side, strip, :]).astype(BF16) for side in range(2)]
        common = [near[0, half, :], near[1, half, :]] + [g2[p, rows, :] for p in range(3)]
        for b in range(2):
            full = jnp.concatenate([near[b, strip, :], pooled[1 - b]] + common, 0)
            if kind == 0:
                kb[b, hp] = full
            else:
                vbt[b, hp] = full.T
    for b, hp in units:
        first, second = (lower_ok, upper_ok) if b == 0 else (upper_ok, lower_ok)
        slabs = [(0, 128, first), (128, 64, second), (192, 64, lower_ok), (256, 64, upper_ok)]
        slabs += [(320 + 64 * p, 64, bias2[p]) for p in range(3)]
        u = b * 2 + hp
        keep(u, merge(kept(u), attend(kb[b, hp], vbt[b, hp], qbd[b, hp], slabs)))
        if u == 1:
            passed(4)
            phase3(4).start()
            exchange_if(5, soon)
            exchange_if(6, soon & (plane >= EARLY))
            gathered(5)
            pass_on(5)
    exchange_if(6, plane < EARLY)
    gathered(6)
    pass_on(6)
    passed(5)
    phase3(5).start()

    def far_chunk(levels, k_to, vt_to):
        slabs, keys, values = [], ([], []), ([], [])
        for level in levels:
            phase3(level).wait_recv()
            n = 256 // 2**level
            g = group(level)
            for p, bias in enumerate(far_bias(level)):
                slabs.append((64 * len(slabs), 64, bias))
                whole = gathers[level][:, :, p].reshape(g, 4 * n, 128)
                if n >= 16:
                    four = [whole[:, c * n : (c + 1) * n, :].reshape(64, 128) for c in range(4)]
                else:
                    moved = dot(unpack(n), whole.reshape(256, 128)).astype(BF16)
                    four = [moved[c * 64 : (c + 1) * 64] for c in range(4)]
                for hp in range(2):
                    keys[hp].append(four[hp])
                    values[hp].append(four[2 + hp])
        for hp in range(2):
            k_to[hp] = jnp.concatenate(keys[hp], 0)
            vt_to[hp] = jnp.concatenate(values[hp], 0).T
        return slabs

    slabs = far_chunk((3, 4), kc, vct)
    for b, hp in units:
        u = b * 2 + hp
        keep(u, merge(kept(u), attend(kc[hp], vct[hp], qbd[b, hp], slabs)))
        if u == 1:
            passed(6)
            phase3(6).start()
    slabs = far_chunk((5,), kd.at[0], vdt.at[0])
    for b, hp in units:
        u = b * 2 + hp
        keep(u, merge(kept(u), attend(kd[0, hp], vdt[0, hp], qbd[b, hp], slabs)))
    for t in range(1, heads):
        granted(("head", t))
    slabs = far_chunk((6,), kd.at[1], vdt.at[1])
    for b, hp in units:
        u = b * 2 + hp
        _, total, o = merge(kept(u), attend(kd[1, hp], vdt[1, hp], qbd[b, hp], slabs))
        o = (o / total).astype(BF16)
        rows = jnp.concatenate([o[:, :BLOCK], o[:, BLOCK:]], 0)
        if hp == 0:
            upper = rows
            continue
        attended = jnp.concatenate([upper, rows], 0)
        for t in (2, 1, 3):
            part[b, t - 1] = dot(wt[(x + t) % heads], attended).astype(BF16)
            share(b, t).start()
        own_part[b] = dot(wt[x], attended)

    for level, p in all1:
        on(inside["far", level, p], lambda: phase1(level, p).wait_send())
    for level, j in all2:
        phase2(level, j).wait_send()
    for level in (2,) + FAR:
        phase3(level).wait_send()
    for up in (True, False):
        on(inside["near", up], lambda: neighbour(up).wait_send())

    for b in range(2):
        total = own_part[b]
        for t in (1, 3, 2):
            share(b, t).wait_recv()
            total = total + got[t - 1, b].astype(F32)
        out_ref[:, b * BLOCK : (b + 1) * BLOCK] = total.astype(BF16)

    for b in range(2):
        for t in range(1, heads):
            share(b, t).wait_send()


def solution(mesh):
    devices, heads = mesh.shape["seq"], mesh.shape["head"]

    def shards(q, k, v, w):
        rows, width = q.shape
        lanes = w.shape[1] // heads
        vmem = pl.BlockSpec(memory_space=pltpu.VMEM)
        dma = pltpu.SemaphoreType.DMA

        def gather(level):
            return pltpu.VMEM((2 ** (level - 3), 2, 3, 4 * (rows >> level), 128), BF16)

        def stage(level):
            return pltpu.VMEM((4 * (rows >> level), 128), BF16)

        return pl.pallas_call(
            functools.partial(kernel, devices, heads),
            out_shape=jax.ShapeDtypeStruct((lanes, rows), BF16),
            in_specs=[pl.BlockSpec(memory_space=pltpu.HBM)] * 4,
            out_specs=vmem,
            scratch_shapes=[
                pltpu.VMEM((rows, width), BF16),
                pltpu.VMEM((rows, width), BF16),
                pltpu.VMEM((rows, width), BF16),
                pltpu.VMEM((width, heads * lanes), BF16),
                pltpu.VMEM((2, 4 * (BLOCK + HALF), 128), BF16),
                pltpu.VMEM((2, 4 * (BLOCK + HALF), 128), BF16),
                pltpu.VMEM((3, 4 * HALF, 128), BF16),
                gather(3), gather(4), gather(5), gather(6),
                stage(2), stage(3), stage(4), stage(5), stage(6),
                pltpu.VMEM((2, 2, 128, 256), BF16),
                pltpu.VMEM((2, 2, 512, 128), BF16),
                pltpu.VMEM((2, 2, 128, 512), BF16),
                pltpu.VMEM((2, 384, 128), BF16),
                pltpu.VMEM((2, 128, 384), BF16),
                pltpu.VMEM((2, 2, 192, 128), BF16),
                pltpu.VMEM((2, 2, 128, 192), BF16),
                pltpu.VMEM((heads, lanes, width), BF16),
                pltpu.VMEM((2, lanes, BLOCK), F32),
                pltpu.VMEM((2, heads - 1, lanes, BLOCK), BF16),
                pltpu.VMEM((heads - 1, 2, lanes, BLOCK), BF16),
                pltpu.VMEM((4, 8, 256), F32),
                pltpu.VMEM((4, 8, 256), F32),
                pltpu.VMEM((4, HEAD_DIM, 256), F32),
                pltpu.SemaphoreType.REGULAR((26,)),
                dma((4,)),
                dma((5, 3)), dma((5, 3)), dma((11,)), dma((11,)), dma((5,)), dma((5,)),
                dma((2,)), dma((2,)),
                dma((2, heads - 1)), dma((2, heads - 1)),
            ],
            compiler_params=pltpu.CompilerParams(
                collective_id=0, has_side_effects=True, vmem_limit_bytes=55040 * 1024
            ),
            cost_estimate=pl.CostEstimate(
                flops=2_000_000_000, bytes_accessed=1_200_000, transcendentals=1_600_000
            ),
        )(q, k, v, w)

    placed = (P("seq", "head"), P("seq", "head"), P("seq", "head"), P("head", None))
    return jax.shard_map(
        shards, mesh=mesh, in_specs=placed, out_specs=P("head", "seq"), check_vma=False
    )
```

```python
import functools

import jax
import jax.numpy as jnp
from jax import lax
from jax.experimental import pallas as pl
from jax.experimental.pallas import tpu as pltpu
from jax.sharding import PartitionSpec as P

HEAD_DIM = 64
BLOCK = 128
LEVELS = 6
HALF = BLOCK // 2
F32 = jnp.float32
BF16 = jnp.bfloat16
MESH = pl.DeviceIdType.MESH
FAR = (3, 4, 5, 6)
OFF = -1e30
EARLY, MIDDLE, LATE = 4, 6, 8


def dot(a, b):
    return jnp.dot(a, b, preferred_element_type=F32)


def iota(shape, dim):
    return lax.broadcasted_iota(jnp.int32, shape, dim)


def pool(rows, fine, level, repeat):
    r, c = iota((rows, fine), 0), iota((rows, fine), 1)
    hit = (c >> level) == (r & (repeat - 1))
    return jnp.where(hit, 2.0**-level, 0.0).astype(BF16)


def unpack(n):
    r, c = iota((256, 256), 0), iota((256, 256), 1)
    group, inside = r >> 6, r & 63
    source, row = inside // n, inside & (n - 1)
    return jnp.where(c == source * (4 * n) + group * n + row, 1.0, 0.0).astype(BF16)


def scores_top(s, slabs):
    top = None
    for start, rows, bias in slabs:
        m = jnp.max(s[start : start + rows], axis=0, keepdims=True)
        if bias is not None:
            m = m + bias
        top = m if top is None else jnp.maximum(top, m)
    return top


def attend(k, vt, q, slabs):
    s = dot(k, q)
    top = scores_top(s, slabs)
    parts, total = [], None
    for start, rows, bias in slabs:
        shift = top if bias is None else top - bias
        p = jnp.exp(s[start : start + rows] - shift)
        t = jnp.sum(p, axis=0, keepdims=True)
        total = t if total is None else total + t
        parts.append(p.astype(BF16))
    o = dot(vt, jnp.concatenate(parts, 0))
    o = jnp.concatenate([o[:HEAD_DIM, :BLOCK], o[HEAD_DIM:, BLOCK:]], 1)
    return top, total, o


def merge(a, b):
    top = jnp.maximum(a[0], b[0])
    fa, fb = jnp.exp(a[0] - top), jnp.exp(b[0] - top)
    return top, a[1] * fa + b[1] * fb, a[2] * fa + b[2] * fb


def kernel(
    devices, heads,
    q_hbm, k_hbm, v_hbm, w_hbm, out_ref,
    q_ref, k_ref, v_ref, w_ref, rim, near, g2, g3, g4, g5, g6, s2, s3, s4, s5, s6,
    qbd, kb, vbt, kc, vct, kd, vdt, wt, own_part, part, got, st_m, st_l, st_o, grants, in_s,
    p1_s, p1_r, p2_s, p2_r, p3_s, p3_r, near_s, near_r, part_s, part_r,
):
    d = lax.axis_index("seq")
    x = lax.axis_index("head")
    core = d % 2
    gathers = {3: g3, 4: g4, 5: g5, 6: g6}
    stages = {2: s2, 3: s3, 4: s4, 5: s5, 6: s6}

    def seq(steps):
        return (d + steps + 2 * devices) % devices

    def group(level):
        return 2 ** (level - 2)

    def far_steps(level, p):
        g = group(level)
        if p == 0:
            return 2 * g
        if p == 1:
            return -2 * g
        return (3 - 6 * ((d // g) % 2)) * g

    def remote(src, dst, send, recv, axis, target):
        return pltpu.make_async_remote_copy(
            src_ref=src, dst_ref=dst, send_sem=send, recv_sem=recv,
            device_id={axis: target}, device_id_type=MESH,
        )

    def far_target(level, p):
        target = seq(far_steps(level, p))
        if level == 4 and p == 2:
            target = target + 2 - 4 * ((target // 2) % 2)
        return target

    def phase1(level, p):
        at = (level - 2, p)
        rank = (d % group(level)) // 2
        if level == 2:
            dst = g2.at[p]
        elif level == 4 and p == 2:
            dst = g4.at[1 - rank, core, p]
        else:
            dst = gathers[level].at[rank, core, p]
        return remote(stages[level], dst, p1_s.at[at], p1_r.at[at], "seq", far_target(level, p))

    def phase2_target(level, j):
        chips = group(level) // 2
        mine = (d // 2) % chips
        return d - 2 * mine + 2 * ((mine + j) % chips)

    def phase2(level, j):
        slot = {4: 0, 5: 1, 6: 4}[level] + j - 1
        block = gathers[level].at[(d // 2) % (group(level) // 2), core]
        return remote(block, block, p2_s.at[slot], p2_r.at[slot], "seq", phase2_target(level, j))

    def phase3(level):
        if level == 2:
            src, dst = g2.at[core], g2.at[2]
        else:
            src = dst = gathers[level].at[:, core]
        slot = level - 2
        return remote(src, dst, p3_s.at[slot], p3_r.at[slot], "seq", d + 1 - 2 * core)

    def neighbour(up):
        side = 0 if up else 1
        return remote(
            rim.at[side], near.at[side], near_s.at[side], near_r.at[side], "seq", seq(1 if up else -1)
        )

    def share(b, t):
        at = (b, t - 1)
        return remote(part.at[b, t - 1], got.at[t - 1, b], part_s.at[at], part_r.at[at], "head", (x + t) % heads)

    all1 = [(level, p) for level in (6, 5, 4, 3, 2) for p in range(3 if level > 2 else 2)]
    all2 = [(level, j) for level in (4, 5, 6) for j in range(1, group(level) // 2)]

    def pass_on(level):
        for other, j in all2:
            if other == level:
                phase2(level, j).start()

    def passed(level):
        for other, j in all2:
            if other == level:
                phase2(level, j).wait_recv()

    back = (1, 0, 2)
    relations = {}
    for level, p in all1:
        there = d // group(level) + far_steps(level, p) // group(level)
        inside = (there >= 0) & (there < devices // group(level))
        relations["far", level, p] = ("seq", far_target(level, p), ("far", level, back[p]), inside)
    for up in (True, False):
        inside = d < devices - 1 if up else d > 0
        relations["near", up] = ("seq", seq(1 if up else -1), ("near", not up), inside)
    for j in range(1, 8):
        relations["mate", j] = ("seq", phase2_target(6, j), ("mate", 8 - j), True)
    for t in range(1, heads):
        relations["head", t] = ("head", (x + t) % heads, ("head", heads - t), True)
    slots = {name: i for i, name in enumerate(relations)}
    inside = {name: relation[3] for name, relation in relations.items()}
    above, below = {}, {}
    for name, (axis, target, _, valid) in relations.items():
        here = d if axis == "seq" else x
        above[name] = (target > here) & valid
        below[name] = (target < here) & valid

    def on(condition, *steps):
        @pl.when(condition)
        def _():
            for step in steps:
                step()

    def signal(semaphore, name):
        axis, target = relations[name][:2]
        pl.semaphore_signal(semaphore, inc=1, device_id={axis: target}, device_id_type=MESH)

    def granted(name, *steps):
        on(above[name], lambda: pl.semaphore_wait(grants.at[slots[name]], 1), *steps)

    def arrived(level, p):
        on(inside["far", level, back[p]], lambda: phase1(level, p).wait_recv())

    loads = [
        pltpu.make_async_copy(src, dst, in_s.at[i])
        for i, (src, dst) in enumerate(
            [(k_hbm, k_ref), (v_hbm, v_ref), (q_hbm, q_ref), (w_hbm, w_ref)]
        )
    ]
    loads[0].start()
    loads[1].start()
    barrier = pltpu.get_barrier_semaphore()
    for name in relations:
        on(above[name], lambda: signal(barrier, name))
    loads[2].start()
    loads[3].start()
    count = sum(jnp.where(below[name], 1, 0) for name in relations)
    on(count > 0, lambda: pl.semaphore_wait(barrier, count))
    for name in relations:
        on(below[name], lambda: signal(grants.at[slots[relations[name][2]]], name))

    pools = jnp.concatenate(
        [pool(BLOCK, 256, 1, 128), pool(64, 256, 2, 64), pool(32, 256, 3, 32), pool(16, 256, 4, 16),
         pool(32, 256, 5, 8), pool(16, 256, 6, 4)], 0)
    loads[0].wait()
    loads[1].wait()
    k, v = k_ref[...], v_ref[...]
    ck, cv = dot(pools, k), dot(pools, v)
    blocks = [ck[:, :128], ck[:, 128:], cv[:, :128], cv[:, 128:]]
    for level, start, n in ((2, 128, 64), (3, 192, 32), (4, 224, 16)):
        for c in range(4):
            stages[level][c * n : (c + 1) * n, :] = blocks[c][start : start + n].astype(BF16)
    for level, start, n in ((5, 240, 8), (6, 272, 4)):
        owner = iota((4 * n, 128), 0) // n
        packed = blocks[0][start : start + 4 * n]
        for c in range(1, 4):
            packed = jnp.where(owner == c, blocks[c][start : start + 4 * n], packed)
        stages[level][...] = packed.astype(BF16)
    fine = [k[:, :128], k[:, 128:], v[:, :128], v[:, 128:]]
    for side in range(2):
        edge = BLOCK * (1 - side)
        for c in range(4):
            rim[side, c * BLOCK : (c + 1) * BLOCK, :] = fine[c][edge : edge + BLOCK]
            rim[side, 512 + c * HALF : 512 + (c + 1) * HALF, :] = blocks[c][side * HALF : (side + 1) * HALF].astype(BF16)

    for level, p in all1:
        on(below["far", level, p], lambda: phase1(level, p).start())
    on(below["near", False], lambda: neighbour(False).start())

    def clear(ref):
        ref[...] = jnp.zeros(ref.shape, ref.dtype)

    for level, p in all1:
        slot = g2.at[p] if level == 2 else gathers[level].at[(d % group(level)) // 2, core, p]
        on(jnp.logical_not(inside["far", level, back[p]]), lambda: clear(slot))
    on(d == 0, lambda: clear(near.at[0]))
    on(d == devices - 1, lambda: clear(near.at[1]))
    granted(("near", True), lambda: neighbour(True).start())

    plane = d // 8
    soon, middle, last = plane < MIDDLE, (plane >= MIDDLE) & (plane < LATE), plane >= LATE

    def exchange_if(level, condition):
        for p in range(3 if level > 2 else 2):
            name = ("far", level, p)
            on(
                above[name] & condition,
                lambda: pl.semaphore_wait(grants.at[slots[name]], 1),
                lambda: phase1(level, p).start(),
            )

    for level in (2, 3, 4, 5):
        exchange_if(level, last)

    loads[2].wait()
    qt = (q_ref[...].astype(F32) * HEAD_DIM**-0.5).T
    feature = iota((BLOCK, BLOCK), 0)
    for b in range(2):
        for hp in range(2):
            piece = qt[hp * BLOCK : (hp + 1) * BLOCK, b * BLOCK : (b + 1) * BLOCK]
            low = jnp.where(feature < HEAD_DIM, piece, 0.0)
            high = jnp.where(feature < HEAD_DIM, 0.0, piece)
            qbd[b, hp] = jnp.concatenate([low, high], 1).astype(BF16)

    def keep(u, state):
        st_m[u, 0:1, :], st_l[u, 0:1, :], st_o[u] = state

    def kept(u):
        return st_m[u, 0:1, :], st_l[u, 0:1, :], st_o[u]

    units = [(b, hp) for b in range(2) for hp in range(2)]
    for hp in range(2):
        lanes = slice(hp * BLOCK, (hp + 1) * BLOCK)
        vt = v_ref[:, lanes].T
        kk = k_ref[:, lanes]
        for b in range(2):
            keep(b * 2 + hp, attend(kk, vt, qbd[b, hp], [(0, 256, None)]))

    loads[3].wait()
    for i in range(heads):
        wt[i] = w_ref[:, i * 256 : (i + 1) * 256].T

    def gathered(level):
        for p in range(3 if level > 2 else 2):
            arrived(level, p)

    for level in (2, 3, 4):
        exchange_if(level, jnp.logical_not(last))
    exchange_if(5, middle)
    exchange_if(6, middle | last)
    for j in range(1, 8):
        granted(("mate", j))

    gathered(2)
    phase3(2).start()
    gathered(3)
    phase3(3).start()
    gathered(4)
    pass_on(4)
    on(inside["near", False], lambda: neighbour(True).wait_recv())
    on(inside["near", True], lambda: neighbour(False).wait_recv())
    half_pool = pool(HALF, BLOCK, 1, HALF)
    lower_ok = jnp.where(d > 0, 0.0, OFF).astype(F32)
    upper_ok = jnp.where(d < devices - 1, 0.0, OFF).astype(F32)

    def far_bias(level):
        g, out = group(level), []
        e, last = d // g, devices // g - 1
        steps = (-2, 2, 3 - 6 * (e % 2))
        for step in steps:
            there = e + step
            out.append(jnp.where((there >= 0) & (there <= last), 0.0, OFF).astype(F32))
        return out

    bias2 = far_bias(2)
    phase3(2).wait_recv()
    for c in range(4):
        kind, hp = c // 2, c % 2
        strip = slice(c * BLOCK, (c + 1) * BLOCK)
        rows = slice(c * HALF, (c + 1) * HALF)
        half = slice(512 + c * HALF, 512 + (c + 1) * HALF)
        pooled = [dot(half_pool, near[side, strip, :]).astype(BF16) for side in range(2)]
        common = [near[0, half, :], near[1, half, :]] + [g2[p, rows, :] for p in range(3)]
        for b in range(2):
            full = jnp.concatenate([near[b, strip, :], pooled[1 - b]] + common, 0)
            if kind == 0:
                kb[b, hp] = full
            else:
                vbt[b, hp] = full.T
    for b, hp in units:
        first, second = (lower_ok, upper_ok) if b == 0 else (upper_ok, lower_ok)
        slabs = [(0, 128, first), (128, 64, second), (192, 64, lower_ok), (256, 64, upper_ok)]
        slabs += [(320 + 64 * p, 64, bias2[p]) for p in range(3)]
        u = b * 2 + hp
        keep(u, merge(kept(u), attend(kb[b, hp], vbt[b, hp], qbd[b, hp], slabs)))
        if u == 1:
            passed(4)
            phase3(4).start()
            exchange_if(5, soon)
            exchange_if(6, soon & (plane >= EARLY))
            gathered(5)
            pass_on(5)
    exchange_if(6, plane < EARLY)
    gathered(6)
    pass_on(6)
    passed(5)
    phase3(5).start()

    def far_chunk(levels, k_to, vt_to):
        slabs, keys, values = [], ([], []), ([], [])
        for level in levels:
            phase3(level).wait_recv()
            n = 256 // 2**level
            g = group(level)
            for p, bias in enumerate(far_bias(level)):
                slabs.append((64 * len(slabs), 64, bias))
                whole = gathers[level][:, :, p].reshape(g, 4 * n, 128)
                if n >= 16:
                    four = [whole[:, c * n : (c + 1) * n, :].reshape(64, 128) for c in range(4)]
                else:
                    moved = dot(unpack(n), whole.reshape(256, 128)).astype(BF16)
                    four = [moved[c * 64 : (c + 1) * 64] for c in range(4)]
                for hp in range(2):
                    keys[hp].append(four[hp])
                    values[hp].append(four[2 + hp])
        for hp in range(2):
            k_to[hp] = jnp.concatenate(keys[hp], 0)
            vt_to[hp] = jnp.concatenate(values[hp], 0).T
        return slabs

    slabs = far_chunk((3, 4), kc, vct)
    for b, hp in units:
        u = b * 2 + hp
        keep(u, merge(kept(u), attend(kc[hp], vct[hp], qbd[b, hp], slabs)))
        if u == 1:
            passed(6)
            phase3(6).start()
    slabs = far_chunk((5,), kd.at[0], vdt.at[0])
    for b, hp in units:
        u = b * 2 + hp
        keep(u, merge(kept(u), attend(kd[0, hp], vdt[0, hp], qbd[b, hp], slabs)))
    for t in range(1, heads):
        granted(("head", t))
    slabs = far_chunk((6,), kd.at[1], vdt.at[1])
    for b, hp in units:
        u = b * 2 + hp
        _, total, o = merge(kept(u), attend(kd[1, hp], vdt[1, hp], qbd[b, hp], slabs))
        o = (o / total).astype(BF16)
        rows = jnp.concatenate([o[:, :BLOCK], o[:, BLOCK:]], 0)
        if hp == 0:
            upper = rows
            continue
        attended = jnp.concatenate([upper, rows], 0)
        for t in (2, 1, 3):
            part[b, t - 1] = dot(wt[(x + t) % heads], attended).astype(BF16)
            share(b, t).start()
        own_part[b] = dot(wt[x], attended)

    for level, p in all1:
        on(inside["far", level, p], lambda: phase1(level, p).wait_send())
    for level, j in all2:
        phase2(level, j).wait_send()
    for level in (2,) + FAR:
        phase3(level).wait_send()
    for up in (True, False):
        on(inside["near", up], lambda: neighbour(up).wait_send())

    for b in range(2):
        total = own_part[b]
        for t in (1, 3, 2):
            share(b, t).wait_recv()
            total = total + got[t - 1, b].astype(F32)
        out_ref[:, b * BLOCK : (b + 1) * BLOCK] = total.astype(BF16)

    for b in range(2):
        for t in range(1, heads):
            share(b, t).wait_send()


def solution(mesh):
    devices, heads = mesh.shape["seq"], mesh.shape["head"]

    def shards(q, k, v, w):
        rows, width = q.shape
        lanes = w.shape[1] // heads
        vmem = pl.BlockSpec(memory_space=pltpu.VMEM)
        dma = pltpu.SemaphoreType.DMA

        def gather(level):
            return pltpu.VMEM((2 ** (level - 3), 2, 3, 4 * (rows >> level), 128), BF16)

        def stage(level):
            return pltpu.VMEM((4 * (rows >> level), 128), BF16)

        return pl.pallas_call(
            functools.partial(kernel, devices, heads),
            out_shape=jax.ShapeDtypeStruct((lanes, rows), BF16),
            in_specs=[pl.BlockSpec(memory_space=pltpu.HBM)] * 4,
            out_specs=vmem,
            scratch_shapes=[
                pltpu.VMEM((rows, width), BF16),
                pltpu.VMEM((rows, width), BF16),
                pltpu.VMEM((rows, width), BF16),
                pltpu.VMEM((width, heads * lanes), BF16),
                pltpu.VMEM((2, 4 * (BLOCK + HALF), 128), BF16),
                pltpu.VMEM((2, 4 * (BLOCK + HALF), 128), BF16),
                pltpu.VMEM((3, 4 * HALF, 128), BF16),
                gather(3), gather(4), gather(5), gather(6),
                stage(2), stage(3), stage(4), stage(5), stage(6),
                pltpu.VMEM((2, 2, 128, 256), BF16),
                pltpu.VMEM((2, 2, 512, 128), BF16),
                pltpu.VMEM((2, 2, 128, 512), BF16),
                pltpu.VMEM((2, 384, 128), BF16),
                pltpu.VMEM((2, 128, 384), BF16),
                pltpu.VMEM((2, 2, 192, 128), BF16),
                pltpu.VMEM((2, 2, 128, 192), BF16),
                pltpu.VMEM((heads, lanes, width), BF16),
                pltpu.VMEM((2, lanes, BLOCK), F32),
                pltpu.VMEM((2, heads - 1, lanes, BLOCK), BF16),
                pltpu.VMEM((heads - 1, 2, lanes, BLOCK), BF16),
                pltpu.VMEM((4, 8, 256), F32),
                pltpu.VMEM((4, 8, 256), F32),
                pltpu.VMEM((4, HEAD_DIM, 256), F32),
                pltpu.SemaphoreType.REGULAR((26,)),
                dma((4,)),
                dma((5, 3)), dma((5, 3)), dma((11,)), dma((11,)), dma((5,)), dma((5,)),
                dma((2,)), dma((2,)),
                dma((2, heads - 1)), dma((2, heads - 1)),
            ],
            compiler_params=pltpu.CompilerParams(
                collective_id=0, has_side_effects=True, vmem_limit_bytes=55040 * 1024
            ),
            cost_estimate=pl.CostEstimate(
                flops=2_000_000_000, bytes_accessed=1_200_000, transcendentals=1_600_000
            ),
        )(q, k, v, w)

    placed = (P("seq", "head"), P("seq", "head"), P("seq", "head"), P("head", None))
    return jax.shard_map(
        shards, mesh=mesh, in_specs=placed, out_specs=P("head", "seq"), check_vma=False
    )
```

```python
import functools

import jax
import jax.numpy as jnp
from jax import lax
from jax.experimental import pallas as pl
from jax.experimental.pallas import tpu as pltpu
from jax.sharding import PartitionSpec as P

HEAD_DIM = 64
BLOCK = 128
LEVELS = 6
HALF = BLOCK // 2
F32 = jnp.float32
BF16 = jnp.bfloat16
MESH = pl.DeviceIdType.MESH
FAR = (3, 4, 5, 6)
OFF = -1e30
EARLY, MIDDLE, LATE = 4, 6, 8


def dot(a, b):
    return jnp.dot(a, b, preferred_element_type=F32)


def iota(shape, dim):
    return lax.broadcasted_iota(jnp.int32, shape, dim)


def pool(rows, fine, level, repeat):
    r, c = iota((rows, fine), 0), iota((rows, fine), 1)
    hit = (c >> level) == (r & (repeat - 1))
    return jnp.where(hit, 2.0**-level, 0.0).astype(BF16)


def unpack(n):
    r, c = iota((256, 256), 0), iota((256, 256), 1)
    group, inside = r >> 6, r & 63
    source, row = inside // n, inside & (n - 1)
    return jnp.where(c == source * (4 * n) + group * n + row, 1.0, 0.0).astype(BF16)


def scores_top(s, slabs):
    top = None
    for start, rows, bias in slabs:
        m = jnp.max(s[start : start + rows], axis=0, keepdims=True)
        if bias is not None:
            m = m + bias
        top = m if top is None else jnp.maximum(top, m)
    return top


def attend(k, vt, q, slabs):
    s = dot(k, q)
    top = scores_top(s, slabs)
    parts, total = [], None
    for start, rows, bias in slabs:
        shift = top if bias is None else top - bias
        p = jnp.exp(s[start : start + rows] - shift)
        t = jnp.sum(p, axis=0, keepdims=True)
        total = t if total is None else total + t
        parts.append(p.astype(BF16))
    o = dot(vt, jnp.concatenate(parts, 0))
    o = jnp.concatenate([o[:HEAD_DIM, :BLOCK], o[HEAD_DIM:, BLOCK:]], 1)
    return top, total, o


def merge(a, b):
    top = jnp.maximum(a[0], b[0])
    fa, fb = jnp.exp(a[0] - top), jnp.exp(b[0] - top)
    return top, a[1] * fa + b[1] * fb, a[2] * fa + b[2] * fb


def kernel(
    devices, heads,
    q_hbm, k_hbm, v_hbm, w_hbm, out_ref,
    q_ref, k_ref, v_ref, w_ref, rim, near, g2, g3, g4, g5, g6, s2, s3, s4, s5, s6,
    qbd, kb, vbt, kc, vct, kd, vdt, wt, own_part, part, got, st_m, st_l, st_o, grants, in_s,
    p1_s, p1_r, p2_s, p2_r, p3_s, p3_r, near_s, near_r, part_s, part_r,
):
    d = lax.axis_index("seq")
    x = lax.axis_index("head")
    core = d % 2
    gathers = {3: g3, 4: g4, 5: g5, 6: g6}
    stages = {2: s2, 3: s3, 4: s4, 5: s5, 6: s6}

    def seq(steps):
        return (d + steps + 2 * devices) % devices

    def group(level):
        return 2 ** (level - 2)

    def far_steps(level, p):
        g = group(level)
        if p == 0:
            return 2 * g
        if p == 1:
            return -2 * g
        return (3 - 6 * ((d // g) % 2)) * g

    def remote(src, dst, send, recv, axis, target):
        return pltpu.make_async_remote_copy(
            src_ref=src, dst_ref=dst, send_sem=send, recv_sem=recv,
            device_id={axis: target}, device_id_type=MESH,
        )

    def far_target(level, p):
        target = seq(far_steps(level, p))
        if level == 4 and p == 2:
            target = target + 2 - 4 * ((target // 2) % 2)
        return target

    def phase1(level, p):
        at = (level - 2, p)
        rank = (d % group(level)) // 2
        if level == 2:
            dst = g2.at[p]
        elif level == 4 and p == 2:
            dst = g4.at[1 - rank, core, p]
        else:
            dst = gathers[level].at[rank, core, p]
        return remote(stages[level], dst, p1_s.at[at], p1_r.at[at], "seq", far_target(level, p))

    def phase2_target(level, j):
        chips = group(level) // 2
        mine = (d // 2) % chips
        return d - 2 * mine + 2 * ((mine + j) % chips)

    def phase2(level, j):
        slot = {4: 0, 5: 1, 6: 4}[level] + j - 1
        block = gathers[level].at[(d // 2) % (group(level) // 2), core]
        return remote(block, block, p2_s.at[slot], p2_r.at[slot], "seq", phase2_target(level, j))

    def phase3(level):
        if level == 2:
            src, dst = g2.at[core], g2.at[2]
        else:
            src = dst = gathers[level].at[:, core]
        slot = level - 2
        return remote(src, dst, p3_s.at[slot], p3_r.at[slot], "seq", d + 1 - 2 * core)

    def neighbour(up):
        side = 0 if up else 1
        return remote(
            rim.at[side], near.at[side], near_s.at[side], near_r.at[side], "seq", seq(1 if up else -1)
        )

    def share(b, t):
        at = (b, t - 1)
        return remote(part.at[b, t - 1], got.at[t - 1, b], part_s.at[at], part_r.at[at], "head", (x + t) % heads)

    all1 = [(level, p) for level in (6, 5, 4, 3, 2) for p in range(3 if level > 2 else 2)]
    all2 = [(level, j) for level in (4, 5, 6) for j in range(1, group(level) // 2)]

    def pass_on(level):
        for other, j in all2:
            if other == level:
                phase2(level, j).start()

    def passed(level):
        for other, j in all2:
            if other == level:
                phase2(level, j).wait_recv()

    back = (1, 0, 2)
    relations = {}
    for level, p in all1:
        there = d // group(level) + far_steps(level, p) // group(level)
        inside = (there >= 0) & (there < devices // group(level))
        relations["far", level, p] = ("seq", far_target(level, p), ("far", level, back[p]), inside)
    for up in (True, False):
        inside = d < devices - 1 if up else d > 0
        relations["near", up] = ("seq", seq(1 if up else -1), ("near", not up), inside)
    for j in range(1, 8):
        relations["mate", j] = ("seq", phase2_target(6, j), ("mate", 8 - j), True)
    for t in range(1, heads):
        relations["head", t] = ("head", (x + t) % heads, ("head", heads - t), True)
    slots = {name: i for i, name in enumerate(relations)}
    inside = {name: relation[3] for name, relation in relations.items()}
    above, below = {}, {}
    for name, (axis, target, _, valid) in relations.items():
        here = d if axis == "seq" else x
        above[name] = (target > here) & valid
        below[name] = (target < here) & valid

    def on(condition, *steps):
        @pl.when(condition)
        def _():
            for step in steps:
                step()

    def signal(semaphore, name):
        axis, target = relations[name][:2]
        pl.semaphore_signal(semaphore, inc=1, device_id={axis: target}, device_id_type=MESH)

    def granted(name, *steps):
        on(above[name], lambda: pl.semaphore_wait(grants.at[slots[name]], 1), *steps)

    def arrived(level, p):
        on(inside["far", level, back[p]], lambda: phase1(level, p).wait_recv())

    loads = [
        pltpu.make_async_copy(src, dst, in_s.at[i])
        for i, (src, dst) in enumerate(
            [(k_hbm, k_ref), (v_hbm, v_ref), (q_hbm, q_ref), (w_hbm, w_ref)]
        )
    ]
    loads[0].start()
    loads[1].start()
    barrier = pltpu.get_barrier_semaphore()
    for name in relations:
        on(above[name], lambda: signal(barrier, name))
    loads[2].start()
    loads[3].start()
    count = sum(jnp.where(below[name], 1, 0) for name in relations)
    on(count > 0, lambda: pl.semaphore_wait(barrier, count))
    for name in relations:
        on(below[name], lambda: signal(grants.at[slots[relations[name][2]]], name))

    pools = jnp.concatenate(
        [pool(BLOCK, 256, 1, 128), pool(64, 256, 2, 64), pool(32, 256, 3, 32), pool(16, 256, 4, 16),
         pool(32, 256, 5, 8), pool(16, 256, 6, 4)], 0)
    loads[0].wait()
    loads[1].wait()
    k, v = k_ref[...], v_ref[...]
    ck, cv = dot(pools, k), dot(pools, v)
    blocks = [ck[:, :128], ck[:, 128:], cv[:, :128], cv[:, 128:]]
    for level, start, n in ((2, 128, 64), (3, 192, 32), (4, 224, 16)):
        for c in range(4):
            stages[level][c * n : (c + 1) * n, :] = blocks[c][start : start + n].astype(BF16)
    for level, start, n in ((5, 240, 8), (6, 272, 4)):
        owner = iota((4 * n, 128), 0) // n
        packed = blocks[0][start : start + 4 * n]
        for c in range(1, 4):
            packed = jnp.where(owner == c, blocks[c][start : start + 4 * n], packed)
        stages[level][...] = packed.astype(BF16)
    fine = [k[:, :128], k[:, 128:], v[:, :128], v[:, 128:]]
    for side in range(2):
        edge = BLOCK * (1 - side)
        for c in range(4):
            rim[side, c * BLOCK : (c + 1) * BLOCK, :] = fine[c][edge : edge + BLOCK]
            rim[side, 512 + c * HALF : 512 + (c + 1) * HALF, :] = blocks[c][side * HALF : (side + 1) * HALF].astype(BF16)

    for level, p in all1:
        on(below["far", level, p], lambda: phase1(level, p).start())
    on(below["near", False], lambda: neighbour(False).start())

    def clear(ref):
        ref[...] = jnp.zeros(ref.shape, ref.dtype)

    for level, p in all1:
        slot = g2.at[p] if level == 2 else gathers[level].at[(d % group(level)) // 2, core, p]
        on(jnp.logical_not(inside["far", level, back[p]]), lambda: clear(slot))
    on(d == 0, lambda: clear(near.at[0]))
    on(d == devices - 1, lambda: clear(near.at[1]))
    granted(("near", True), lambda: neighbour(True).start())

    plane = d // 8
    soon, middle, last = plane < MIDDLE, (plane >= MIDDLE) & (plane < LATE), plane >= LATE

    def exchange_if(level, condition):
        for p in range(3 if level > 2 else 2):
            name = ("far", level, p)
            on(
                above[name] & condition,
                lambda: pl.semaphore_wait(grants.at[slots[name]], 1),
                lambda: phase1(level, p).start(),
            )

    for level in (2, 3, 4, 5):
        exchange_if(level, last)

    loads[2].wait()
    qt = (q_ref[...].astype(F32) * HEAD_DIM**-0.5).T
    feature = iota((BLOCK, BLOCK), 0)
    for b in range(2):
        for hp in range(2):
            piece = qt[hp * BLOCK : (hp + 1) * BLOCK, b * BLOCK : (b + 1) * BLOCK]
            low = jnp.where(feature < HEAD_DIM, piece, 0.0)
            high = jnp.where(feature < HEAD_DIM, 0.0, piece)
            qbd[b, hp] = jnp.concatenate([low, high], 1).astype(BF16)

    def keep(u, state):
        st_m[u, 0:1, :], st_l[u, 0:1, :], st_o[u] = state

    def kept(u):
        return st_m[u, 0:1, :], st_l[u, 0:1, :], st_o[u]

    units = [(b, hp) for b in range(2) for hp in range(2)]
    for hp in range(2):
        lanes = slice(hp * BLOCK, (hp + 1) * BLOCK)
        vt = v_ref[:, lanes].T
        kk = k_ref[:, lanes]
        for b in range(2):
            keep(b * 2 + hp, attend(kk, vt, qbd[b, hp], [(0, 256, None)]))

    loads[3].wait()
    for i in range(heads):
        wt[i] = w_ref[:, i * 256 : (i + 1) * 256].T

    def gathered(level):
        for p in range(3 if level > 2 else 2):
            arrived(level, p)

    for level in (2, 3, 4):
        exchange_if(level, jnp.logical_not(last))
    exchange_if(5, middle)
    exchange_if(6, middle | last)
    for j in range(1, 8):
        granted(("mate", j))

    gathered(2)
    phase3(2).start()
    gathered(3)
    phase3(3).start()
    gathered(4)
    pass_on(4)
    on(inside["near", False], lambda: neighbour(True).wait_recv())
    on(inside["near", True], lambda: neighbour(False).wait_recv())
    half_pool = pool(HALF, BLOCK, 1, HALF)
    lower_ok = jnp.where(d > 0, 0.0, OFF).astype(F32)
    upper_ok = jnp.where(d < devices - 1, 0.0, OFF).astype(F32)

    def far_bias(level):
        g, out = group(level), []
        e, last = d // g, devices // g - 1
        steps = (-2, 2, 3 - 6 * (e % 2))
        for step in steps:
            there = e + step
            out.append(jnp.where((there >= 0) & (there <= last), 0.0, OFF).astype(F32))
        return out

    bias2 = far_bias(2)
    phase3(2).wait_recv()
    for c in range(4):
        kind, hp = c // 2, c % 2
        strip = slice(c * BLOCK, (c + 1) * BLOCK)
        rows = slice(c * HALF, (c + 1) * HALF)
        half = slice(512 + c * HALF, 512 + (c + 1) * HALF)
        pooled = [dot(half_pool, near[side, strip, :]).astype(BF16) for side in range(2)]
        common = [near[0, half, :], near[1, half, :]] + [g2[p, rows, :] for p in range(3)]
        for b in range(2):
            full = jnp.concatenate([near[b, strip, :], pooled[1 - b]] + common, 0)
            if kind == 0:
                kb[b, hp] = full
            else:
                vbt[b, hp] = full.T
    for b, hp in units:
        first, second = (lower_ok, upper_ok) if b == 0 else (upper_ok, lower_ok)
        slabs = [(0, 128, first), (128, 64, second), (192, 64, lower_ok), (256, 64, upper_ok)]
        slabs += [(320 + 64 * p, 64, bias2[p]) for p in range(3)]
        u = b * 2 + hp
        keep(u, merge(kept(u), attend(kb[b, hp], vbt[b, hp], qbd[b, hp], slabs)))
        if u == 1:
            passed(4)
            phase3(4).start()
            exchange_if(5, soon)
            gathered(5)
            pass_on(5)
        if u == 2:
            exchange_if(6, soon & (plane >= EARLY))
    exchange_if(6, plane < EARLY)
    gathered(6)
    pass_on(6)
    passed(5)
    phase3(5).start()

    def far_chunk(levels, k_to, vt_to):
        slabs, keys, values = [], ([], []), ([], [])
        for level in levels:
            phase3(level).wait_recv()
            n = 256 // 2**level
            g = group(level)
            for p, bias in enumerate(far_bias(level)):
                slabs.append((64 * len(slabs), 64, bias))
                whole = gathers[level][:, :, p].reshape(g, 4 * n, 128)
                if n >= 16:
                    four = [whole[:, c * n : (c + 1) * n, :].reshape(64, 128) for c in range(4)]
                else:
                    moved = dot(unpack(n), whole.reshape(256, 128)).astype(BF16)
                    four = [moved[c * 64 : (c + 1) * 64] for c in range(4)]
                for hp in range(2):
                    keys[hp].append(four[hp])
                    values[hp].append(four[2 + hp])
        for hp in range(2):
            k_to[hp] = jnp.concatenate(keys[hp], 0)
            vt_to[hp] = jnp.concatenate(values[hp], 0).T
        return slabs

    slabs = far_chunk((3, 4), kc, vct)
    for b, hp in units:
        u = b * 2 + hp
        keep(u, merge(kept(u), attend(kc[hp], vct[hp], qbd[b, hp], slabs)))
        if u == 1:
            passed(6)
            phase3(6).start()
    slabs = far_chunk((5,), kd.at[0], vdt.at[0])
    for b, hp in units:
        u = b * 2 + hp
        keep(u, merge(kept(u), attend(kd[0, hp], vdt[0, hp], qbd[b, hp], slabs)))
    for t in range(1, heads):
        granted(("head", t))
    slabs = far_chunk((6,), kd.at[1], vdt.at[1])
    for b, hp in units:
        u = b * 2 + hp
        _, total, o = merge(kept(u), attend(kd[1, hp], vdt[1, hp], qbd[b, hp], slabs))
        o = (o / total).astype(BF16)
        rows = jnp.concatenate([o[:, :BLOCK], o[:, BLOCK:]], 0)
        if hp == 0:
            upper = rows
            continue
        attended = jnp.concatenate([upper, rows], 0)
        for t in (2, 1, 3):
            part[b, t - 1] = dot(wt[(x + t) % heads], attended).astype(BF16)
            share(b, t).start()
        own_part[b] = dot(wt[x], attended)

    for level, p in all1:
        on(inside["far", level, p], lambda: phase1(level, p).wait_send())
    for level, j in all2:
        phase2(level, j).wait_send()
    for level in (2,) + FAR:
        phase3(level).wait_send()
    for up in (True, False):
        on(inside["near", up], lambda: neighbour(up).wait_send())

    for b in range(2):
        total = own_part[b]
        for t in (1, 3, 2):
            share(b, t).wait_recv()
            total = total + got[t - 1, b].astype(F32)
        out_ref[:, b * BLOCK : (b + 1) * BLOCK] = total.astype(BF16)

    for b in range(2):
        for t in range(1, heads):
            share(b, t).wait_send()


def solution(mesh):
    devices, heads = mesh.shape["seq"], mesh.shape["head"]

    def shards(q, k, v, w):
        rows, width = q.shape
        lanes = w.shape[1] // heads
        vmem = pl.BlockSpec(memory_space=pltpu.VMEM)
        dma = pltpu.SemaphoreType.DMA

        def gather(level):
            return pltpu.VMEM((2 ** (level - 3), 2, 3, 4 * (rows >> level), 128), BF16)

        def stage(level):
            return pltpu.VMEM((4 * (rows >> level), 128), BF16)

        return pl.pallas_call(
            functools.partial(kernel, devices, heads),
            out_shape=jax.ShapeDtypeStruct((lanes, rows), BF16),
            in_specs=[pl.BlockSpec(memory_space=pltpu.HBM)] * 4,
            out_specs=vmem,
            scratch_shapes=[
                pltpu.VMEM((rows, width), BF16),
                pltpu.VMEM((rows, width), BF16),
                pltpu.VMEM((rows, width), BF16),
                pltpu.VMEM((width, heads * lanes), BF16),
                pltpu.VMEM((2, 4 * (BLOCK + HALF), 128), BF16),
                pltpu.VMEM((2, 4 * (BLOCK + HALF), 128), BF16),
                pltpu.VMEM((3, 4 * HALF, 128), BF16),
                gather(3), gather(4), gather(5), gather(6),
                stage(2), stage(3), stage(4), stage(5), stage(6),
                pltpu.VMEM((2, 2, 128, 256), BF16),
                pltpu.VMEM((2, 2, 512, 128), BF16),
                pltpu.VMEM((2, 2, 128, 512), BF16),
                pltpu.VMEM((2, 384, 128), BF16),
                pltpu.VMEM((2, 128, 384), BF16),
                pltpu.VMEM((2, 2, 192, 128), BF16),
                pltpu.VMEM((2, 2, 128, 192), BF16),
                pltpu.VMEM((heads, lanes, width), BF16),
                pltpu.VMEM((2, lanes, BLOCK), F32),
                pltpu.VMEM((2, heads - 1, lanes, BLOCK), BF16),
                pltpu.VMEM((heads - 1, 2, lanes, BLOCK), BF16),
                pltpu.VMEM((4, 8, 256), F32),
                pltpu.VMEM((4, 8, 256), F32),
                pltpu.VMEM((4, HEAD_DIM, 256), F32),
                pltpu.SemaphoreType.REGULAR((26,)),
                dma((4,)),
                dma((5, 3)), dma((5, 3)), dma((11,)), dma((11,)), dma((5,)), dma((5,)),
                dma((2,)), dma((2,)),
                dma((2, heads - 1)), dma((2, heads - 1)),
            ],
            compiler_params=pltpu.CompilerParams(
                collective_id=0, has_side_effects=True, vmem_limit_bytes=55040 * 1024
            ),
            cost_estimate=pl.CostEstimate(
                flops=2_000_000_000, bytes_accessed=1_200_000, transcendentals=1_600_000
            ),
        )(q, k, v, w)

    placed = (P("seq", "head"), P("seq", "head"), P("seq", "head"), P("head", None))
    return jax.shard_map(
        shards, mesh=mesh, in_specs=placed, out_specs=P("head", "seq"), check_vma=False
    )
```

```python
import functools

import jax
import jax.numpy as jnp
from jax import lax
from jax.experimental import pallas as pl
from jax.experimental.pallas import tpu as pltpu
from jax.sharding import PartitionSpec as P

HEAD_DIM = 64
BLOCK = 128
LEVELS = 6
HALF = BLOCK // 2
F32 = jnp.float32
BF16 = jnp.bfloat16
MESH = pl.DeviceIdType.MESH
FAR = (3, 4, 5, 6)
OFF = -1e30
EARLY, MIDDLE, LATE = 4, 6, 7


def dot(a, b):
    return jnp.dot(a, b, preferred_element_type=F32)


def iota(shape, dim):
    return lax.broadcasted_iota(jnp.int32, shape, dim)


def pool(rows, fine, level, repeat):
    r, c = iota((rows, fine), 0), iota((rows, fine), 1)
    hit = (c >> level) == (r & (repeat - 1))
    return jnp.where(hit, 2.0**-level, 0.0).astype(BF16)


def unpack(n):
    r, c = iota((256, 256), 0), iota((256, 256), 1)
    group, inside = r >> 6, r & 63
    source, row = inside // n, inside & (n - 1)
    return jnp.where(c == source * (4 * n) + group * n + row, 1.0, 0.0).astype(BF16)


def scores_top(s, slabs):
    top = None
    for start, rows, bias in slabs:
        m = jnp.max(s[start : start + rows], axis=0, keepdims=True)
        if bias is not None:
            m = m + bias
        top = m if top is None else jnp.maximum(top, m)
    return top


def attend(k, vt, q, slabs):
    s = dot(k, q)
    top = scores_top(s, slabs)
    parts, total = [], None
    for start, rows, bias in slabs:
        shift = top if bias is None else top - bias
        p = jnp.exp(s[start : start + rows] - shift)
        t = jnp.sum(p, axis=0, keepdims=True)
        total = t if total is None else total + t
        parts.append(p.astype(BF16))
    o = dot(vt, jnp.concatenate(parts, 0))
    o = jnp.concatenate([o[:HEAD_DIM, :BLOCK], o[HEAD_DIM:, BLOCK:]], 1)
    return top, total, o


def merge(a, b):
    top = jnp.maximum(a[0], b[0])
    fa, fb = jnp.exp(a[0] - top), jnp.exp(b[0] - top)
    return top, a[1] * fa + b[1] * fb, a[2] * fa + b[2] * fb


def kernel(
    devices, heads,
    q_hbm, k_hbm, v_hbm, w_hbm, out_ref,
    q_ref, k_ref, v_ref, w_ref, rim, near, g2, g3, g4, g5, g6, s2, s3, s4, s5, s6,
    qbd, kb, vbt, kc, vct, kd, vdt, wt, own_part, part, got, st_m, st_l, st_o, grants, in_s,
    p1_s, p1_r, p2_s, p2_r, p3_s, p3_r, near_s, near_r, part_s, part_r,
):
    d = lax.axis_index("seq")
    x = lax.axis_index("head")
    core = d % 2
    gathers = {3: g3, 4: g4, 5: g5, 6: g6}
    stages = {2: s2, 3: s3, 4: s4, 5: s5, 6: s6}

    def seq(steps):
        return (d + steps + 2 * devices) % devices

    def group(level):
        return 2 ** (level - 2)

    def far_steps(level, p):
        g = group(level)
        if p == 0:
            return 2 * g
        if p == 1:
            return -2 * g
        return (3 - 6 * ((d // g) % 2)) * g

    def remote(src, dst, send, recv, axis, target):
        return pltpu.make_async_remote_copy(
            src_ref=src, dst_ref=dst, send_sem=send, recv_sem=recv,
            device_id={axis: target}, device_id_type=MESH,
        )

    def far_target(level, p):
        target = seq(far_steps(level, p))
        if level == 4 and p == 2:
            target = target + 2 - 4 * ((target // 2) % 2)
        return target

    def phase1(level, p):
        at = (level - 2, p)
        rank = (d % group(level)) // 2
        if level == 2:
            dst = g2.at[p]
        elif level == 4 and p == 2:
            dst = g4.at[1 - rank, core, p]
        else:
            dst = gathers[level].at[rank, core, p]
        return remote(stages[level], dst, p1_s.at[at], p1_r.at[at], "seq", far_target(level, p))

    def phase2_target(level, j):
        chips = group(level) // 2
        mine = (d // 2) % chips
        return d - 2 * mine + 2 * ((mine + j) % chips)

    def phase2(level, j):
        slot = {4: 0, 5: 1, 6: 4}[level] + j - 1
        block = gathers[level].at[(d // 2) % (group(level) // 2), core]
        return remote(block, block, p2_s.at[slot], p2_r.at[slot], "seq", phase2_target(level, j))

    def phase3(level):
        if level == 2:
            src, dst = g2.at[core], g2.at[2]
        else:
            src = dst = gathers[level].at[:, core]
        slot = level - 2
        return remote(src, dst, p3_s.at[slot], p3_r.at[slot], "seq", d + 1 - 2 * core)

    def neighbour(up):
        side = 0 if up else 1
        return remote(
            rim.at[side], near.at[side], near_s.at[side], near_r.at[side], "seq", seq(1 if up else -1)
        )

    def share(b, t):
        at = (b, t - 1)
        return remote(part.at[b, t - 1], got.at[t - 1, b], part_s.at[at], part_r.at[at], "head", (x + t) % heads)

    all1 = [(level, p) for level in (6, 5, 4, 3, 2) for p in range(3 if level > 2 else 2)]
    all2 = [(level, j) for level in (4, 5, 6) for j in range(1, group(level) // 2)]

    def pass_on(level):
        for other, j in all2:
            if other == level:
                phase2(level, j).start()

    def passed(level):
        for other, j in all2:
            if other == level:
                phase2(level, j).wait_recv()

    back = (1, 0, 2)
    relations = {}
    for level, p in all1:
        there = d // group(level) + far_steps(level, p) // group(level)
        inside = (there >= 0) & (there < devices // group(level))
        relations["far", level, p] = ("seq", far_target(level, p), ("far", level, back[p]), inside)
    for up in (True, False):
        inside = d < devices - 1 if up else d > 0
        relations["near", up] = ("seq", seq(1 if up else -1), ("near", not up), inside)
    for j in range(1, 8):
        relations["mate", j] = ("seq", phase2_target(6, j), ("mate", 8 - j), True)
    for t in range(1, heads):
        relations["head", t] = ("head", (x + t) % heads, ("head", heads - t), True)
    slots = {name: i for i, name in enumerate(relations)}
    inside = {name: relation[3] for name, relation in relations.items()}
    above, below = {}, {}
    for name, (axis, target, _, valid) in relations.items():
        here = d if axis == "seq" else x
        above[name] = (target > here) & valid
        below[name] = (target < here) & valid

    def on(condition, *steps):
        @pl.when(condition)
        def _():
            for step in steps:
                step()

    def signal(semaphore, name):
        axis, target = relations[name][:2]
        pl.semaphore_signal(semaphore, inc=1, device_id={axis: target}, device_id_type=MESH)

    def granted(name, *steps):
        on(above[name], lambda: pl.semaphore_wait(grants.at[slots[name]], 1), *steps)

    def arrived(level, p):
        on(inside["far", level, back[p]], lambda: phase1(level, p).wait_recv())

    loads = [
        pltpu.make_async_copy(src, dst, in_s.at[i])
        for i, (src, dst) in enumerate(
            [(k_hbm, k_ref), (v_hbm, v_ref), (q_hbm, q_ref), (w_hbm, w_ref)]
        )
    ]
    loads[0].start()
    loads[1].start()
    barrier = pltpu.get_barrier_semaphore()
    for name in relations:
        on(above[name], lambda: signal(barrier, name))
    loads[2].start()
    loads[3].start()
    count = sum(jnp.where(below[name], 1, 0) for name in relations)
    on(count > 0, lambda: pl.semaphore_wait(barrier, count))
    for name in relations:
        on(below[name], lambda: signal(grants.at[slots[relations[name][2]]], name))

    pools = jnp.concatenate(
        [pool(BLOCK, 256, 1, 128), pool(64, 256, 2, 64), pool(32, 256, 3, 32), pool(16, 256, 4, 16),
         pool(32, 256, 5, 8), pool(16, 256, 6, 4)], 0)
    loads[0].wait()
    loads[1].wait()
    k, v = k_ref[...], v_ref[...]
    ck, cv = dot(pools, k), dot(pools, v)
    blocks = [ck[:, :128], ck[:, 128:], cv[:, :128], cv[:, 128:]]
    for level, start, n in ((2, 128, 64), (3, 192, 32), (4, 224, 16)):
        for c in range(4):
            stages[level][c * n : (c + 1) * n, :] = blocks[c][start : start + n].astype(BF16)
    for level, start, n in ((5, 240, 8), (6, 272, 4)):
        owner = iota((4 * n, 128), 0) // n
        packed = blocks[0][start : start + 4 * n]
        for c in range(1, 4):
            packed = jnp.where(owner == c, blocks[c][start : start + 4 * n], packed)
        stages[level][...] = packed.astype(BF16)
    fine = [k[:, :128], k[:, 128:], v[:, :128], v[:, 128:]]
    for side in range(2):
        edge = BLOCK * (1 - side)
        for c in range(4):
            rim[side, c * BLOCK : (c + 1) * BLOCK, :] = fine[c][edge : edge + BLOCK]
            rim[side, 512 + c * HALF : 512 + (c + 1) * HALF, :] = blocks[c][side * HALF : (side + 1) * HALF].astype(BF16)

    for level, p in all1:
        on(below["far", level, p], lambda: phase1(level, p).start())
    on(below["near", False], lambda: neighbour(False).start())

    def clear(ref):
        ref[...] = jnp.zeros(ref.shape, ref.dtype)

    for level, p in all1:
        slot = g2.at[p] if level == 2 else gathers[level].at[(d % group(level)) // 2, core, p]
        on(jnp.logical_not(inside["far", level, back[p]]), lambda: clear(slot))
    on(d == 0, lambda: clear(near.at[0]))
    on(d == devices - 1, lambda: clear(near.at[1]))
    granted(("near", True), lambda: neighbour(True).start())

    plane = d // 8
    soon, middle, last = plane < MIDDLE, (plane >= MIDDLE) & (plane < LATE), plane >= LATE

    def exchange_if(level, condition):
        for p in range(3 if level > 2 else 2):
            name = ("far", level, p)
            on(
                above[name] & condition,
                lambda: pl.semaphore_wait(grants.at[slots[name]], 1),
                lambda: phase1(level, p).start(),
            )

    for level in (2, 3, 4, 5):
        exchange_if(level, last)

    loads[2].wait()
    qt = (q_ref[...].astype(F32) * HEAD_DIM**-0.5).T
    feature = iota((BLOCK, BLOCK), 0)
    for b in range(2):
        for hp in range(2):
            piece = qt[hp * BLOCK : (hp + 1) * BLOCK, b * BLOCK : (b + 1) * BLOCK]
            low = jnp.where(feature < HEAD_DIM, piece, 0.0)
            high = jnp.where(feature < HEAD_DIM, 0.0, piece)
            qbd[b, hp] = jnp.concatenate([low, high], 1).astype(BF16)

    def keep(u, state):
        st_m[u, 0:1, :], st_l[u, 0:1, :], st_o[u] = state

    def kept(u):
        return st_m[u, 0:1, :], st_l[u, 0:1, :], st_o[u]

    units = [(b, hp) for b in range(2) for hp in range(2)]
    for hp in range(2):
        lanes = slice(hp * BLOCK, (hp + 1) * BLOCK)
        vt = v_ref[:, lanes].T
        kk = k_ref[:, lanes]
        for b in range(2):
            keep(b * 2 + hp, attend(kk, vt, qbd[b, hp], [(0, 256, None)]))

    loads[3].wait()
    for i in range(heads):
        wt[i] = w_ref[:, i * 256 : (i + 1) * 256].T

    def gathered(level):
        for p in range(3 if level > 2 else 2):
            arrived(level, p)

    for level in (2, 3, 4):
        exchange_if(level, jnp.logical_not(last))
    exchange_if(5, middle)
    exchange_if(6, middle | last)
    for j in range(1, 8):
        granted(("mate", j))

    gathered(2)
    phase3(2).start()
    gathered(3)
    phase3(3).start()
    gathered(4)
    pass_on(4)
    on(inside["near", False], lambda: neighbour(True).wait_recv())
    on(inside["near", True], lambda: neighbour(False).wait_recv())
    half_pool = pool(HALF, BLOCK, 1, HALF)
    lower_ok = jnp.where(d > 0, 0.0, OFF).astype(F32)
    upper_ok = jnp.where(d < devices - 1, 0.0, OFF).astype(F32)

    def far_bias(level):
        g, out = group(level), []
        e, last = d // g, devices // g - 1
        steps = (-2, 2, 3 - 6 * (e % 2))
        for step in steps:
            there = e + step
            out.append(jnp.where((there >= 0) & (there <= last), 0.0, OFF).astype(F32))
        return out

    bias2 = far_bias(2)
    phase3(2).wait_recv()
    for c in range(4):
        kind, hp = c // 2, c % 2
        strip = slice(c * BLOCK, (c + 1) * BLOCK)
        rows = slice(c * HALF, (c + 1) * HALF)
        half = slice(512 + c * HALF, 512 + (c + 1) * HALF)
        pooled = [dot(half_pool, near[side, strip, :]).astype(BF16) for side in range(2)]
        common = [near[0, half, :], near[1, half, :]] + [g2[p, rows, :] for p in range(3)]
        for b in range(2):
            full = jnp.concatenate([near[b, strip, :], pooled[1 - b]] + common, 0)
            if kind == 0:
                kb[b, hp] = full
            else:
                vbt[b, hp] = full.T
    for b, hp in units:
        first, second = (lower_ok, upper_ok) if b == 0 else (upper_ok, lower_ok)
        slabs = [(0, 128, first), (128, 64, second), (192, 64, lower_ok), (256, 64, upper_ok)]
        slabs += [(320 + 64 * p, 64, bias2[p]) for p in range(3)]
        u = b * 2 + hp
        keep(u, merge(kept(u), attend(kb[b, hp], vbt[b, hp], qbd[b, hp], slabs)))
        if u == 1:
            passed(4)
            phase3(4).start()
            exchange_if(5, soon)
            exchange_if(6, soon & (plane >= EARLY))
            gathered(5)
            pass_on(5)
    exchange_if(6, plane < EARLY)
    gathered(6)
    pass_on(6)
    passed(5)
    phase3(5).start()

    def far_chunk(levels, k_to, vt_to):
        slabs, keys, values = [], ([], []), ([], [])
        for level in levels:
            phase3(level).wait_recv()
            n = 256 // 2**level
            g = group(level)
            for p, bias in enumerate(far_bias(level)):
                slabs.append((64 * len(slabs), 64, bias))
                whole = gathers[level][:, :, p].reshape(g, 4 * n, 128)
                if n >= 16:
                    four = [whole[:, c * n : (c + 1) * n, :].reshape(64, 128) for c in range(4)]
                else:
                    moved = dot(unpack(n), whole.reshape(256, 128)).astype(BF16)
                    four = [moved[c * 64 : (c + 1) * 64] for c in range(4)]
                for hp in range(2):
                    keys[hp].append(four[hp])
                    values[hp].append(four[2 + hp])
        for hp in range(2):
            k_to[hp] = jnp.concatenate(keys[hp], 0)
            vt_to[hp] = jnp.concatenate(values[hp], 0).T
        return slabs

    slabs = far_chunk((3, 4), kc, vct)
    for b, hp in units:
        u = b * 2 + hp
        keep(u, merge(kept(u), attend(kc[hp], vct[hp], qbd[b, hp], slabs)))
        if u == 1:
            passed(6)
            phase3(6).start()
    slabs = far_chunk((5,), kd.at[0], vdt.at[0])
    for b, hp in units:
        u = b * 2 + hp
        keep(u, merge(kept(u), attend(kd[0, hp], vdt[0, hp], qbd[b, hp], slabs)))
    for t in range(1, heads):
        granted(("head", t))
    slabs = far_chunk((6,), kd.at[1], vdt.at[1])
    for b, hp in units:
        u = b * 2 + hp
        _, total, o = merge(kept(u), attend(kd[1, hp], vdt[1, hp], qbd[b, hp], slabs))
        o = (o / total).astype(BF16)
        rows = jnp.concatenate([o[:, :BLOCK], o[:, BLOCK:]], 0)
        if hp == 0:
            upper = rows
            continue
        attended = jnp.concatenate([upper, rows], 0)
        for t in (2, 1, 3):
            part[b, t - 1] = dot(wt[(x + t) % heads], attended).astype(BF16)
            share(b, t).start()
        own_part[b] = dot(wt[x], attended)

    for level, p in all1:
        on(inside["far", level, p], lambda: phase1(level, p).wait_send())
    for level, j in all2:
        phase2(level, j).wait_send()
    for level in (2,) + FAR:
        phase3(level).wait_send()
    for up in (True, False):
        on(inside["near", up], lambda: neighbour(up).wait_send())

    for b in range(2):
        total = own_part[b]
        for t in (1, 3, 2):
            share(b, t).wait_recv()
            total = total + got[t - 1, b].astype(F32)
        out_ref[:, b * BLOCK : (b + 1) * BLOCK] = total.astype(BF16)

    for b in range(2):
        for t in range(1, heads):
            share(b, t).wait_send()


def solution(mesh):
    devices, heads = mesh.shape["seq"], mesh.shape["head"]

    def shards(q, k, v, w):
        rows, width = q.shape
        lanes = w.shape[1] // heads
        vmem = pl.BlockSpec(memory_space=pltpu.VMEM)
        dma = pltpu.SemaphoreType.DMA

        def gather(level):
            return pltpu.VMEM((2 ** (level - 3), 2, 3, 4 * (rows >> level), 128), BF16)

        def stage(level):
            return pltpu.VMEM((4 * (rows >> level), 128), BF16)

        return pl.pallas_call(
            functools.partial(kernel, devices, heads),
            out_shape=jax.ShapeDtypeStruct((lanes, rows), BF16),
            in_specs=[pl.BlockSpec(memory_space=pltpu.HBM)] * 4,
            out_specs=vmem,
            scratch_shapes=[
                pltpu.VMEM((rows, width), BF16),
                pltpu.VMEM((rows, width), BF16),
                pltpu.VMEM((rows, width), BF16),
                pltpu.VMEM((width, heads * lanes), BF16),
                pltpu.VMEM((2, 4 * (BLOCK + HALF), 128), BF16),
                pltpu.VMEM((2, 4 * (BLOCK + HALF), 128), BF16),
                pltpu.VMEM((3, 4 * HALF, 128), BF16),
                gather(3), gather(4), gather(5), gather(6),
                stage(2), stage(3), stage(4), stage(5), stage(6),
                pltpu.VMEM((2, 2, 128, 256), BF16),
                pltpu.VMEM((2, 2, 512, 128), BF16),
                pltpu.VMEM((2, 2, 128, 512), BF16),
                pltpu.VMEM((2, 384, 128), BF16),
                pltpu.VMEM((2, 128, 384), BF16),
                pltpu.VMEM((2, 2, 192, 128), BF16),
                pltpu.VMEM((2, 2, 128, 192), BF16),
                pltpu.VMEM((heads, lanes, width), BF16),
                pltpu.VMEM((2, lanes, BLOCK), F32),
                pltpu.VMEM((2, heads - 1, lanes, BLOCK), BF16),
                pltpu.VMEM((heads - 1, 2, lanes, BLOCK), BF16),
                pltpu.VMEM((4, 8, 256), F32),
                pltpu.VMEM((4, 8, 256), F32),
                pltpu.VMEM((4, HEAD_DIM, 256), F32),
                pltpu.SemaphoreType.REGULAR((26,)),
                dma((4,)),
                dma((5, 3)), dma((5, 3)), dma((11,)), dma((11,)), dma((5,)), dma((5,)),
                dma((2,)), dma((2,)),
                dma((2, heads - 1)), dma((2, heads - 1)),
            ],
            compiler_params=pltpu.CompilerParams(
                collective_id=0, has_side_effects=True, vmem_limit_bytes=55040 * 1024
            ),
            cost_estimate=pl.CostEstimate(
                flops=2_000_000_000, bytes_accessed=1_200_000, transcendentals=1_600_000
            ),
        )(q, k, v, w)

    placed = (P("seq", "head"), P("seq", "head"), P("seq", "head"), P("head", None))
    return jax.shard_map(
        shards, mesh=mesh, in_specs=placed, out_specs=P("head", "seq"), check_vma=False
    )
```
